32 devices in a mesh: grid: 16 (over z, y, core), orb: 2 (over x).
Axes of the slice: x: 2, y: 2, z: 4, core: 2. Of those that a mesh axis runs over, the one named last changes fastest.
Arguments:
- density: float32 [32, 3, 128, 128], P('grid', None, 'orb'), may hold values from -4 to 4
- basis_values: float32 [32, 1280, 768], P(('grid', 'orb')), may hold values from -0.5 to 0.5
- quad_weights: float32 [32, 1280], P(('grid', 'orb')), may hold values from 0.01 to 0.1
- ext_potential: float32 [32, 1280], P(('grid', 'orb')), may hold values from 0 to 4
- batch_blocks: int32 [32, 6], P(('grid', 'orb')), may hold values from 0 to 31, as said below
- domain_blocks: int32 [64, 4], P(('grid', 'orb')), may hold values from 0 to 31, as said below
- coefficients: float32 [64, 4, 128, 128], P(('grid', 'orb')), may hold values from -0.25 to 0.25
Outputs:
- density_out: float32 [32, 3, 128, 128], P('grid', None, 'orb')
- coefficients_out: float32 [64, 4, 128, 128], P(('grid', 'orb'))
The draws below stay inside these ranges and needn't reach their ends.
Inputs may be any that keep to these rules, and one draw needn't show every extreme that they name: `batch_blocks`: the batches on grid index g (batch numbers g * 32 / 16 onward) list the 6 blocks from (g - 1) * 2 onward, taken modulo 32, each once, in some order. `domain_blocks`: the domains on grid index g list 4 distinct blocks among the 6 blocks from (g - 1) * 2 onward, taken modulo 32, at least one of the first 2 and one of the last 2 of them.
All inputs are finite; a program needn't handle non-finite values.
Results may differ from the reference program's by a relative error of at most 0.0003.
Values sent between devices are 32-bit elements; how exact they have to be, the bound alone decides.
No kernel may reach another device: no remote copies, remote signals or barrier semaphores. Data moves between devices by JAX's collectives and lax.ppermute only.
A program may use at most 64 MiB of HBM per device.

```python
import math
import jax
import jax.numpy as jnp
from jax import lax

NB = 128
BF = 6
DB = 4
PTS = 1280
FB = 2
ITERS = 2
NFB = 32
NBATCH = 32
NDOM = 64


def draw_block_lists(key, rows, count):
    subkeys = jax.random.split(key, 3)
    first_pick = jax.random.randint(subkeys[0], (rows, 1), 0, FB)
    last_pick = jax.random.randint(subkeys[1], (rows, 1), 2 * FB, 3 * FB)
    shuffled = jax.vmap(lambda row_key: jax.random.permutation(row_key, 3 * FB))(jax.random.split(subkeys[2], rows))
    positions = jnp.arange(3 * FB, dtype=jnp.int32)[None, :]
    scores = jnp.where(positions == first_pick, -2, jnp.where(positions == last_pick, -1, shuffled.astype(jnp.int32)))
    chosen = jnp.argsort(scores, axis=1, stable=True)[:, :count].astype(jnp.int32)
    owner_grid = jnp.arange(rows, dtype=jnp.int32) // (rows // (NFB // FB))
    return jnp.mod(owner_grid[:, None] * FB - FB + chosen, NFB).astype(jnp.int32)


def draw_batch_blocks(key, part):
    return draw_block_lists(jax.random.fold_in(key, 11), NBATCH, BF)


def draw_domain_blocks(key, part):
    return draw_block_lists(jax.random.fold_in(key, 23), NDOM, DB)


def block_scale(own_key, extent, shards, smallest, largest):
    factor_of, own = 1.0, jax.random.fold_in(own_key, 6)
    for axis_at, shards_of in shards:
        draws = jnp.exp(jax.random.uniform(jax.random.fold_in(own, axis_at), (shards_of,), jnp.float32, smallest / len(shards), largest / len(shards)))
        factor_of = factor_of * jnp.repeat(draws, extent[axis_at] // shards_of).reshape([-1 if axis == axis_at else 1 for axis in range(len(extent))])
    return factor_of


def normal_values(own_key, dims, spread, most, pieces=(), kind=jnp.bfloat16):
    gain = block_scale(own_key, dims, pieces, -0.22, 0.18) if pieces else 1.0
    entries = jax.random.normal(own_key, dims, jnp.float32) * spread * gain
    return jnp.minimum(jnp.maximum(entries, -most), most).astype(kind)


def setup_inputs(seed: int = 0) -> dict:
    seeds = jax.random.split(jax.random.key(seed), 8)
    return {
        "density": normal_values(seeds[0], (NFB, 3, NB, NB), 0.25, 4.0, ((0, 16), (2, 2)), jnp.float32),
        "basis_values": normal_values(seeds[1], (NBATCH, PTS, BF * NB), NB ** -0.5, 0.5, ((0, 32),), jnp.float32),
        "quad_weights": jnp.clip(jnp.exp(math.log(0.1) - 2.3025851 * jax.random.uniform(seeds[2], (NBATCH, PTS), jnp.float32) ** block_scale(seeds[2], (NBATCH, PTS), ((0, 32),), -0.2, 0.2)), 0.01, 0.1),
        "ext_potential": jnp.clip(4.0 * jax.random.uniform(seeds[3], (NBATCH, PTS), jnp.float32) ** block_scale(seeds[3], (NBATCH, PTS), ((0, 32),), -0.2, 0.2), 0.0, 4.0),
        "batch_blocks": draw_batch_blocks(jax.random.fold_in(seeds[7], 71), 0),
        "domain_blocks": draw_domain_blocks(jax.random.fold_in(seeds[7], 71), 0),
        "coefficients": normal_values(seeds[6], (NDOM, DB, NB, NB), (DB * NB) ** -0.5, 0.25, ((0, 32),), jnp.float32),
    }


step_scale = 0.5


def pair_index(blocks, anchor, total_blocks):
    relative = jnp.mod(blocks - anchor, total_blocks)
    offset = jnp.mod(blocks[None, :] - blocks[:, None] + 1, total_blocks)
    inside = offset <= 2
    positions = relative[:, None] * 3 + jnp.where(inside, offset, 0)
    return positions, inside


def gather_tiles(flat_band, positions, inside):
    return jnp.where(inside[..., None, None], flat_band[positions], 0.0)


def place_tiles(flat_band, positions, inside, block_tiles):
    masked = jnp.where(inside[..., None, None], block_tiles, 0.0)
    rows = masked.reshape(-1, block_tiles.shape[-2], block_tiles.shape[-1])
    return flat_band.at[positions.reshape(-1)].add(rows)


def batch_fock(basis, weights, external, block_tiles):
    count_blocks = block_tiles.shape[0]
    block_size = block_tiles.shape[2]
    width = count_blocks * block_size
    batch_density = block_tiles.transpose(0, 2, 1, 3).reshape(width, width)
    projected = jnp.dot(basis, batch_density, precision=lax.Precision.HIGHEST, preferred_element_type=jnp.float32)
    density_points = jnp.sum(projected * basis, axis=1)
    potential = external - jnp.power(density_points * density_points + 1.0, 1.0 / 6.0)
    scaled = basis * (weights * potential)[:, None]
    fock_tiles = jnp.einsum("pm,pn->mn", scaled, basis, precision=lax.Precision.HIGHEST)
    return fock_tiles.reshape(count_blocks, block_size, count_blocks, block_size).transpose(0, 2, 1, 3)


def domain_update(fock_blocks, current):
    gradient = jnp.einsum("ijab,jbc->iac", fock_blocks, current, precision=lax.Precision.HIGHEST)
    intersection = jnp.einsum("iab,iac->bc", current, gradient, precision=lax.Precision.HIGHEST)
    updated = current - step_scale * (gradient - jnp.einsum("iab,bc->iac", current, intersection, precision=lax.Precision.HIGHEST))
    outer_terms = jnp.einsum("iab,jcb->ijac", updated, updated, precision=lax.Precision.HIGHEST)
    return updated, outer_terms


def reference(density, basis_values, quad_weights, ext_potential, batch_blocks, domain_blocks, coefficients):
    band_blocks = density
    current = coefficients
    for iteration in range(ITERS):
        flat_band = band_blocks.reshape(-1, NB, NB)

        def per_batch(accumulated, element):
            basis, weights, external, blocks = element
            positions, inside = pair_index(blocks, 0, NFB)
            block_tiles = gather_tiles(flat_band, positions, inside)
            fock_tiles = batch_fock(basis, weights, external, block_tiles)
            return place_tiles(accumulated, positions, inside, fock_tiles), 0.0

        fock_flat, ignored = lax.scan(per_batch, jnp.zeros_like(flat_band), (basis_values, quad_weights, ext_potential, batch_blocks))

        def per_domain(accumulated, element):
            blocks, domain_coef = element
            positions, inside = pair_index(blocks, 0, NFB)
            updated, outer_terms = domain_update(gather_tiles(fock_flat, positions, inside), domain_coef)
            return place_tiles(accumulated, positions, inside, outer_terms), updated

        new_flat, current = lax.scan(per_domain, jnp.zeros_like(flat_band), (domain_blocks, current))
        band_blocks = new_flat.reshape(NFB, 3, NB, NB)
    return band_blocks, current
```

```python
import functools
import jax
import jax.numpy as jnp
from jax import lax
from jax.experimental import pallas as pl
from jax.experimental.pallas import tpu as pltpu
from jax.sharding import PartitionSpec as P

ITERS = 2
step_scale = 0.5

NB = 128
SB = 2 * NB
TILE = 8
HALF = NB // 2
PACKED = NB + TILE
VMEM_BYTES = 40 * 1024 * 1024
POINT_CHUNK = 256
f32 = jnp.float32
bf16 = jnp.bfloat16

LOW = slice(0, PACKED)
HIGH = slice(PACKED + HALF, 2 * PACKED + HALF)
A_ROWS = 2 * PACKED + HALF
B_ROWS = 2 * NB + HALF
PAIR = PACKED + NB
GIVE_ROWS = PAIR + HALF
FINAL_ROWS = PAIR + NB


def split(value):
    high = value.astype(bf16)
    return high, (value - high.astype(f32)).astype(bf16)


def dot3(left, right, contract=((1,), (0,))):
    def one(a, b):
        return lax.dot_general(a, b, (contract, ((), ())), preferred_element_type=f32)

    return one(left[0], right[0]) + (one(left[0], right[1]) + one(left[1], right[0]))


def both(pair, *index):
    return pair[0][index], pair[1][index]


def row_col():
    rows = lax.broadcasted_iota(jnp.int32, (NB, NB), 0)
    return rows, lax.broadcasted_iota(jnp.int32, (NB, NB), 1)


def aligned(value, unit):
    return pl.multiple_of(value * unit, unit)


def core_of():
    return lax.rem(lax.axis_index("grid"), 2)


def relative(block, total_blocks):
    anchor = (lax.axis_index("grid") - 1) * 2
    return lax.rem(block - anchor + total_blocks, total_blocks)


def whole_call(kernel, outs, scratch, name, smem=(), count=0, flops=0, moved=0):
    specs = [
        pl.BlockSpec(memory_space=pltpu.SMEM if i in smem else pltpu.VMEM) for i in range(count)
    ]
    return pl.pallas_call(
        kernel,
        out_shape=[jax.ShapeDtypeStruct(shape, kind) for shape, kind in outs],
        in_specs=specs,
        out_specs=[pl.BlockSpec(memory_space=pltpu.VMEM) for _ in outs],
        scratch_shapes=scratch,
        compiler_params=pltpu.CompilerParams(vmem_limit_bytes=VMEM_BYTES),
        cost_estimate=pl.CostEstimate(flops=flops, bytes_accessed=moved, transcendentals=0),
        name=name,
    )


def sort_kernel(total_blocks, blocks, basis, th, tl, nh, nl):
    for j in range(6):
        at = aligned(relative(blocks[0, j], total_blocks), NB)
        column = basis[:, j * NB : (j + 1) * NB]
        nh[:, pl.ds(at, NB)], nl[:, pl.ds(at, NB)] = split(column)
        th[pl.ds(at, NB), :], tl[pl.ds(at, NB), :] = split(column.T)


def pack_pair(pair_ref, at):
    rows, cols = row_col()
    first = pair_ref[at, :NB, :NB]
    last = pair_ref[at, NB:, NB:]
    merged = jnp.where(rows <= cols, first, last)
    diagonal = jnp.sum(jnp.where(rows == cols, last, 0.0), axis=0, keepdims=True)
    return merged, jnp.broadcast_to(diagonal, (TILE, NB)), pair_ref[at, :NB, NB:]


def store_packed(pair_ref, cross_ref, out_a, out_b, give, keep):
    core = core_of()
    for at, a_at, b_at in ((core, 0, 0), (core + 1, PACKED + HALF, NB + HALF)):
        merged, diagonal, off = pack_pair(pair_ref, at)
        out_a[a_at : a_at + NB, :] = merged
        out_a[a_at + NB : a_at + PACKED, :] = diagonal
        out_b[b_at : b_at + NB, :] = off
    out_a[PACKED : PACKED + HALF, :] = cross_ref[core, :HALF, :]
    out_b[NB : NB + HALF, :] = cross_ref[core, HALF:, :]
    merged, diagonal, off = pack_pair(pair_ref, 2 - 2 * core)
    give[:NB, :] = merged
    give[NB:PACKED, :] = diagonal
    give[PACKED:PAIR, :] = off
    give[PAIR:, :] = cross_ref[1 - core, pl.ds(aligned(1 - core, HALF), HALF), :]
    keep[...] = cross_ref[1 - core, pl.ds(aligned(core, HALF), HALF), :]


def store_final(pair_ref, cross_ref, near, keep, give, edge):
    core = core_of()
    places = ((1, near), (2 - 2 * core, give), (2 * core, edge))
    for at, target in places:
        merged, diagonal, off = pack_pair(pair_ref, at)
        target[:NB, :] = merged
        target[NB:PACKED, :] = diagonal
        target[PACKED:PAIR, :] = off
    give[PAIR:, :] = cross_ref[1 - core]
    keep[...] = cross_ref[1 - core]
    edge[PAIR:, :] = cross_ref[core]


def load_packed(side_a, side_b, mid, other):
    core = core_of()
    pairs = [
        (core, side_a[:NB, :], side_a[NB : NB + 1, :], side_b[:NB, :]),
        (
            core + 1,
            side_a[PACKED + HALF : PACKED + HALF + NB, :],
            side_a[PACKED + HALF + NB : PACKED + HALF + NB + 1, :],
            side_b[NB + HALF :, :],
        ),
        (2 - 2 * core, other[:NB, :], other[NB : NB + 1, :], other[PACKED:PAIR, :]),
    ]
    return core, pairs


def load_cross(cross_ref, core, side_a, side_b, mid, other):
    cross_ref[core, :HALF, :] = side_a[PACKED : PACKED + HALF, :]
    cross_ref[core, HALF:, :] = side_b[NB : NB + HALF, :]
    cross_ref[1 - core, pl.ds(aligned(core, HALF), HALF), :] = mid[...]
    cross_ref[1 - core, pl.ds(aligned(1 - core, HALF), HALF), :] = other[PAIR:, :]


def unpack_pair(merged, diagonal):
    rows, cols = row_col()
    turned = merged.T
    first = jnp.where(rows <= cols, merged, turned)
    last = jnp.where(rows > cols, merged, jnp.where(rows < cols, turned, diagonal))
    return first, last


def fock_body(weights, external, basis_t, basis_n, pairs_ref, terms, scaled, pair_ref, cross_ref):
    points = weights.shape[1]
    pairs = [split(pairs_ref[j]) for j in range(3)]
    terms = [(row, col, split(value)) for row, col, value in terms]
    for start in range(0, points, POINT_CHUNK):
        cols = slice(start, start + POINT_CHUNK)

        def value_of(low, count):
            piece = both(basis_t, slice(low * NB, (low + count) * NB), cols)
            return piece, piece[0].astype(f32) + piece[1].astype(f32)

        rho = jnp.zeros((1, POINT_CHUNK), f32)
        for j in range(3):
            piece, value = value_of(2 * j, 2)
            rho = rho + jnp.sum(dot3(pairs[j], piece) * value, axis=0, keepdims=True)
        for row, col, matrix in terms:
            piece, _ = value_of(col, 1)
            _, value = value_of(row, 1)
            rho = rho + jnp.sum(dot3(matrix, piece) * value, axis=0, keepdims=True)
        potential = external[:, cols] - jnp.exp(jnp.log(rho * rho + 1.0) * (1.0 / 6.0))
        scale = weights[:, cols] * potential
        for j in range(3):
            _, value = value_of(2 * j, 2)
            high, low = split(value * scale)
            scaled[0][2 * j * NB : 2 * (j + 1) * NB, cols] = high
            scaled[1][2 * j * NB : 2 * (j + 1) * NB, cols] = low
    for j in range(3):
        first = 2 * j * NB - (NB if j else 0)
        left = both(scaled, slice(first, 2 * (j + 1) * NB), slice(None))
        block = dot3(left, both(basis_n, slice(None), slice(2 * j * NB, 2 * (j + 1) * NB)))
        if j:
            cross_ref[j - 1] = block[:NB, :NB]
            pair_ref[j] = block[NB:, :]
        else:
            pair_ref[j] = block


def fock_first(
    weights, external, th, tl, nh, nl, own, edge, other,
    out_a, out_b, give, keep, dens, sh, sl, pair_ref, cross_ref,
):
    core = core_of()
    for i in range(2):
        for j in range(2):
            index = 3 * i + j - i + 1
            rows, cols = slice(i * NB, (i + 1) * NB), slice(j * NB, (j + 1) * NB)
            dens[1, rows, cols] = own[index]
            dens[2 * core, rows, cols] = edge[index - 1 + core]
            dens[2 - 2 * core, rows, cols] = other[index]
    low = jnp.where(core == 0, edge[4], other[5])
    high = jnp.where(core == 0, other[0], edge[0])
    terms = [(1, 2, low), (2, 1, own[0]), (3, 4, own[5]), (4, 3, high)]
    fock_body(
        weights, external, (th, tl), (nh, nl), dens, terms, (sh, sl), pair_ref, cross_ref
    )
    store_packed(pair_ref, cross_ref, out_a, out_b, give, keep)


def fock_later(
    weights, external, th, tl, nh, nl, side_a, side_b, mid, other,
    out_a, out_b, give, keep, dens, sh, sl, pair_ref, cross_ref,
):
    rows, cols = row_col()
    core, pairs = load_packed(side_a, side_b, mid, other)
    for at, merged, diagonal, off in pairs:
        twice = merged * 2.0
        dens[at, :NB, :NB] = jnp.where(rows < cols, twice, jnp.where(rows == cols, merged, 0.0))
        dens[at, NB:, NB:] = jnp.where(rows > cols, twice, jnp.where(rows == cols, diagonal, 0.0))
        dens[at, :NB, NB:] = off * 2.0
        dens[at, NB:, :NB] = jnp.zeros((NB, NB), f32)
    load_cross(cross_ref, core, side_a, side_b, mid, other)
    terms = [(1, 2, cross_ref[0] * 2.0), (3, 4, cross_ref[1] * 2.0)]
    fock_body(
        weights, external, (th, tl), (nh, nl), dens, terms, (sh, sl), pair_ref, cross_ref
    )
    store_packed(pair_ref, cross_ref, out_a, out_b, give, keep)


def domain_body(
    total_blocks, lists, coef, side_a, side_b, mid, other,
    fh, fl, gradient, moved, pair_ref, cross_ref,
):
    core, pairs = load_packed(side_a, side_b, mid, other)
    load_cross(cross_ref, core, side_a, side_b, mid, other)
    for at, merged, diagonal, off in pairs:
        first, last = unpack_pair(merged, diagonal)
        pair_ref[at, :NB, :NB] = first
        pair_ref[at, :NB, NB:] = off
        pair_ref[at, NB:, :NB] = off.T
        pair_ref[at, NB:, NB:] = last
    zero = jnp.zeros((NB, NB), f32)
    between = [(cross_ref[j], cross_ref[j].T) for j in range(2)]
    for j in range(3):
        top = NB if j else 0
        slab = [pair_ref[j]]
        if j:
            slab = [jnp.concatenate([between[j - 1][0], zero], axis=1)] + slab
        if j < 2:
            slab = slab + [jnp.concatenate([zero, between[j][1]], axis=1)]
        slab = jnp.concatenate(slab, axis=0)
        start = 2 * j * NB - top
        stop = start + slab.shape[0]
        product = dot3(split(slab), split(coef[2 * j * NB : 2 * (j + 1) * NB, :]))
        if j == 0:
            gradient[start:stop, :] = product
        else:
            seen = (2 * j + 1) * NB
            gradient[start:seen, :] += product[: seen - start]
            gradient[seen:stop, :] = product[seen - start :]
    domains = len(lists)
    mixed = []
    for d in range(domains):
        cols = slice(d * NB, (d + 1) * NB)
        mixed.append(dot3(split(coef[:, cols]), split(gradient[:, cols]), ((0,), (0,))))
    for d in range(0, domains, 2):
        cols = slice(d * NB, (d + 2) * NB)
        square = jnp.concatenate(
            [
                jnp.concatenate([mixed[d], zero], axis=1),
                jnp.concatenate([zero, mixed[d + 1]], axis=1),
            ],
            axis=0,
        )
        moved[:, cols] = dot3(split(coef[:, cols]), split(square))


def new_rows(total_blocks, lists, coef, gradient, moved):
    for d, (blocks, row) in enumerate(lists):
        cols = slice(d * NB, (d + 1) * NB)
        for i in range(4):
            at = aligned(relative(blocks[row, i], total_blocks), NB)
            rows = pl.ds(at, NB)
            value = coef[rows, cols] - step_scale * (gradient[rows, cols] - moved[rows, cols])
            yield d, i, rows, cols, value


def density_body(coef, pair_ref, cross_ref):
    pieces = split(coef[...])
    contract = ((1,), (1,))
    for j in range(3):
        piece = both(pieces, slice(2 * j * NB, 2 * (j + 1) * NB))
        pair_ref[j] = dot3(piece, piece, contract)
    for j in range(2):
        first = both(pieces, slice((2 * j + 1) * NB, (2 * j + 2) * NB))
        last = both(pieces, slice((2 * j + 2) * NB, (2 * j + 3) * NB))
        cross_ref[j] = dot3(first, last, contract)


def domain_first(
    total_blocks, own_lists, other_lists, own, partner, side_a, side_b, mid, other,
    coef_out, out_a, out_b, give, keep, coef, gradient, moved, pair_ref, cross_ref,
):
    lists = [(own_lists, 0), (own_lists, 1), (other_lists, 0), (other_lists, 1)]
    coef[...] = jnp.zeros_like(coef)
    for d, (blocks, row) in enumerate(lists):
        source = own if d < 2 else partner
        for i in range(4):
            at = aligned(relative(blocks[row, i], total_blocks), NB)
            coef[pl.ds(at, NB), d * NB : (d + 1) * NB] = source[row, i]
    domain_body(
        total_blocks, lists, coef, side_a, side_b, mid, other,
        None, None, gradient, moved, pair_ref, cross_ref,
    )
    coef_out[...] = jnp.zeros_like(coef_out)
    for _, _, rows, cols, value in new_rows(total_blocks, lists, coef, gradient, moved):
        coef_out[rows, cols] = value
    density_body(coef_out, pair_ref, cross_ref)
    store_packed(pair_ref, cross_ref, out_a, out_b, give, keep)


def domain_last(
    total_blocks, own_lists, other_lists, coef, side_a, side_b, mid, other,
    result, near, keep, give, edge, fresh, gradient, moved, pair_ref, cross_ref,
):
    lists = [(own_lists, 0), (own_lists, 1), (other_lists, 0), (other_lists, 1)]
    domain_body(
        total_blocks, lists, coef, side_a, side_b, mid, other,
        None, None, gradient, moved, pair_ref, cross_ref,
    )
    fresh[...] = jnp.zeros_like(fresh)
    for d, i, rows, cols, value in new_rows(total_blocks, lists, coef, gradient, moved):
        fresh[rows, cols] = value
        if d < 2:
            result[d, i] = value
    density_body(fresh, pair_ref, cross_ref)
    store_final(pair_ref, cross_ref, near, keep, give, edge)


def owner_kernel(near, keep, edge, from_core, from_edge, out, full):
    core = core_of()
    total = near[...] + from_core[:PAIR, :] + from_edge[:PAIR, :]
    first, last = unpack_pair(total[:NB], total[NB : NB + 1])
    off = total[PACKED:PAIR]
    mid = keep[...] + from_core[PAIR:, :]
    side = edge[PAIR:, :] + from_edge[PAIR:, :]
    below = jnp.where(core == 0, side, mid)
    above = jnp.where(core == 0, mid, side)
    full[0, 0] = below.T
    full[0, 1] = first
    full[0, 2] = off
    full[1, 0] = off.T
    full[1, 1] = last
    full[1, 2] = above
    start = aligned(lax.axis_index("orb"), HALF)
    for i in range(2):
        for s in range(3):
            out[i, s] = full[i, s, pl.ds(start, HALF), :]


def to_core(value):
    count = lax.axis_size("grid")
    return lax.ppermute(value, "grid", [(i, i ^ 1) for i in range(count)])


def to_edge(value):
    count = lax.axis_size("grid")
    route = [(i, (i + 1) % count if i % 2 else (i - 1) % count) for i in range(count)]
    return lax.ppermute(value, "grid", route)


def to_orb(value):
    return lax.ppermute(value, "orb", [(0, 1), (1, 0)])


def add_near(core, side_a, side_b, keep, arrived):
    packed, off = arrived[:PACKED], arrived[PACKED:PAIR]

    def placed(piece, gap):
        zero = jnp.zeros_like(piece)
        parts = [
            jnp.where(core == 1, piece, zero),
            jnp.zeros((gap, NB), f32),
            jnp.where(core == 0, piece, zero),
        ]
        return jnp.concatenate(parts, axis=0)

    return side_a + placed(packed, HALF), side_b + placed(off, HALF), keep + arrived[PAIR:]


def near_part(core, side_a, side_b, mid):
    packed = lax.dynamic_slice_in_dim(side_a, (1 - core) * (PACKED + HALF), PACKED, 0)
    off = lax.dynamic_slice_in_dim(side_b, (1 - core) * (NB + HALF), NB, 0)
    return jnp.concatenate([packed, off, mid], axis=0)


def total_over_all(core, side_a, side_b, give, keep):
    side_a, side_b, keep = add_near(core, side_a, side_b, keep, to_core(give))
    first_a = to_orb(side_a)
    first_b = to_edge(side_b)
    side_a = side_a + first_a
    side_b = side_b + first_b
    last_a = to_edge(side_a)
    last_b = to_orb(jnp.concatenate([side_b, keep], axis=0))
    side_a = side_a + last_a
    side_b = side_b + last_b[:B_ROWS]
    keep = keep + last_b[B_ROWS:]
    return side_a, side_b, keep, to_core(near_part(core, side_a, side_b, keep))


def total_over_grid(core, side_a, side_b, give, keep):
    side_a, side_b, keep = add_near(core, side_a, side_b, keep, to_core(give))
    arrived = to_edge(jnp.concatenate([side_a, side_b], axis=0))
    side_a = side_a + arrived[:A_ROWS]
    side_b = side_b + arrived[A_ROWS:]
    return side_a, side_b, keep, to_core(near_part(core, side_a, side_b, keep))


def shards(
    density, basis_values, quad_weights, ext_potential, batch_blocks, domain_blocks, coefficients
):
    total_blocks = density.shape[0] * lax.axis_size("grid")
    points = basis_values.shape[1]
    core = lax.rem(lax.axis_index("grid"), 2)
    window = 6 * NB
    half_shape, full_shape = (points, window), (window, points)
    packed_outs = [((A_ROWS, NB), f32), ((B_ROWS, NB), f32), ((GIVE_ROWS, NB), f32), ((HALF, NB), f32)]
    band_scratch = [pltpu.VMEM((3, SB, SB), f32), pltpu.VMEM((2, NB, NB), f32)]

    basis = whole_call(
        functools.partial(sort_kernel, total_blocks),
        [(full_shape, bf16)] * 2 + [(half_shape, bf16)] * 2,
        [],
        "sort_basis",
        smem=(0,),
        count=2,
        moved=12 * points * window,
    )(batch_blocks, basis_values[0])

    partner = to_orb(density)
    first_half = lax.axis_index("orb") == 0
    own = jnp.concatenate(
        [jnp.where(first_half, density, partner), jnp.where(first_half, partner, density)], axis=2
    ).reshape(6, NB, NB)
    from_edge = to_edge(lax.dynamic_slice_in_dim(own, core, 5, 0))
    from_core = to_core(own)
    coefficients_ready, own = lax.optimization_barrier((coefficients, own))
    other_coefficients = to_orb(coefficients_ready)
    other_lists = to_orb(domain_blocks)

    fock_scratch = [
        pltpu.VMEM((3, SB, SB), f32),
        pltpu.VMEM(full_shape, bf16),
        pltpu.VMEM(full_shape, bf16),
    ] + band_scratch
    domain_scratch = [pltpu.VMEM((window, 4 * NB), f32)] * 2 + band_scratch
    fock_cost = 2 * 3 * 8 * points * SB * SB

    coef = None
    packed = None
    for iteration in range(ITERS):
        if iteration == 0:
            kernel, operands = fock_first, (own, from_edge, from_core)
        else:
            kernel, operands = fock_later, packed
        made = whole_call(
            kernel, packed_outs, fock_scratch, "fock", count=6 + len(operands), flops=fock_cost
        )(quad_weights, ext_potential, *basis, *operands)
        packed = total_over_all(core, *made)
        if iteration < ITERS - 1:
            if iteration == 0:
                outs = [((window, 4 * NB), f32)] + packed_outs
                coef, *made = whole_call(
                    functools.partial(domain_first, total_blocks),
                    outs,
                    [pltpu.VMEM((window, 4 * NB), f32)] + domain_scratch,
                    "domains",
                    smem=(0, 1),
                    count=8,
                    flops=fock_cost // 2,
                )(domain_blocks, other_lists, coefficients, other_coefficients, *packed)
            packed = total_over_grid(core, *made)
        else:
            outs = [(coefficients.shape, f32), ((PAIR, NB), f32), ((NB, NB), f32)] + [
                ((FINAL_ROWS, NB), f32)
            ] * 2
            result, near, keep, give, edge = whole_call(
                functools.partial(domain_last, total_blocks),
                outs,
                [pltpu.VMEM((window, 4 * NB), f32)] + domain_scratch,
                "domains_last",
                smem=(0, 1),
                count=7,
                flops=fock_cost // 2,
            )(domain_blocks, other_lists, coef, *packed)
            arrived_edge = to_edge(edge)
            arrived_core = to_core(give)
            (rows,) = whole_call(
                owner_kernel,
                [(density.shape, f32)],
                [pltpu.VMEM((2, 3, NB, NB), f32)],
                "owner_rows",
                count=5,
            )(near, keep, edge, arrived_core, arrived_edge)
    return (rows, result)


def solution(mesh):
    in_specs = (
        P("grid", None, "orb", None),
        P(("grid", "orb"), None, None),
        P(("grid", "orb"), None),
        P(("grid", "orb"), None),
        P(("grid", "orb"), None),
        P(("grid", "orb"), None),
        P(("grid", "orb"), None, None, None),
    )
    out_specs = (P("grid", None, "orb", None), P(("grid", "orb"), None, None, None))
    return jax.shard_map(shards, mesh=mesh, in_specs=in_specs, out_specs=out_specs, check_vma=False)
```

```python
import functools
import jax
import jax.numpy as jnp
from jax import lax
from jax.experimental import pallas as pl
from jax.experimental.pallas import tpu as pltpu
from jax.sharding import PartitionSpec as P

ITERS = 2
step_scale = 0.5

NB = 128
SB = 2 * NB
TILE = 8
HALF = NB // 2
PACKED = NB + TILE
VMEM_BYTES = 16 * 1024 * 1024
POINT_CHUNK = 256
f32 = jnp.float32
bf16 = jnp.bfloat16

LOW = slice(0, PACKED)
HIGH = slice(PACKED + HALF, 2 * PACKED + HALF)
A_ROWS = 2 * PACKED + HALF
B_ROWS = 2 * NB + HALF
PAIR = PACKED + NB
GIVE_ROWS = PAIR + HALF


def split(value):
    high = value.astype(bf16)
    return high, (value - high.astype(f32)).astype(bf16)


def dot3(left, right, contract=((1,), (0,))):
    def one(a, b):
        return lax.dot_general(a, b, (contract, ((), ())), preferred_element_type=f32)

    return one(left[0], right[0]) + (one(left[0], right[1]) + one(left[1], right[0]))


def both(pair, *index):
    return pair[0][index], pair[1][index]


def row_col():
    rows = lax.broadcasted_iota(jnp.int32, (NB, NB), 0)
    return rows, lax.broadcasted_iota(jnp.int32, (NB, NB), 1)


def aligned(value, unit):
    return pl.multiple_of(value * unit, unit)


def core_of():
    return lax.rem(lax.axis_index("grid"), 2)


def relative(block, total_blocks):
    anchor = (lax.axis_index("grid") - 1) * 2
    return lax.rem(block - anchor + total_blocks, total_blocks)


def whole_call(kernel, outs, scratch, name, smem=(), count=0, flops=0, moved=0):
    specs = [
        pl.BlockSpec(memory_space=pltpu.SMEM if i in smem else pltpu.VMEM) for i in range(count)
    ]
    return pl.pallas_call(
        kernel,
        out_shape=[jax.ShapeDtypeStruct(shape, kind) for shape, kind in outs],
        in_specs=specs,
        out_specs=[pl.BlockSpec(memory_space=pltpu.VMEM) for _ in outs],
        scratch_shapes=scratch,
        compiler_params=pltpu.CompilerParams(vmem_limit_bytes=VMEM_BYTES),
        cost_estimate=pl.CostEstimate(flops=flops, bytes_accessed=moved, transcendentals=0),
        name=name,
    )


def sort_kernel(total_blocks, blocks, basis, th, tl, nh, nl):
    for j in range(6):
        at = aligned(relative(blocks[0, j], total_blocks), NB)
        column = basis[:, j * NB : (j + 1) * NB]
        nh[:, pl.ds(at, NB)], nl[:, pl.ds(at, NB)] = split(column)
        th[pl.ds(at, NB), :], tl[pl.ds(at, NB), :] = split(column.T)


def pack_pair(pair_ref, at):
    rows, cols = row_col()
    first = pair_ref[at, :NB, :NB]
    last = pair_ref[at, NB:, NB:]
    merged = jnp.where(rows <= cols, first, last)
    diagonal = jnp.sum(jnp.where(rows == cols, last, 0.0), axis=0, keepdims=True)
    return merged, jnp.broadcast_to(diagonal, (TILE, NB)), pair_ref[at, :NB, NB:]


def store_packed(pair_ref, cross_ref, out_a, out_b, give, keep):
    core = core_of()
    for at, a_at, b_at in ((core, 0, 0), (core + 1, PACKED + HALF, NB + HALF)):
        merged, diagonal, off = pack_pair(pair_ref, at)
        out_a[a_at : a_at + NB, :] = merged
        out_a[a_at + NB : a_at + PACKED, :] = diagonal
        out_b[b_at : b_at + NB, :] = off
    out_a[PACKED : PACKED + HALF, :] = cross_ref[core, :HALF, :]
    out_b[NB : NB + HALF, :] = cross_ref[core, HALF:, :]
    merged, diagonal, off = pack_pair(pair_ref, 2 - 2 * core)
    give[:NB, :] = merged
    give[NB:PACKED, :] = diagonal
    give[PACKED:PAIR, :] = off
    give[PAIR:, :] = cross_ref[1 - core, pl.ds(aligned(1 - core, HALF), HALF), :]
    keep[...] = cross_ref[1 - core, pl.ds(aligned(core, HALF), HALF), :]


def store_final(pair_ref, cross_ref, turned_ref, own, give, edge):
    core = core_of()
    half = aligned(lax.axis_index("orb"), HALF)
    for j in range(2):
        turned_ref[j] = cross_ref[j].T

    def store_pair(at, target, first):
        for i in range(2):
            rows = pl.ds(half + i * NB, HALF)
            for j in range(2):
                index = 2 * i + j + 1 - first
                target[index] = pair_ref[at, rows, j * NB : (j + 1) * NB]

    def store_upper(target):
        target[0] = turned_ref[1, pl.ds(half, HALF), :]
        store_pair(2, target, 0)

    def store_lower(target):
        store_pair(0, target, 1)
        target[4] = cross_ref[0, pl.ds(half, HALF), :]

    own[0] = turned_ref[0, pl.ds(half, HALF), :]
    store_pair(1, own, 0)
    own[5] = cross_ref[1, pl.ds(half, HALF), :]

    @pl.when(core == 0)
    def _():
        store_upper(give)
        store_lower(edge)

    @pl.when(core == 1)
    def _():
        store_lower(give)
        store_upper(edge)


def load_packed(side_a, side_b, mid, other):
    core = core_of()
    pairs = [
        (core, side_a[:NB, :], side_a[NB : NB + 1, :], side_b[:NB, :]),
        (
            core + 1,
            side_a[PACKED + HALF : PACKED + HALF + NB, :],
            side_a[PACKED + HALF + NB : PACKED + HALF + NB + 1, :],
            side_b[NB + HALF :, :],
        ),
        (2 - 2 * core, other[:NB, :], other[NB : NB + 1, :], other[PACKED:PAIR, :]),
    ]
    return core, pairs


def load_cross(cross_ref, core, side_a, side_b, mid, other):
    cross_ref[core, :HALF, :] = side_a[PACKED : PACKED + HALF, :]
    cross_ref[core, HALF:, :] = side_b[NB : NB + HALF, :]
    cross_ref[1 - core, pl.ds(aligned(core, HALF), HALF), :] = mid[...]
    cross_ref[1 - core, pl.ds(aligned(1 - core, HALF), HALF), :] = other[PAIR:, :]


def unpack_pair(merged, diagonal):
    rows, cols = row_col()
    turned = merged.T
    first = jnp.where(rows <= cols, merged, turned)
    last = jnp.where(rows > cols, merged, jnp.where(rows < cols, turned, diagonal))
    return first, last


def fock_body(weights, external, basis_t, basis_n, pairs_ref, terms, scaled, pair_ref, cross_ref):
    points = weights.shape[1]
    pairs = [split(pairs_ref[j]) for j in range(3)]
    terms = [(row, col, split(value)) for row, col, value in terms]
    for start in range(0, points, POINT_CHUNK):
        cols = slice(start, start + POINT_CHUNK)

        def value_of(low, count):
            piece = both(basis_t, slice(low * NB, (low + count) * NB), cols)
            return piece, piece[0].astype(f32) + piece[1].astype(f32)

        rho = jnp.zeros((1, POINT_CHUNK), f32)
        for j in range(3):
            piece, value = value_of(2 * j, 2)
            rho = rho + jnp.sum(dot3(pairs[j], piece) * value, axis=0, keepdims=True)
        for row, col, matrix in terms:
            piece, _ = value_of(col, 1)
            _, value = value_of(row, 1)
            rho = rho + jnp.sum(dot3(matrix, piece) * value, axis=0, keepdims=True)
        potential = external[:, cols] - jnp.exp(jnp.log(rho * rho + 1.0) * (1.0 / 6.0))
        scale = weights[:, cols] * potential
        for j in range(3):
            _, value = value_of(2 * j, 2)
            high, low = split(value * scale)
            scaled[0][2 * j * NB : 2 * (j + 1) * NB, cols] = high
            scaled[1][2 * j * NB : 2 * (j + 1) * NB, cols] = low
    for j in range(3):
        first = 2 * j * NB - (NB if j else 0)
        left = both(scaled, slice(first, 2 * (j + 1) * NB), slice(None))
        block = dot3(left, both(basis_n, slice(None), slice(2 * j * NB, 2 * (j + 1) * NB)))
        if j:
            cross_ref[j - 1] = block[:NB, :NB]
            pair_ref[j] = block[NB:, :]
        else:
            pair_ref[j] = block


def fock_first(
    weights, external, th, tl, nh, nl, own, own_far, edge, edge_far, other, other_far,
    out_a, out_b, give, keep, dens, sh, sl, pair_ref, cross_ref, ends_ref,
):
    core = core_of()
    orb = lax.axis_index("orb")
    for at, places in (
        (1, ((own, 0, orb), (own_far, 0, 1 - orb))),
        (2 * core, ((edge, 0, orb), (edge_far, 1 - core, 1 - orb))),
        (2 - 2 * core, ((other, 0, orb), (other_far, 0, 1 - orb))),
    ):
        for source, first, half in places:
            for i in range(2):
                rows = pl.ds(aligned(half, HALF) + i * NB, HALF)
                for j in range(2):
                    index = 2 * i + j + 1 - first
                    dens[at, rows, j * NB : (j + 1) * NB] = source[index]
    ends = [
        (0, edge, 5, edge_far, 4, other, 5, other_far, 5),
        (1, own, 0, own_far, 0, own, 0, own_far, 0),
        (2, own, 5, own_far, 5, own, 5, own_far, 5),
        (3, other, 0, other_far, 0, edge, 0, edge_far, 0),
    ]
    mine = pl.ds(aligned(orb, HALF), HALF)
    theirs = pl.ds(aligned(1 - orb, HALF), HALF)
    for at, near_ref, a, near_far, b, far_ref, c, far_far, d in ends:
        ends_ref[at, mine, :] = jnp.where(core == 0, near_ref[a], far_ref[c])
        ends_ref[at, theirs, :] = jnp.where(core == 0, near_far[b], far_far[d])
    places = ((1, 2), (2, 1), (3, 4), (4, 3))
    terms = [(row, col, ends_ref[at]) for at, (row, col) in enumerate(places)]
    fock_body(
        weights, external, (th, tl), (nh, nl), dens, terms, (sh, sl), pair_ref, cross_ref
    )
    store_packed(pair_ref, cross_ref, out_a, out_b, give, keep)


def fock_later(
    weights, external, th, tl, nh, nl, side_a, side_b, mid, other,
    out_a, out_b, give, keep, dens, sh, sl, pair_ref, cross_ref, ends_ref,
):
    rows, cols = row_col()
    core, pairs = load_packed(side_a, side_b, mid, other)
    for at, merged, diagonal, off in pairs:
        twice = merged * 2.0
        dens[at, :NB, :NB] = jnp.where(rows < cols, twice, jnp.where(rows == cols, merged, 0.0))
        dens[at, NB:, NB:] = jnp.where(rows > cols, twice, jnp.where(rows == cols, diagonal, 0.0))
        dens[at, :NB, NB:] = off * 2.0
        dens[at, NB:, :NB] = jnp.zeros((NB, NB), f32)
    load_cross(cross_ref, core, side_a, side_b, mid, other)
    terms = [(1, 2, cross_ref[0] * 2.0), (3, 4, cross_ref[1] * 2.0)]
    fock_body(
        weights, external, (th, tl), (nh, nl), dens, terms, (sh, sl), pair_ref, cross_ref
    )
    store_packed(pair_ref, cross_ref, out_a, out_b, give, keep)


def domain_body(
    total_blocks, lists, coef, side_a, side_b, mid, other,
    fh, fl, gradient, moved, pair_ref, cross_ref,
):
    core, pairs = load_packed(side_a, side_b, mid, other)
    load_cross(cross_ref, core, side_a, side_b, mid, other)
    for at, merged, diagonal, off in pairs:
        first, last = unpack_pair(merged, diagonal)
        pair_ref[at, :NB, :NB] = first
        pair_ref[at, :NB, NB:] = off
        pair_ref[at, NB:, :NB] = off.T
        pair_ref[at, NB:, NB:] = last
    zero = jnp.zeros((NB, NB), f32)
    between = [(cross_ref[j], cross_ref[j].T) for j in range(2)]
    for j in range(3):
        top = NB if j else 0
        slab = [pair_ref[j]]
        if j:
            slab = [jnp.concatenate([between[j - 1][0], zero], axis=1)] + slab
        if j < 2:
            slab = slab + [jnp.concatenate([zero, between[j][1]], axis=1)]
        slab = jnp.concatenate(slab, axis=0)
        start = 2 * j * NB - top
        stop = start + slab.shape[0]
        product = dot3(split(slab), split(coef[2 * j * NB : 2 * (j + 1) * NB, :]))
        if j == 0:
            gradient[start:stop, :] = product
        else:
            seen = (2 * j + 1) * NB
            gradient[start:seen, :] += product[: seen - start]
            gradient[seen:stop, :] = product[seen - start :]
    domains = len(lists)
    mixed = []
    for d in range(domains):
        cols = slice(d * NB, (d + 1) * NB)
        mixed.append(dot3(split(coef[:, cols]), split(gradient[:, cols]), ((0,), (0,))))
    for d in range(0, domains, 2):
        cols = slice(d * NB, (d + 2) * NB)
        square = jnp.concatenate(
            [
                jnp.concatenate([mixed[d], zero], axis=1),
                jnp.concatenate([zero, mixed[d + 1]], axis=1),
            ],
            axis=0,
        )
        moved[:, cols] = dot3(split(coef[:, cols]), split(square))


def new_rows(total_blocks, lists, coef, gradient, moved):
    for d, (blocks, row) in enumerate(lists):
        cols = slice(d * NB, (d + 1) * NB)
        for i in range(4):
            at = aligned(relative(blocks[row, i], total_blocks), NB)
            rows = pl.ds(at, NB)
            value = coef[rows, cols] - step_scale * (gradient[rows, cols] - moved[rows, cols])
            yield d, i, rows, cols, value


def density_body(coef, pair_ref, cross_ref):
    pieces = split(coef[...])
    contract = ((1,), (1,))
    for j in range(3):
        piece = both(pieces, slice(2 * j * NB, 2 * (j + 1) * NB))
        pair_ref[j] = dot3(piece, piece, contract)
    for j in range(2):
        first = both(pieces, slice((2 * j + 1) * NB, (2 * j + 2) * NB))
        last = both(pieces, slice((2 * j + 2) * NB, (2 * j + 3) * NB))
        cross_ref[j] = dot3(first, last, contract)


def domain_first(
    total_blocks, own_lists, other_lists, own, partner, partner_last, side_a, side_b, mid, other,
    coef_out, out_a, out_b, give, keep, coef, gradient, moved, pair_ref, cross_ref,
):
    lists = [(own_lists, 0), (own_lists, 1), (other_lists, 0), (other_lists, 1)]
    coef[...] = jnp.zeros_like(coef)
    for d, (blocks, row) in enumerate(lists):
        for i in range(4):
            at = aligned(relative(blocks[row, i], total_blocks), NB)
            coef[pl.ds(at, NB), d * NB : (d + 1) * NB] = (
                own[row, i] if d < 2 else (partner, partner_last)[row][i]
            )
    domain_body(
        total_blocks, lists, coef, side_a, side_b, mid, other,
        None, None, gradient, moved, pair_ref, cross_ref,
    )
    coef_out[...] = jnp.zeros_like(coef_out)
    for _, _, rows, cols, value in new_rows(total_blocks, lists, coef, gradient, moved):
        coef_out[rows, cols] = value
    density_body(coef_out, pair_ref, cross_ref)
    store_packed(pair_ref, cross_ref, out_a, out_b, give, keep)


def domain_last(
    total_blocks, own_lists, other_lists, coef, side_a, side_b, mid, other,
    result, own, give, edge, fresh, gradient, moved, pair_ref, cross_ref, turned_ref,
):
    lists = [(own_lists, 0), (own_lists, 1), (other_lists, 0), (other_lists, 1)]
    domain_body(
        total_blocks, lists, coef, side_a, side_b, mid, other,
        None, None, gradient, moved, pair_ref, cross_ref,
    )
    fresh[...] = jnp.zeros_like(fresh)
    for d, i, rows, cols, value in new_rows(total_blocks, lists, coef, gradient, moved):
        fresh[rows, cols] = value
        if d < 2:
            result[d, i] = value
    density_body(fresh, pair_ref, cross_ref)
    store_final(pair_ref, cross_ref, turned_ref, own, give, edge)


def owner_kernel(own, from_core, from_edge, out):
    core = core_of()
    lower = jnp.where(core == 0, from_core[...], from_edge[...])
    upper = jnp.where(core == 0, from_edge[...], from_core[...])
    out[0] = own[0] + upper[0]
    out[1:5] = own[1:5] + upper[1:] + lower[:4]
    out[5] = own[5] + lower[4]


def to_core(value):
    count = lax.axis_size("grid")
    return lax.ppermute(value, "grid", [(i, i ^ 1) for i in range(count)])


def to_edge(value):
    count = lax.axis_size("grid")
    route = [(i, (i + 1) % count if i % 2 else (i - 1) % count) for i in range(count)]
    return lax.ppermute(value, "grid", route)


def to_orb(value):
    return lax.ppermute(value, "orb", [(0, 1), (1, 0)])


def add_near(core, side_a, side_b, keep, arrived):
    packed, off = arrived[:PACKED], arrived[PACKED:PAIR]

    def placed(piece, gap):
        zero = jnp.zeros_like(piece)
        parts = [
            jnp.where(core == 1, piece, zero),
            jnp.zeros((gap, NB), f32),
            jnp.where(core == 0, piece, zero),
        ]
        return jnp.concatenate(parts, axis=0)

    return side_a + placed(packed, HALF), side_b + placed(off, HALF), keep + arrived[PAIR:]


def near_part(core, side_a, side_b, mid):
    packed = lax.dynamic_slice_in_dim(side_a, (1 - core) * (PACKED + HALF), PACKED, 0)
    off = lax.dynamic_slice_in_dim(side_b, (1 - core) * (NB + HALF), NB, 0)
    return jnp.concatenate([packed, off, mid], axis=0)


def total_over_all(core, side_a, side_b, give, keep):
    side_a, side_b, keep = add_near(core, side_a, side_b, keep, to_core(give))
    first_a = to_orb(side_a)
    first_b = to_edge(side_b)
    side_a = side_a + first_a
    side_b = side_b + first_b
    last_a = to_edge(side_a)
    last_b = to_orb(jnp.concatenate([side_b, keep], axis=0))
    side_a = side_a + last_a
    side_b = side_b + last_b[:B_ROWS]
    keep = keep + last_b[B_ROWS:]
    return side_a, side_b, keep, to_core(near_part(core, side_a, side_b, keep))


def total_over_grid(core, side_a, side_b, give, keep):
    side_a, side_b, keep = add_near(core, side_a, side_b, keep, to_core(give))
    arrived = to_edge(jnp.concatenate([side_a, side_b], axis=0))
    side_a = side_a + arrived[:A_ROWS]
    side_b = side_b + arrived[A_ROWS:]
    return side_a, side_b, keep, to_core(near_part(core, side_a, side_b, keep))


def shards(
    density, basis_values, quad_weights, ext_potential, batch_blocks, domain_blocks, coefficients
):
    total_blocks = density.shape[0] * lax.axis_size("grid")
    points = basis_values.shape[1]
    core = lax.rem(lax.axis_index("grid"), 2)
    window = 6 * NB
    half_shape, full_shape = (points, window), (window, points)
    packed_outs = [((A_ROWS, NB), f32), ((B_ROWS, NB), f32), ((GIVE_ROWS, NB), f32), ((HALF, NB), f32)]
    band_scratch = [pltpu.VMEM((3, SB, SB), f32), pltpu.VMEM((2, NB, NB), f32)]

    basis = whole_call(
        functools.partial(sort_kernel, total_blocks),
        [(full_shape, bf16)] * 2 + [(half_shape, bf16)] * 2,
        [],
        "sort_basis",
        smem=(0,),
        count=2,
        moved=12 * points * window,
    )(batch_blocks, basis_values[0])

    own = density.reshape(6, HALF, NB)
    edge = to_edge(own)
    own_far = to_orb(own)
    other = to_core(own)
    other_far = to_core(own_far)
    edge_far = to_orb(lax.dynamic_slice_in_dim(edge, 1 - core, 5, 0))
    window_density = (own, own_far, edge, edge_far, other, other_far)
    coefficients_ready, edge_far = lax.optimization_barrier((coefficients, edge_far))
    window_density = (own, own_far, edge, edge_far, other, other_far)
    partner_coefficients = to_orb(coefficients_ready[0])
    other_lists = to_orb(domain_blocks)

    fock_scratch = [
        pltpu.VMEM((3, SB, SB), f32),
        pltpu.VMEM(full_shape, bf16),
        pltpu.VMEM(full_shape, bf16),
    ] + band_scratch + [pltpu.VMEM((4, NB, NB), f32)]
    domain_scratch = [pltpu.VMEM((window, 4 * NB), f32)] * 2 + band_scratch
    fock_cost = 2 * 3 * 8 * points * SB * SB

    coef = None
    packed = None
    for iteration in range(ITERS):
        if iteration == 0:
            kernel, operands = fock_first, window_density
        else:
            kernel, operands = fock_later, packed
        made = whole_call(
            kernel, packed_outs, fock_scratch, "fock", count=6 + len(operands), flops=fock_cost
        )(quad_weights, ext_potential, *basis, *operands)
        if iteration == 0:
            give, partner_coefficients, other_lists, rest = lax.optimization_barrier(
                (made[2], partner_coefficients, other_lists, coefficients[1])
            )
            made = (made[0], made[1], give, made[3])
            partner_last = to_orb(rest)
        packed = total_over_all(core, *made)
        if iteration < ITERS - 1:
            if iteration == 0:
                outs = [((window, 4 * NB), f32)] + packed_outs
                coef, *made = whole_call(
                    functools.partial(domain_first, total_blocks),
                    outs,
                    [pltpu.VMEM((window, 4 * NB), f32)] + domain_scratch,
                    "domains",
                    smem=(0, 1),
                    count=9,
                    flops=fock_cost // 2,
                )(domain_blocks, other_lists, coefficients, partner_coefficients, partner_last, *packed)
            packed = total_over_grid(core, *made)
        else:
            message = ((5, HALF, NB), f32)
            outs = [(coefficients.shape, f32), ((6, HALF, NB), f32), message, message]
            result, own, give, edge = whole_call(
                functools.partial(domain_last, total_blocks),
                outs,
                [pltpu.VMEM((window, 4 * NB), f32)]
                + domain_scratch
                + [pltpu.VMEM((2, NB, NB), f32)],
                "domains_last",
                smem=(0, 1),
                count=7,
                flops=fock_cost // 2,
            )(domain_blocks, other_lists, coef, *packed)
            arrived_edge = to_edge(edge)
            arrived_core = to_core(give)
            (rows,) = whole_call(
                owner_kernel, [((6, HALF, NB), f32)], [], "owner_rows", count=3
            )(own, arrived_core, arrived_edge)
            rows = rows.reshape(density.shape)
    return (rows, result)


def solution(mesh):
    in_specs = (
        P("grid", None, "orb", None),
        P(("grid", "orb"), None, None),
        P(("grid", "orb"), None),
        P(("grid", "orb"), None),
        P(("grid", "orb"), None),
        P(("grid", "orb"), None),
        P(("grid", "orb"), None, None, None),
    )
    out_specs = (P("grid", None, "orb", None), P(("grid", "orb"), None, None, None))
    return jax.shard_map(shards, mesh=mesh, in_specs=in_specs, out_specs=out_specs, check_vma=False)
```

```python
import functools
import jax
import jax.numpy as jnp
from jax import lax
from jax.experimental import pallas as pl
from jax.experimental.pallas import tpu as pltpu
from jax.sharding import PartitionSpec as P

ITERS = 2
step_scale = 0.5

NB = 128
SB = 2 * NB
TILE = 8
HALF = NB // 2
PACKED = NB + TILE
VMEM_BYTES = 16 * 1024 * 1024
POINT_CHUNK = 256
f32 = jnp.float32
bf16 = jnp.bfloat16

LOW = slice(0, PACKED)
HIGH = slice(PACKED + HALF, 2 * PACKED + HALF)
A_ROWS = 2 * PACKED + HALF
B_ROWS = 2 * NB + HALF
PAIR = PACKED + NB
GIVE_ROWS = PAIR + HALF
EARLY = 9
KEEP_AT = 2 * NB + HALF


def split(value):
    high = value.astype(bf16)
    return high, (value - high.astype(f32)).astype(bf16)


def dot3(left, right, contract=((1,), (0,))):
    def one(a, b):
        return lax.dot_general(a, b, (contract, ((), ())), preferred_element_type=f32)

    return one(left[0], right[0]) + (one(left[0], right[1]) + one(left[1], right[0]))


def both(pair, *index):
    return pair[0][index], pair[1][index]


def row_col():
    rows = lax.broadcasted_iota(jnp.int32, (NB, NB), 0)
    return rows, lax.broadcasted_iota(jnp.int32, (NB, NB), 1)


def aligned(value, unit):
    return pl.multiple_of(value * unit, unit)


def core_of():
    return lax.rem(lax.axis_index("grid"), 2)


def relative(block, total_blocks):
    anchor = (lax.axis_index("grid") - 1) * 2
    return lax.rem(block - anchor + total_blocks, total_blocks)


def vmem(shape, kind=f32):
    return pltpu.VMEM(shape, kind)


def call(kernel, operands, outs, name, scratch=(), smem=(), plain=(), flops=0):
    specs, pinned = [], []
    for i, operand in enumerate(operands):
        specs.append(pl.BlockSpec(memory_space=pltpu.SMEM if i in smem else pltpu.VMEM))
        if i in smem or i in plain:
            pinned.append(hbm(operand) if i in smem else operand)
        else:
            pinned.append(pltpu.with_memory_space_constraint(operand, pltpu.VMEM))
    return pl.pallas_call(
        kernel,
        out_shape=list(outs),
        in_specs=specs,
        out_specs=[pl.BlockSpec(memory_space=pltpu.VMEM) for _ in outs],
        scratch_shapes=list(scratch),
        compiler_params=pltpu.CompilerParams(vmem_limit_bytes=VMEM_BYTES),
        cost_estimate=pl.CostEstimate(flops=flops, bytes_accessed=0, transcendentals=0),
        name=name,
    )(*pinned)


def sort_kernel(total_blocks, blocks, basis, th, tl, nh, nl, done, columns, arrived):
    def copy(j):
        source = basis.at[0, :, pl.ds(j * NB, NB)]
        return pltpu.make_async_copy(source, columns.at[j], arrived.at[j])

    for j in range(6):
        copy(j).start()
    for j in range(6):
        at = pl.ds(aligned(relative(blocks[0, j], total_blocks), NB), NB)
        copy(j).wait()
        column = columns[j]
        nh[:, at], nl[:, at] = split(column)
        th[at, :], tl[at, :] = split(column.T)
    done[...] = jnp.zeros_like(done)


def cut_kernel(own, halves, other, near, early, rest, sems):
    copies = [
        pltpu.make_async_copy(own, near, sems.at[0]),
        pltpu.make_async_copy(halves.at[pl.ds(0, EARLY)], early, sems.at[1]),
        pltpu.make_async_copy(halves.at[pl.ds(EARLY, 16 - EARLY)], rest, sems.at[2]),
    ]
    for copy in copies:
        copy.start()
    for copy in copies:
        copy.wait()


def hbm(value):
    return pltpu.with_memory_space_constraint(value, pltpu.HBM)


def cut(own, halves, other):
    return pl.pallas_call(
        cut_kernel,
        out_shape=[vmem(own.shape), vmem((EARLY, HALF, NB)), vmem((16 - EARLY, HALF, NB))],
        in_specs=[pl.BlockSpec(memory_space=pl.ANY)] * 2 + [pl.BlockSpec(memory_space=pltpu.VMEM)],
        out_specs=[pl.BlockSpec(memory_space=pltpu.VMEM)] * 3,
        scratch_shapes=[pltpu.SemaphoreType.DMA((3,))],
        compiler_params=pltpu.CompilerParams(vmem_limit_bytes=VMEM_BYTES),
        name="cut",
    )(hbm(own), hbm(halves), other)


def hold_kernel(value, done, out):
    out[...] = value[...]


def sort_basis(total_blocks, batch_blocks, basis_values, unit):
    points, window = basis_values.shape[1:]
    halves = [vmem((window, points), bf16)] * 2 + [vmem((points, window), bf16)] * 2
    return pl.pallas_call(
        functools.partial(sort_kernel, total_blocks),
        out_shape=halves + [vmem((TILE, NB))],
        in_specs=[pl.BlockSpec(memory_space=pltpu.SMEM), pl.BlockSpec(memory_space=pl.ANY)],
        out_specs=[pl.BlockSpec(memory_space=pltpu.VMEM)] * 5,
        scratch_shapes=[vmem((6, points, NB)), pltpu.SemaphoreType.DMA((6,))],
        compiler_params=pltpu.CompilerParams(vmem_limit_bytes=VMEM_BYTES),
        cost_estimate=pl.CostEstimate(flops=6 * unit, bytes_accessed=0, transcendentals=0),
        name="sort_basis",
    )(hbm(batch_blocks), hbm(basis_values))


def put_pair(pair, packed, off):
    rows, cols = row_col()
    first, last = pair[:NB, :NB], pair[NB:, NB:]
    diagonal = jnp.sum(jnp.where(rows == cols, last, 0.0), axis=0, keepdims=True)
    packed[:NB, :] = jnp.where(rows <= cols, first, last)
    packed[NB:PACKED, :] = jnp.broadcast_to(diagonal, (TILE, NB))
    off[...] = pair[:NB, NB:]


def put_side(low, cross, high, side_a, side_b):
    put_pair(low, side_a.at[LOW], side_b.at[:NB])
    put_pair(high, side_a.at[HIGH], side_b.at[KEEP_AT - NB : KEEP_AT])
    side_a[PACKED : PACKED + HALF, :] = cross[:HALF]
    side_b[NB : NB + HALF, :] = cross[HALF:]


def put_other(pair, cross_ref, give, keep):
    core = core_of()
    put_pair(pair, give.at[:PACKED], give.at[PACKED:PAIR])
    give[PAIR:, :] = cross_ref[pl.ds(aligned(1 - core, HALF), HALF), :]
    keep[...] = cross_ref[pl.ds(aligned(core, HALF), HALF), :]


def side_parts(side_a, side_b):
    low = (side_a[:NB, :], side_a[NB : NB + 1, :], side_b[:NB, :])
    start = PACKED + HALF
    high = (
        side_a[start : start + NB, :],
        side_a[start + NB : start + NB + 1, :],
        side_b[NB + HALF : KEEP_AT, :],
    )
    cross = jnp.concatenate([side_a[PACKED:start, :], side_b[NB : NB + HALF, :]], axis=0)
    return low, cross, high


def other_parts(side_b, other, cross_ref):
    core = core_of()
    cross_ref[pl.ds(aligned(core, HALF), HALF), :] = side_b[KEEP_AT:, :]
    cross_ref[pl.ds(aligned(1 - core, HALF), HALF), :] = other[PAIR:, :]
    return (other[:NB, :], other[NB : NB + 1, :], other[PACKED:PAIR, :]), cross_ref[...]


def unpack(part):
    merged, diagonal, off = part
    rows, cols = row_col()
    turned = merged.T
    first = jnp.where(rows <= cols, merged, turned)
    last = jnp.where(rows > cols, merged, jnp.where(rows < cols, turned, diagonal))
    return join(first, off, off.T, last)


def join(a, b, c, d):
    return jnp.concatenate(
        [jnp.concatenate([a, b], axis=1), jnp.concatenate([c, d], axis=1)], axis=0
    )


def upper_form(part):
    merged, diagonal, off = part
    rows, cols = row_col()
    twice = merged * 2.0
    first = jnp.where(rows < cols, twice, jnp.where(rows == cols, merged, 0.0))
    last = jnp.where(rows > cols, twice, jnp.where(rows == cols, diagonal, 0.0))
    return join(first, off * 2.0, jnp.zeros((NB, NB), f32), last)


def near_kernel(side_a, side_b, keep, arrived, out_a, out_b, out_keep):
    core = core_of()
    out_a[...] = side_a[...]
    out_b[...] = side_b[...]
    out_keep[...] = keep[...] + arrived[PAIR:, :]
    rows_a = pl.ds(pl.multiple_of((1 - core) * (PACKED + HALF), TILE), PACKED)
    rows_b = pl.ds(pl.multiple_of((1 - core) * (NB + HALF), TILE), NB)
    out_a[rows_a, :] = side_a[rows_a, :] + arrived[:PACKED, :]
    out_b[rows_b, :] = side_b[rows_b, :] + arrived[PACKED:PAIR, :]


def add_kernel(left, right, out):
    out[...] = left[...] + right[...]


def add_keep_kernel(side_b, arrived, keep, out):
    out[:KEEP_AT, :] = side_b[...] + arrived[...]
    out[KEEP_AT:, :] = keep[...]


def side_near(out_a, out_b, near):
    core = core_of()
    rows_a = pl.ds(pl.multiple_of((1 - core) * (PACKED + HALF), TILE), PACKED)
    rows_b = pl.ds(pl.multiple_of((1 - core) * (NB + HALF), TILE), NB)
    near[:PACKED, :] = out_a[rows_a, :]
    near[PACKED:PAIR, :] = out_b[rows_b, :]
    near[PAIR:, :] = out_b[KEEP_AT:, :]


def total_kernel(side_a, arrived_a, side_b, arrived_b, out_a, out_b, near):
    out_a[...] = side_a[...] + arrived_a[...]
    out_b[...] = side_b[...] + arrived_b[...]
    side_near(out_a, out_b, near)


def join_kernel(side_a, side_b, keep, arrived, out, out_keep):
    near_kernel(side_a, side_b, keep, arrived, out.at[:A_ROWS], out.at[A_ROWS:], out_keep)


def total_grid_kernel(side, arrived, keep, out_a, out_b, near):
    out_a[...] = side[:A_ROWS, :] + arrived[:A_ROWS, :]
    out_b[:KEEP_AT, :] = side[A_ROWS:, :] + arrived[A_ROWS:, :]
    out_b[KEEP_AT:, :] = keep[...]
    side_near(out_a, out_b, near)


def add_density(terms, th, tl, before, after):
    points = th.shape[1]
    for start in range(0, points, POINT_CHUNK):
        cols = slice(start, start + POINT_CHUNK)
        rho = before(cols)
        for matrix, at, count, values in terms:
            rows = pl.ds(pl.multiple_of(at, HALF), count)
            value = []
            for value_at, value_count in values:
                value_rows = pl.ds(pl.multiple_of(value_at, HALF), value_count)
                value.append(th[value_rows, cols].astype(f32) + tl[value_rows, cols].astype(f32))
            value = value[0] if len(value) == 1 else jnp.concatenate(value, axis=0)
            product = dot3(matrix, (th[rows, cols], tl[rows, cols]))
            rho = rho + jnp.sum(product * value, axis=0, keepdims=True)
        after(cols, rho)


def half_terms(source, first, pair, half, ends):
    body = join(*[source[2 * i + j + 1 - first] for i in range(2) for j in range(2)])
    at = pair * SB
    rows = [(at + half * HALF, HALF), (at + NB + half * HALF, HALF)]
    terms = [(split(body), at, SB, rows)]
    for index, row, col in ends:
        terms.append((split(source[index]), col * NB, NB, [(row * NB + half * HALF, HALF)]))
    return terms


def rho_first(th, tl, own, own_far, edge, other, other_far, early, rho):
    core = core_of()
    orb = lax.axis_index("orb")
    own_ends = ((0, 2, 1), (5, 3, 4))
    other_ends = ((5 * core, 4 - 3 * core, 3 - core),)
    edge_ends = ((5 - 5 * core, 1 + 3 * core, 2 + core),)
    terms = (
        half_terms(own, 0, 1, orb, own_ends)
        + half_terms(own_far, 0, 1, 1 - orb, own_ends)
        + half_terms(other, 0, 2 - 2 * core, orb, other_ends)
        + half_terms(other_far, 0, 2 - 2 * core, 1 - orb, other_ends)
        + half_terms(edge, 0, 2 * core, orb, edge_ends)
    )

    def store(cols, value):
        rho[:, cols] = value

    add_density(terms, th, tl, lambda cols: jnp.zeros((1, POINT_CHUNK), f32), store)


def far_kernel(lists, edge, sorted_first, out):
    first = 1 - core_of()
    for i in range(5):
        out[i * HALF : (i + 1) * HALF, :] = edge[i + first]
    lanes = lax.broadcasted_iota(jnp.int32, (TILE, NB), 1)
    row = jnp.zeros((TILE, NB), f32)
    for d in range(2):
        for i in range(4):
            row = jnp.where(lanes == 4 * d + i, lists[d, i].astype(f32), row)
    out[5 * HALF :, :] = row


def rho_side(th, tl, side_a, side_b, rho):
    core = core_of()
    low, cross, high = side_parts(side_a, side_b)
    at = core * SB
    terms = [
        (split(upper_form(low)), at, SB, [(at, SB)]),
        (split(upper_form(high)), at + SB, SB, [(at + SB, SB)]),
        (split(cross * 2.0), at + SB, NB, [(at + NB, NB)]),
    ]

    def store(cols, value):
        rho[:, cols] = value

    add_density(terms, th, tl, lambda cols: jnp.zeros((1, POINT_CHUNK), f32), store)


def scaled_rows(th, tl, at, count, scale):
    rows = pl.ds(pl.multiple_of(at, NB), count)
    return split((th[rows, :].astype(f32) + tl[rows, :].astype(f32)) * scale[...])


def fock_block(left, nh, nl, at, count):
    cols = pl.ds(pl.multiple_of(at, NB), count)
    return dot3(left, (nh[:, cols], nl[:, cols]))


def fock_other(terms, weights, external, th, tl, nh, nl, rho, scale, give, keep, cross_ref):
    core = core_of()

    def store(cols, value):
        potential = external[:, cols] - jnp.exp(jnp.log(value * value + 1.0) * (1.0 / 6.0))
        scale[:, cols] = weights[:, cols] * potential

    add_density(terms, th, tl, lambda cols: rho[:, cols], store)
    at = (2 - 2 * core) * SB
    pair = fock_block(scaled_rows(th, tl, at, SB, scale), nh, nl, at, SB)
    row = (3 - 2 * core) * NB
    cross_ref[...] = fock_block(scaled_rows(th, tl, row, NB, scale), nh, nl, row + NB, NB)
    put_other(pair, cross_ref, give, keep)


def fock_other_first(
    weights, external, th, tl, nh, nl, rho, edge_far, scale, give, keep, cross_ref
):
    core = core_of()
    ends = ((4 - 4 * core, 1 + 3 * core, 2 + core),)

    def far(index):
        return edge_far[pl.ds(aligned(index, HALF), HALF), :]

    body = join(*[far(2 * i + j + core) for i in range(2) for j in range(2)])
    half = 1 - lax.axis_index("orb")
    at = 2 * core * SB
    rows = [(at + half * HALF, HALF), (at + NB + half * HALF, HALF)]
    terms = [(split(body), at, SB, rows)]
    for index, row, col in ends:
        terms.append((split(far(index)), col * NB, NB, [(row * NB + half * HALF, HALF)]))
    fock_other(terms, weights, external, th, tl, nh, nl, rho, scale, give, keep, cross_ref)


def fock_other_later(
    weights, external, th, tl, nh, nl, rho, side_b, other, scale, give, keep, cross_ref
):
    core = core_of()
    part, cross = other_parts(side_b, other, cross_ref)
    at = (2 - 2 * core) * SB
    row = (3 - 2 * core) * NB
    terms = [
        (split(upper_form(part)), at, SB, [(at, SB)]),
        (split(cross * 2.0), row + NB, NB, [(row, NB)]),
    ]
    fock_other(terms, weights, external, th, tl, nh, nl, rho, scale, give, keep, cross_ref)


def fock_side(th, tl, nh, nl, scale, side_a, side_b):
    at = core_of() * SB
    low = fock_block(scaled_rows(th, tl, at, SB, scale), nh, nl, at, SB)
    both_rows = fock_block(scaled_rows(th, tl, at + NB, 3 * NB, scale), nh, nl, at + SB, SB)
    put_side(low, both_rows[:NB, :NB], both_rows[NB:], side_a, side_b)


def coefficient_parts(value, high, low, turned_high, turned_low):
    high[...], low[...] = split(value)
    turned_high[...], turned_low[...] = split(value.T)


def spread_kernel(
    total_blocks, own_lists, other_lists, own, early, partner, coef, ch, cl, th, tl
):
    coef[...] = jnp.zeros_like(coef)
    for d in range(4):
        for i in range(4):
            blocks = own_lists if d < 2 else other_lists
            at = aligned(relative(blocks[d % 2, i], total_blocks), NB)
            cols = slice(d * NB, (d + 1) * NB)
            if d < 2:
                coef[pl.ds(at, NB), cols] = own[4 * d + i]
                continue
            for half in range(2):
                index = 2 * (4 * (d - 2) + i) + half
                value = early[index] if index < EARLY else partner[index - EARLY]
                coef[pl.ds(at + half * HALF, HALF), cols] = value
    coefficient_parts(coef[...], ch, cl, th, tl)


def turn_kernel(coef, th, tl):
    th[...], tl[...] = split(coef[...].T)


def mixing(th, tl, at, count, gradient):
    cols = pl.ds(pl.multiple_of(at, NB), count)
    return [
        dot3((th[d * NB : (d + 1) * NB, cols], tl[d * NB : (d + 1) * NB, cols]), both(gradient, slice(None), slice(d * NB, (d + 1) * NB)))
        for d in range(4)
    ]


def domain_side(side_a, side_b, ch, cl, th, tl, gradient, mixed):
    low, cross, high = side_parts(side_a, side_b)
    at = core_of() * SB
    zero = jnp.zeros((NB, NB), f32)
    first = jnp.concatenate([unpack(low), jnp.concatenate([zero, cross.T], axis=1)], axis=0)
    last = jnp.concatenate([jnp.concatenate([cross, zero], axis=1), unpack(high)], axis=0)

    def coef(start):
        rows = pl.ds(pl.multiple_of(start, SB), SB)
        return ch[rows, :], cl[rows, :]

    upper = dot3(split(first), coef(at))
    lower = dot3(split(last), coef(at + SB))
    gradient[:NB, :] = upper[:NB]
    gradient[NB : 3 * NB, :] = upper[NB:] + lower[: 2 * NB]
    gradient[3 * NB :, :] = lower[2 * NB :]
    for d, value in enumerate(mixing(th, tl, at, 4 * NB, split(gradient[...]))):
        mixed[d] = value


def domain_new(
    total_blocks, own_lists, other_lists, coef, ch, cl, th, tl, gradient, mixed, side_b, other,
    fresh, fh, fl, work, cross_ref,
):
    core = core_of()
    part, cross = other_parts(side_b, other, cross_ref)
    zero = jnp.zeros((NB, NB), f32)
    beside = jnp.where(core == 0, cross, cross.T)
    across = jnp.where(core == 0, cross.T, cross)
    placed = jnp.concatenate(
        [jnp.where(core == 0, beside, zero), jnp.where(core == 0, zero, beside)], axis=1
    )
    slab = jnp.concatenate([unpack(part), placed], axis=0)
    other_at = (2 - 2 * core) * SB
    other_rows = pl.ds(pl.multiple_of(other_at, SB), SB)
    side_block = pl.ds(pl.multiple_of((3 - core) * NB, NB), NB)
    touching = pl.ds(pl.multiple_of((4 - 3 * core) * NB, NB), NB)
    work[pl.ds(pl.multiple_of(core * SB, SB), 4 * NB), :] = gradient[...]
    product = dot3(split(slab), (ch[other_rows, :], cl[other_rows, :]))
    work[other_rows, :] = product[:SB]
    back = dot3(split(across), (ch[side_block, :], cl[side_block, :]))
    work[touching, :] += back
    work[side_block, :] += product[SB:]
    first = mixing(th, tl, other_at, SB, split(work[other_rows, :]))
    second = mixing(th, tl, (3 - core) * NB, NB, split(product[SB:]))
    total = [mixed[d] + first[d] + second[d] for d in range(4)]
    for d in range(0, 4, 2):
        cols = slice(d * NB, (d + 2) * NB)
        square = split(join(total[d], zero, zero, total[d + 1]))
        moved = dot3((ch[:, cols], cl[:, cols]), square)
        for r in range(6):
            rows = slice(r * NB, (r + 1) * NB)
            for e in range(2):
                blocks = own_lists if d == 0 else other_lists
                present = relative(blocks[e, 0], total_blocks) == r
                for i in range(1, 4):
                    present = present | (relative(blocks[e, i], total_blocks) == r)
                at = slice((d + e) * NB, (d + e + 1) * NB)
                kept = jnp.where(present, work[rows, at], 0.0)
                value = coef[rows, at] - step_scale * (kept - moved[rows, e * NB : (e + 1) * NB])
                fresh[rows, at] = value
                fh[rows, at], fl[rows, at] = split(value)


def outer(fh, fl, at, count, from_at, from_count):
    left = pl.ds(pl.multiple_of(at, HALF), count)
    right = pl.ds(pl.multiple_of(from_at, NB), from_count)
    return dot3((fh[left, :], fl[left, :]), (fh[right, :], fl[right, :]), ((1,), (1,)))


def domain_other(
    total_blocks, own_lists, other_lists, coef, ch, cl, th, tl, gradient, mixed, side_b, other,
    fresh, fh, fl, give, keep, work, cross_ref,
):
    domain_new(
        total_blocks, own_lists, other_lists, coef, ch, cl, th, tl, gradient, mixed, side_b,
        other, fresh, fh, fl, work, cross_ref,
    )
    core = core_of()
    at = (2 - 2 * core) * SB
    row = (3 - 2 * core) * NB
    cross_ref[...] = outer(fh, fl, row, NB, row + NB, NB)
    put_other(outer(fh, fl, at, SB, at, SB), cross_ref, give, keep)


def density_side(fh, fl, side_a, side_b):
    at = core_of() * SB
    cross = outer(fh, fl, at + NB, NB, at + SB, NB)
    put_side(
        outer(fh, fl, at, SB, at, SB), cross, outer(fh, fl, at + SB, SB, at + SB, SB),
        side_a, side_b,
    )


def owner_half(fh, fl, pair, target, first):
    half = lax.axis_index("orb") * HALF
    for i in range(2):
        rows = outer(fh, fl, pair * SB + i * NB + half, HALF, pair * SB, SB)
        target[2 * i + 1 - first] = rows[:, :NB]
        target[2 * i + 2 - first] = rows[:, NB:]


def end_half(fh, fl, row, col):
    return outer(fh, fl, row * NB + lax.axis_index("orb") * HALF, HALF, col * NB, NB)


def domain_edge(
    total_blocks, own_lists, other_lists, coef, ch, cl, th, tl, gradient, mixed, side_b, other,
    fresh, fh, fl, edge, give, work, cross_ref,
):
    domain_new(
        total_blocks, own_lists, other_lists, coef, ch, cl, th, tl, gradient, mixed, side_b,
        other, fresh, fh, fl, work, cross_ref,
    )
    core = core_of()
    owner_half(fh, fl, 2 * core, edge, 1 - core)
    edge[4 - 4 * core] = end_half(fh, fl, 1 + 3 * core, 2 + core)
    owner_half(fh, fl, 2 - 2 * core, give, core)
    give[4 * core] = end_half(fh, fl, 4 - 3 * core, 3 - core)


def domain_last(total_blocks, own_lists, fresh, fh, fl, result, own):
    owner_half(fh, fl, 1, own, 0)
    own[0] = end_half(fh, fl, 2, 1)
    own[5] = end_half(fh, fl, 3, 4)
    for d in range(2):
        for i in range(4):
            at = aligned(relative(own_lists[d, i], total_blocks), NB)
            result[d, i] = fresh[pl.ds(at, NB), d * NB : (d + 1) * NB]


def owner_kernel(own, from_core, from_edge, out):
    core = core_of()
    lower = jnp.where(core == 0, from_core[...], from_edge[...])
    upper = jnp.where(core == 0, from_edge[...], from_core[...])
    out[0] = own[0] + upper[0]
    out[1:5] = own[1:5] + upper[1:] + lower[:4]
    out[5] = own[5] + lower[4]


def to_core(value):
    count = lax.axis_size("grid")
    return lax.ppermute(value, "grid", [(i, i ^ 1) for i in range(count)])


def to_edge(value):
    count = lax.axis_size("grid")
    route = [(i, (i + 1) % count if i % 2 else (i - 1) % count) for i in range(count)]
    return lax.ppermute(value, "grid", route)


def to_orb(value):
    return lax.ppermute(value, "orb", [(0, 1), (1, 0)])


A_OUT = vmem((A_ROWS, NB))
B_OUT = vmem((B_ROWS, NB))
BK_OUT = vmem((B_ROWS + HALF, NB))
GIVE_OUT = vmem((GIVE_ROWS, NB))
KEEP_OUT = vmem((HALF, NB))
CROSS = vmem((NB, NB))


def total_over_all(made, before_last, before_sum):
    side_a, side_b, keep, arrived = made
    side_a, side_b, keep = call(
        near_kernel, (side_a, side_b, keep, arrived), (A_OUT, B_OUT, KEEP_OUT), "add_near"
    )
    first_b = to_edge(side_b)
    first_a = to_orb(side_a)
    (side_a,) = call(add_kernel, (side_a, first_a), (A_OUT,), "add_a")
    (side_b,) = call(add_keep_kernel, (side_b, first_b, keep), (BK_OUT,), "add_b")
    last_a = to_edge(side_a)
    side_b = before_last(side_b)
    last_b = before_sum(to_orb(side_b))
    side_a, side_b, near = call(
        total_kernel, (side_a, last_a, side_b, last_b), (A_OUT, BK_OUT, GIVE_OUT), "add_all"
    )
    return side_a, side_b, to_core(near)


def total_over_grid(made):
    side_a, side_b, keep, arrived = made
    side, keep = call(
        join_kernel,
        (side_a, side_b, keep, arrived),
        (vmem((A_ROWS + B_ROWS, NB)), KEEP_OUT),
        "add_near",
    )
    side_a, side_b, near = call(
        total_grid_kernel, (side, to_edge(side), keep), (A_OUT, BK_OUT, GIVE_OUT), "add_all"
    )
    return side_a, side_b, to_core(near)


def shards(
    density, basis_values, quad_weights, ext_potential, batch_blocks, domain_blocks, coefficients
):
    total_blocks = density.shape[0] * lax.axis_size("grid")
    points = basis_values.shape[1]
    core = lax.rem(lax.axis_index("grid"), 2)
    window = 6 * NB
    row_out = vmem((1, points))
    coef_out = vmem((window, 4 * NB))
    coef_half = vmem((window, 4 * NB), bf16)
    turned_half = vmem((4 * NB, window), bf16)
    unit = 2 * 3 * points * SB * SB

    blocks = coefficients.reshape(8, NB, NB)
    own = density.reshape(6, HALF, NB)
    edge = to_edge(own)
    own_far = to_orb(own)
    other = to_core(own)
    *basis, done = sort_basis(total_blocks, batch_blocks, basis_values, unit)
    th, tl, nh, nl = basis
    near, early, rest = cut(own, blocks.reshape(16, HALF, NB), other)
    early = to_orb(early)
    (own_far,) = call(hold_kernel, (own_far, done), (vmem((6, HALF, NB)),), "hold")
    other_far = to_core(own_far)
    (edge_message,) = call(
        far_kernel,
        (domain_blocks, edge, done),
        (vmem((5 * HALF + TILE, NB)),),
        "far_message",
        smem=(0,),
    )
    edge_far = to_orb(edge_message)
    (rho,) = call(
        rho_first,
        (th, tl, near, own_far, edge, other, other_far, early),
        (row_out,),
        "rho_first",
        flops=5 * unit,
    )
    edge_far, rest, rho = lax.optimization_barrier((edge_far, rest, rho))
    partner = to_orb(rest)
    other_lists = edge_far[5 * HALF, :8].reshape(2, 4).astype(jnp.int32)

    packed = None
    for iteration in range(ITERS):
        if iteration == 0:
            kernel, operands = fock_other_first, (edge_far,)
        else:
            side_a, side_b, arriving = packed
            (rho,) = call(rho_side, (th, tl, side_a, side_b), (row_out,), "rho_side", flops=3 * unit)
            kernel, operands = fock_other_later, (side_b, arriving)
        scale, give, keep = call(
            kernel,
            (quad_weights, ext_potential, *basis, rho, *operands),
            (row_out, GIVE_OUT, KEEP_OUT),
            "fock_other",
            scratch=(CROSS,),
            plain=(0, 1),
            flops=3 * unit,
        )
        arrived = to_core(give)
        side_a, side_b = call(
            fock_side, (*basis, scale), (A_OUT, B_OUT), "fock_side", flops=3 * unit
        )
        ready = {}

        def before_last(value):
            if iteration == 0:
                value, ready["partner"] = lax.optimization_barrier((value, partner))
                return value
            turned = call(turn_kernel, (coef,), (turned_half, turned_half), "turn", flops=unit)
            value, *ready["turned"] = lax.optimization_barrier((value, *turned))
            return value

        def before_sum(value):
            if iteration > 0:
                return value
            spread = call(
                functools.partial(spread_kernel, total_blocks),
                (domain_blocks, other_lists, blocks, hbm(early), hbm(ready["partner"])),
                (coef_out, coef_half, coef_half, turned_half, turned_half),
                "spread",
                smem=(0, 1),
                plain=(2, 3, 4),
                flops=3 * unit,
            )
            value, *ready["spread"] = lax.optimization_barrier((value, *spread))
            return value

        side_a, side_b, arriving = total_over_all(
            (side_a, side_b, keep, arrived), before_last, before_sum
        )
        if iteration == 0:
            coef, *halves = ready["spread"]
        else:
            halves = (ch, cl, *ready["turned"])
        gradient, mixed = call(
            domain_side,
            (side_a, side_b, *halves),
            (vmem((4 * NB, 4 * NB)), vmem((4, NB, NB))),
            "domain_side",
            flops=unit,
        )
        operands = (
            domain_blocks, other_lists, coef, *halves, gradient, mixed, side_b, arriving
        )
        scratch = (coef_out, CROSS)
        if iteration < ITERS - 1:
            coef, ch, cl, give, keep = call(
                functools.partial(domain_other, total_blocks),
                operands,
                (coef_out, coef_half, coef_half, GIVE_OUT, KEEP_OUT),
                "domain_other",
                scratch=scratch,
                smem=(0, 1),
                flops=2 * unit,
            )
            arrived = to_core(give)
            side_a, side_b = call(density_side, (ch, cl), (A_OUT, B_OUT), "density_side", flops=unit)
            packed = total_over_grid((side_a, side_b, keep, arrived))
    message = vmem((5, HALF, NB))
    coef, ch, cl, edge, give = call(
        functools.partial(domain_edge, total_blocks),
        operands,
        (coef_out, coef_half, coef_half, message, message),
        "domain_edge",
        scratch=scratch,
        smem=(0, 1),
        flops=2 * unit,
    )
    from_edge = to_edge(edge)
    from_core = to_core(give)
    result, own = call(
        functools.partial(domain_last, total_blocks),
        (domain_blocks, coef, ch, cl),
        (jax.ShapeDtypeStruct(coefficients.shape, f32), vmem((6, HALF, NB))),
        "domain_last",
        smem=(0,),
        flops=unit,
    )
    (rows,) = call(
        owner_kernel,
        (own, from_core, from_edge),
        (jax.ShapeDtypeStruct((6, HALF, NB), f32),),
        "owner_rows",
    )
    return (rows.reshape(density.shape), result)


def solution(mesh):
    in_specs = (
        P("grid", None, "orb", None),
        P(("grid", "orb"), None, None),
        P(("grid", "orb"), None),
        P(("grid", "orb"), None),
        P(("grid", "orb"), None),
        P(("grid", "orb"), None),
        P(("grid", "orb"), None, None, None),
    )
    out_specs = (P("grid", None, "orb", None), P(("grid", "orb"), None, None, None))
    return jax.shard_map(shards, mesh=mesh, in_specs=in_specs, out_specs=out_specs, check_vma=False)
```

```python
import functools
import jax
import jax.numpy as jnp
from jax import lax
from jax.experimental import pallas as pl
from jax.experimental.pallas import tpu as pltpu
from jax.sharding import PartitionSpec as P

ITERS = 2
step_scale = 0.5

NB = 128
SB = 2 * NB
TILE = 8
HALF = NB // 2
PACKED = NB + TILE
VMEM_BYTES = 16 * 1024 * 1024
POINT_CHUNK = 256
f32 = jnp.float32
bf16 = jnp.bfloat16

LOW = slice(0, PACKED)
HIGH = slice(PACKED + HALF, 2 * PACKED + HALF)
A_ROWS = 2 * PACKED + HALF
B_ROWS = 2 * NB + HALF
PAIR = PACKED + NB
GIVE_ROWS = PAIR + HALF
EARLY = 9
STRIP = HALF + TILE
KEEP_AT = 2 * NB + HALF


def split(value):
    high = value.astype(bf16)
    return high, (value - high.astype(f32)).astype(bf16)


def dot3(left, right, contract=((1,), (0,))):
    def one(a, b):
        return lax.dot_general(a, b, (contract, ((), ())), preferred_element_type=f32)

    cross_left = jnp.concatenate([left[0], left[1]], axis=contract[0][0])
    cross_right = jnp.concatenate([right[1], right[0]], axis=contract[1][0])
    return one(left[0], right[0]) + one(cross_left, cross_right)


def both(pair, *index):
    return pair[0][index], pair[1][index]


def row_col():
    rows = lax.broadcasted_iota(jnp.int32, (NB, NB), 0)
    return rows, lax.broadcasted_iota(jnp.int32, (NB, NB), 1)


def aligned(value, unit):
    return pl.multiple_of(value * unit, unit)


def core_of():
    return lax.rem(lax.axis_index("grid"), 2)


def relative(block, total_blocks):
    anchor = (lax.axis_index("grid") - 1) * 2
    return lax.rem(block - anchor + total_blocks, total_blocks)


def vmem(shape, kind=f32):
    return pltpu.VMEM(shape, kind)


def call(kernel, operands, outs, name, scratch=(), smem=(), plain=(), flops=0):
    specs, pinned = [], []
    for i, operand in enumerate(operands):
        specs.append(pl.BlockSpec(memory_space=pltpu.SMEM if i in smem else pltpu.VMEM))
        if i in smem or i in plain:
            pinned.append(hbm(operand) if i in smem else operand)
        else:
            pinned.append(pltpu.with_memory_space_constraint(operand, pltpu.VMEM))
    return pl.pallas_call(
        kernel,
        out_shape=list(outs),
        in_specs=specs,
        out_specs=[pl.BlockSpec(memory_space=pltpu.VMEM) for _ in outs],
        scratch_shapes=list(scratch),
        compiler_params=pltpu.CompilerParams(vmem_limit_bytes=VMEM_BYTES),
        cost_estimate=pl.CostEstimate(flops=flops, bytes_accessed=0, transcendentals=0),
        name=name,
    )(*pinned)


def sort_kernel(total_blocks, blocks, basis, th, tl, nh, nl, done, columns, arrived):
    def copy(j):
        source = basis.at[0, :, pl.ds(j * NB, NB)]
        return pltpu.make_async_copy(source, columns.at[j], arrived.at[j])

    for j in range(6):
        copy(j).start()
    for j in range(6):
        at = pl.ds(aligned(relative(blocks[0, j], total_blocks), NB), NB)
        copy(j).wait()
        column = columns[j]
        nh[:, at], nl[:, at] = split(column)
        th[at, :], tl[at, :] = split(column.T)
    done[...] = jnp.zeros_like(done)


def cut_kernel(lists, own, halves, other, near, early, rest, row, sems):
    copies = [
        pltpu.make_async_copy(own, near, sems.at[0]),
        pltpu.make_async_copy(halves.at[pl.ds(0, EARLY)], early, sems.at[1]),
        pltpu.make_async_copy(halves.at[pl.ds(EARLY, 16 - EARLY)], rest, sems.at[2]),
    ]
    for copy in copies:
        copy.start()
    lanes = lax.broadcasted_iota(jnp.int32, (TILE, NB), 1)
    values = jnp.zeros((TILE, NB), f32)
    for d in range(2):
        for i in range(4):
            values = jnp.where(lanes == 4 * d + i, lists[d, i].astype(f32), values)
    row[...] = values
    for copy in copies:
        copy.wait()


def hbm(value):
    return pltpu.with_memory_space_constraint(value, pltpu.HBM)


def cut(lists, own, halves, other):
    return pl.pallas_call(
        cut_kernel,
        out_shape=[vmem(own.shape), vmem((EARLY, HALF, NB)), vmem((16 - EARLY, HALF, NB))]
        + [vmem((TILE, NB))],
        in_specs=[pl.BlockSpec(memory_space=pltpu.SMEM)]
        + [pl.BlockSpec(memory_space=pl.ANY)] * 2
        + [pl.BlockSpec(memory_space=pltpu.VMEM)],
        out_specs=[pl.BlockSpec(memory_space=pltpu.VMEM)] * 4,
        scratch_shapes=[pltpu.SemaphoreType.DMA((3,))],
        compiler_params=pltpu.CompilerParams(vmem_limit_bytes=VMEM_BYTES),
        name="cut",
    )(hbm(lists), hbm(own), hbm(halves), other)


def hold_kernel(value, done, out):
    out[...] = value[...]


def sort_basis(total_blocks, batch_blocks, basis_values, unit):
    points, window = basis_values.shape[1:]
    halves = [vmem((window, points), bf16)] * 2 + [vmem((points, window), bf16)] * 2
    return pl.pallas_call(
        functools.partial(sort_kernel, total_blocks),
        out_shape=halves + [vmem((TILE, NB))],
        in_specs=[pl.BlockSpec(memory_space=pltpu.SMEM), pl.BlockSpec(memory_space=pl.ANY)],
        out_specs=[pl.BlockSpec(memory_space=pltpu.VMEM)] * 5,
        scratch_shapes=[vmem((6, points, NB)), pltpu.SemaphoreType.DMA((6,))],
        compiler_params=pltpu.CompilerParams(vmem_limit_bytes=VMEM_BYTES),
        cost_estimate=pl.CostEstimate(flops=6 * unit, bytes_accessed=0, transcendentals=0),
        name="sort_basis",
    )(hbm(batch_blocks), hbm(basis_values))


def put_pair(pair, packed, off):
    rows, cols = row_col()
    first, last = pair[:NB, :NB], pair[NB:, NB:]
    diagonal = jnp.sum(jnp.where(rows == cols, last, 0.0), axis=0, keepdims=True)
    packed[:NB, :] = jnp.where(rows <= cols, first, last)
    packed[NB:PACKED, :] = jnp.broadcast_to(diagonal, (TILE, NB))
    off[...] = pair[:NB, NB:]


def put_side(low, cross, high, side_a, side_b):
    put_pair(low, side_a.at[LOW], side_b.at[:NB])
    put_pair(high, side_a.at[HIGH], side_b.at[KEEP_AT - NB : KEEP_AT])
    side_a[PACKED : PACKED + HALF, :] = cross[:HALF]
    side_b[NB : NB + HALF, :] = cross[HALF:]


def put_other(pair, cross_ref, give, keep):
    core = core_of()
    put_pair(pair, give.at[:PACKED], give.at[PACKED:PAIR])
    give[PAIR:, :] = cross_ref[pl.ds(aligned(1 - core, HALF), HALF), :]
    keep[...] = cross_ref[pl.ds(aligned(core, HALF), HALF), :]


def side_parts(side_a, side_b):
    low = (side_a[:NB, :], side_a[NB : NB + 1, :], side_b[:NB, :])
    start = PACKED + HALF
    high = (
        side_a[start : start + NB, :],
        side_a[start + NB : start + NB + 1, :],
        side_b[NB + HALF : KEEP_AT, :],
    )
    cross = jnp.concatenate([side_a[PACKED:start, :], side_b[NB : NB + HALF, :]], axis=0)
    return low, cross, high


def other_parts(side_b, other, cross_ref):
    core = core_of()
    cross_ref[pl.ds(aligned(core, HALF), HALF), :] = side_b[KEEP_AT:, :]
    cross_ref[pl.ds(aligned(1 - core, HALF), HALF), :] = other[PAIR:, :]
    return (other[:NB, :], other[NB : NB + 1, :], other[PACKED:PAIR, :]), cross_ref[...]


def unpack(part):
    merged, diagonal, off = part
    rows, cols = row_col()
    turned = merged.T
    first = jnp.where(rows <= cols, merged, turned)
    last = jnp.where(rows > cols, merged, jnp.where(rows < cols, turned, diagonal))
    return join(first, off, off.T, last)


def join(a, b, c, d):
    return jnp.concatenate(
        [jnp.concatenate([a, b], axis=1), jnp.concatenate([c, d], axis=1)], axis=0
    )


def upper_form(part):
    merged, diagonal, off = part
    rows, cols = row_col()
    twice = merged * 2.0
    first = jnp.where(rows < cols, twice, jnp.where(rows == cols, merged, 0.0))
    last = jnp.where(rows > cols, twice, jnp.where(rows == cols, diagonal, 0.0))
    return join(first, off * 2.0, jnp.zeros((NB, NB), f32), last)


def near_kernel(side_a, side_b, keep, arrived, out_a, out_b, out_keep):
    core = core_of()
    out_a[...] = side_a[...]
    out_b[...] = side_b[...]
    out_keep[...] = keep[...] + arrived[PAIR:, :]
    rows_a = pl.ds(pl.multiple_of((1 - core) * (PACKED + HALF), TILE), PACKED)
    rows_b = pl.ds(pl.multiple_of((1 - core) * (NB + HALF), TILE), NB)
    out_a[rows_a, :] = side_a[rows_a, :] + arrived[:PACKED, :]
    out_b[rows_b, :] = side_b[rows_b, :] + arrived[PACKED:PAIR, :]


def near_keep_kernel(side_a, side_b, keep, arrived, out_a, out_b):
    near_kernel(side_a, side_b, keep, arrived, out_a.at[:A_ROWS], out_b, out_a.at[A_ROWS:])


def add_kernel(left, right, out):
    out[...] = left[...] + right[...]


def add_keep_kernel(side_a, arrived, out, keep):
    out[...] = side_a[:A_ROWS, :] + arrived[:A_ROWS, :]
    keep[...] = side_a[A_ROWS:, :] + arrived[A_ROWS:, :]


def side_near(out_a, out_b, near):
    core = core_of()
    rows_a = pl.ds(pl.multiple_of((1 - core) * (PACKED + HALF), TILE), PACKED)
    rows_b = pl.ds(pl.multiple_of((1 - core) * (NB + HALF), TILE), NB)
    near[:PACKED, :] = out_a[rows_a, :]
    near[PACKED:PAIR, :] = out_b[rows_b, :]
    near[PAIR:, :] = out_b[KEEP_AT:, :]


def total_kernel(side_a, arrived_a, side_b, arrived_b, keep, out_a, out_b, near):
    out_a[...] = side_a[...] + arrived_a[...]
    out_b[:KEEP_AT, :] = side_b[...] + arrived_b[...]
    out_b[KEEP_AT:, :] = keep[...]
    side_near(out_a, out_b, near)


def near_sum_kernel(near, keep, arrived, out, out_keep):
    out[:PAIR, :] = near[...] + arrived[:PAIR, :]
    out[PAIR:, :] = jnp.zeros((STRIP, NB), f32)
    out_keep[...] = keep[...] + arrived[PAIR:, :]


def near_total_kernel(near, keep, mine, arrived, out, cross):
    out[:PAIR, :] = near[:PAIR, :] + arrived[:PAIR, :]
    cross[...] = mine[PAIR:, :] + arrived[PAIR:, :]
    out[PAIR:, :] = keep[...]


def add_density(terms, th, tl, before, after):
    points = th.shape[1]
    for start in range(0, points, POINT_CHUNK):
        cols = slice(start, start + POINT_CHUNK)
        rho = before(cols)
        for matrix, at, count, values in terms:
            rows = pl.ds(pl.multiple_of(at, HALF), count)
            value = []
            for value_at, value_count in values:
                value_rows = pl.ds(pl.multiple_of(value_at, HALF), value_count)
                value.append(th[value_rows, cols].astype(f32) + tl[value_rows, cols].astype(f32))
            value = value[0] if len(value) == 1 else jnp.concatenate(value, axis=0)
            product = dot3(matrix, (th[rows, cols], tl[rows, cols]))
            rho = rho + jnp.sum(product * value, axis=0, keepdims=True)
        after(cols, rho)


def half_terms(source, first, pair, half, ends):
    body = join(*[source[2 * i + j + 1 - first] for i in range(2) for j in range(2)])
    at = pair * SB
    rows = [(at + half * HALF, HALF), (at + NB + half * HALF, HALF)]
    terms = [(split(body), at, SB, rows)]
    for index, row, col in ends:
        terms.append((split(source[index]), col * NB, NB, [(row * NB + half * HALF, HALF)]))
    return terms


def rho_first(th, tl, own, own_far, edge, other, other_far, early, rho):
    core = core_of()
    orb = lax.axis_index("orb")
    own_ends = ((0, 2, 1), (5, 3, 4))
    other_ends = ((5 * core, 4 - 3 * core, 3 - core),)
    edge_ends = ((5 - 5 * core, 1 + 3 * core, 2 + core),)
    terms = (
        half_terms(own, 0, 1, orb, own_ends)
        + half_terms(own_far, 0, 1, 1 - orb, own_ends)
        + half_terms(other, 0, 2 - 2 * core, orb, other_ends)
        + half_terms(other_far, 0, 2 - 2 * core, 1 - orb, other_ends)
        + half_terms(edge, 0, 2 * core, orb, edge_ends)
    )

    def store(cols, value):
        rho[:, cols] = value

    add_density(terms, th, tl, lambda cols: jnp.zeros((1, POINT_CHUNK), f32), store)


def far_kernel(row, edge, sorted_first, out):
    first = 1 - core_of()
    for i in range(5):
        out[i * HALF : (i + 1) * HALF, :] = edge[i + first]
    out[5 * HALF :, :] = row[...]


def packed_part(ref):
    return ref[:NB, :], ref[NB : NB + 1, :], ref[PACKED:PAIR, :]


def rho_near(th, tl, near, cross, rho):
    def store(cols, value):
        rho[:, cols] = value

    side = core_of() * SB
    terms = [
        (split(upper_form(packed_part(near))), SB, SB, [(SB, SB)]),
        (split(cross[...] * 2.0), side + SB, NB, [(side + NB, NB)]),
    ]
    add_density(terms, th, tl, lambda cols: jnp.zeros((1, POINT_CHUNK), f32), store)


def rho_other(th, tl, before, near, other, rho, mid):
    core = core_of()
    mid[pl.ds(aligned(core, HALF), HALF), :] = near[PAIR:, :]
    mid[pl.ds(aligned(1 - core, HALF), HALF), :] = other[PAIR:, :]
    at = (2 - 2 * core) * SB
    row = (3 - 2 * core) * NB
    terms = [
        (split(upper_form(packed_part(other))), at, SB, [(at, SB)]),
        (split(mid[...] * 2.0), row + NB, NB, [(row, NB)]),
    ]

    def store(cols, value):
        rho[:, cols] = value

    add_density(terms, th, tl, lambda cols: before[:, cols], store)


def scaled_rows(th, tl, at, count, scale):
    rows = pl.ds(pl.multiple_of(at, NB), count)
    return split((th[rows, :].astype(f32) + tl[rows, :].astype(f32)) * scale[...])


def fock_block(left, nh, nl, at, count):
    cols = pl.ds(pl.multiple_of(at, NB), count)
    return dot3(left, (nh[:, cols], nl[:, cols]))


def fock_other(terms, weights, external, th, tl, nh, nl, rho, scale, give, keep, cross_ref):
    core = core_of()

    def store(cols, value):
        scale[:, cols] = value

    add_density(terms, th, tl, lambda cols: rho[:, cols], store)
    value = scale[...]
    potential = external[...] - jnp.exp(jnp.log(value * value + 1.0) * (1.0 / 6.0))
    scale[...] = weights[...] * potential
    at = (2 - 2 * core) * SB
    pair = fock_block(scaled_rows(th, tl, at, SB, scale), nh, nl, at, SB)
    row = (3 - 2 * core) * NB
    cross_ref[...] = fock_block(scaled_rows(th, tl, row, NB, scale), nh, nl, row + NB, NB)
    put_other(pair, cross_ref, give, keep)


def fock_other_first(
    weights, external, th, tl, nh, nl, rho, edge_far, scale, give, keep, cross_ref
):
    core = core_of()
    ends = ((4 - 4 * core, 1 + 3 * core, 2 + core),)

    def far(index):
        return edge_far[pl.ds(aligned(index, HALF), HALF), :]

    body = join(*[far(2 * i + j + core) for i in range(2) for j in range(2)])
    half = 1 - lax.axis_index("orb")
    at = 2 * core * SB
    rows = [(at + half * HALF, HALF), (at + NB + half * HALF, HALF)]
    terms = [(split(body), at, SB, rows)]
    for index, row, col in ends:
        terms.append((split(far(index)), col * NB, NB, [(row * NB + half * HALF, HALF)]))
    fock_other(terms, weights, external, th, tl, nh, nl, rho, scale, give, keep, cross_ref)


def fock_other_later(
    weights, external, th, tl, nh, nl, rho, mine, arrived, scale, give, keep, cross_ref
):
    at = core_of() * 2 * SB
    part = [
        a + b for a, b in zip(packed_part(mine), packed_part(arrived))
    ]
    terms = [(split(upper_form(part)), at, SB, [(at, SB)])]
    fock_other(terms, weights, external, th, tl, nh, nl, rho, scale, give, keep, cross_ref)


def fock_side(th, tl, nh, nl, scale, side_a, side_b):
    at = core_of() * SB
    low = fock_block(scaled_rows(th, tl, at, SB, scale), nh, nl, at, SB)
    both_rows = fock_block(scaled_rows(th, tl, at + NB, 3 * NB, scale), nh, nl, at + SB, SB)
    put_side(low, both_rows[:NB, :NB], both_rows[NB:], side_a, side_b)


def coefficient_parts(value, high, low, turned_high, turned_low):
    high[...], low[...] = split(value)
    turned_high[...], turned_low[...] = split(value.T)


def spread_kernel(
    total_blocks, own_lists, other_lists, own, early, partner, coef, ch, cl, th, tl, present
):
    coef[...] = jnp.zeros_like(coef)
    for d in range(4):
        for i in range(4):
            blocks = own_lists if d < 2 else other_lists
            at = aligned(relative(blocks[d % 2, i], total_blocks), NB)
            cols = slice(d * NB, (d + 1) * NB)
            if d < 2:
                coef[pl.ds(at, NB), cols] = own[4 * d + i]
                continue
            for half in range(2):
                index = 2 * (4 * (d - 2) + i) + half
                value = early[index] if index < EARLY else partner[index - EARLY]
                coef[pl.ds(at + half * HALF, HALF), cols] = value
    coefficient_parts(coef[...], ch, cl, th, tl)
    for d in range(4):
        blocks = own_lists if d < 2 else other_lists
        for r in range(6):
            held = relative(blocks[d % 2, 0], total_blocks) == r
            for i in range(1, 4):
                held = held | (relative(blocks[d % 2, i], total_blocks) == r)
            row = 6 * d + r
            present[row : row + 1, :] = jnp.full((1, NB), jnp.where(held, 1.0, 0.0), f32)


def gather_kernel(first, second, coef, ch, cl, th, tl):
    core = core_of()
    for source, at, block, count in (
        (first, 0, 4 * core, 2),
        (first, SB, 2 + core, 1),
        (second, 0, 4 - 4 * core, 2),
        (second, SB, 3 - core, 1),
    ):
        coef[pl.ds(aligned(block, NB), count * NB), :] = source[at : at + count * NB, :]
    coefficient_parts(coef[...], ch, cl, th, tl)


def mixing(th, tl, at, count, gradient):
    cols = pl.ds(pl.multiple_of(at, NB), count)
    return [
        dot3((th[d * NB : (d + 1) * NB, cols], tl[d * NB : (d + 1) * NB, cols]), both(gradient, slice(None), slice(d * NB, (d + 1) * NB)))
        for d in range(4)
    ]


def domain_side(side_a, side_b, ch, cl, th, tl, gradient, mixed):
    low, cross, high = side_parts(side_a, side_b)
    at = core_of() * SB
    zero = jnp.zeros((NB, NB), f32)
    first = jnp.concatenate([unpack(low), jnp.concatenate([zero, cross.T], axis=1)], axis=0)
    last = jnp.concatenate([jnp.concatenate([cross, zero], axis=1), unpack(high)], axis=0)

    def coef(start):
        rows = pl.ds(pl.multiple_of(start, SB), SB)
        return ch[rows, :], cl[rows, :]

    upper = dot3(split(first), coef(at))
    lower = dot3(split(last), coef(at + SB))
    gradient[:NB, :] = upper[:NB]
    gradient[NB : 3 * NB, :] = upper[NB:] + lower[: 2 * NB]
    gradient[3 * NB :, :] = lower[2 * NB :]
    for d, value in enumerate(mixing(th, tl, at, 4 * NB, split(gradient[...]))):
        mixed[d] = value


def domain_mixed(
    ch, cl, th, tl, gradient, mixed, side_b, other, work, total, cross_ref
):
    core = core_of()
    part, cross = other_parts(side_b, other, cross_ref)
    zero = jnp.zeros((NB, NB), f32)
    beside = jnp.where(core == 0, cross, cross.T)
    across = jnp.where(core == 0, cross.T, cross)
    placed = jnp.concatenate(
        [jnp.where(core == 0, beside, zero), jnp.where(core == 0, zero, beside)], axis=1
    )
    slab = jnp.concatenate([unpack(part), placed], axis=0)
    other_at = (2 - 2 * core) * SB
    other_rows = pl.ds(pl.multiple_of(other_at, SB), SB)
    side_block = pl.ds(pl.multiple_of((3 - core) * NB, NB), NB)
    touching = pl.ds(pl.multiple_of((4 - 3 * core) * NB, NB), NB)
    work[pl.ds(pl.multiple_of(core * SB, SB), 4 * NB), :] = gradient[...]
    product = dot3(split(slab), (ch[other_rows, :], cl[other_rows, :]))
    work[other_rows, :] = product[:SB]
    back = dot3(split(across), (ch[side_block, :], cl[side_block, :]))
    work[touching, :] += back
    work[side_block, :] += product[SB:]
    first = mixing(th, tl, other_at, SB, split(work[other_rows, :]))
    second = mixing(th, tl, (3 - core) * NB, NB, split(product[SB:]))
    for d in range(4):
        total[d] = mixed[d] + first[d] + second[d]


def new_blocks(present, coef, ch, cl, work, total, places, fresh, fh, fl):
    zero = jnp.zeros((NB, NB), f32)
    for d in range(0, 4, 2):
        cols = slice(d * NB, (d + 2) * NB)
        square = split(join(total[d], zero, zero, total[d + 1]))
        for block, count, at in places:
            rows = pl.ds(aligned(block, NB), count * NB)
            moved = dot3((ch[rows, cols], cl[rows, cols]), square)
            for r in range(count):
                rows = pl.ds(aligned(block + r, NB), NB)
                out_rows = slice(at + r * NB, at + (r + 1) * NB)
                for e in range(2):
                    out_cols = slice((d + e) * NB, (d + e + 1) * NB)
                    kept = work[rows, out_cols] * present[pl.ds(6 * (d + e) + block + r, 1), :]
                    piece = moved[r * NB : (r + 1) * NB, e * NB : (e + 1) * NB]
                    value = coef[rows, out_cols] - step_scale * (kept - piece)
                    fresh[out_rows, out_cols] = value
                    fh[out_rows, out_cols], fl[out_rows, out_cols] = split(value)


def outer(left, at, count, right, from_at, from_count):
    left_rows, right_rows = pl.ds(at, count), pl.ds(from_at, from_count)
    return dot3(
        (left[0][left_rows, :], left[1][left_rows, :]),
        (right[0][right_rows, :], right[1][right_rows, :]),
        ((1,), (1,)),
    )


def domain_far_rows(
    present, coef, ch, cl, th, tl, gradient, mixed, side_b, other,
    fresh, fh, fl, work, total, cross_ref,
):
    domain_mixed(ch, cl, th, tl, gradient, mixed, side_b, other, work, total, cross_ref)
    core = core_of()
    places = ((4 * core, 2, 0), (2 + core, 1, SB))
    new_blocks(present, coef, ch, cl, work, total, places, fresh, fh, fl)


def domain_far(
    present, coef, ch, cl, th, tl, gradient, mixed, side_b, other,
    fresh, fh, fl, work, total, message, cross_ref,
):
    domain_far_rows(
        present, coef, ch, cl, th, tl, gradient, mixed, side_b, other,
        fresh, fh, fl, work, total, cross_ref,
    )
    core = core_of()
    far = (fh, fl)
    put_pair(outer(far, 0, SB, far, 0, SB), message.at[:PACKED], message.at[PACKED:PAIR])
    cross = outer(far, SB, NB, far, aligned(1 - core, NB), NB)
    message[PAIR:, :] = jnp.where(core == 0, cross.T, cross)


def other_blocks(present, coef, ch, cl, work, total, fresh, fh, fl):
    core = core_of()
    places = ((4 - 4 * core, 2, 0), (3 - core, 1, SB))
    new_blocks(present, coef, ch, cl, work, total, places, fresh, fh, fl)


def domain_other(
    present, coef, ch, cl, work, total, fresh, fh, fl, give, keep, cross_ref
):
    other_blocks(present, coef, ch, cl, work, total, fresh, fh, fl)
    core = core_of()
    rest = (fh, fl)
    cross = outer(rest, SB, NB, rest, aligned(core, NB), NB)
    cross_ref[...] = jnp.where(core == 0, cross, cross.T)
    put_other(outer(rest, 0, SB, rest, 0, SB), cross_ref, give, keep)


def near_rows(f1, f2):
    core = core_of()
    touching, beside = f1[SB:, :], f2[SB:, :]
    return jnp.concatenate(
        [jnp.where(core == 0, touching, beside), jnp.where(core == 0, beside, touching)], axis=0
    )


def density_near(f1h, f1l, f2h, f2l, near):
    rows = (near_rows(f1h, f2h), near_rows(f1l, f2l))
    put_pair(dot3(rows, rows, ((1,), (1,))), near.at[:PACKED], near.at[PACKED:])


def half_rows(ref):
    def store(index, value):
        ref[pl.ds(aligned(index, HALF), HALF), :] = value

    return store


def half_blocks(ref):
    def store(index, value):
        ref[index] = value

    return store


def owner_half(left, store, first):
    half = lax.axis_index("orb")
    for i in range(2):
        rows = outer(left, pl.multiple_of(i * NB + half * HALF, HALF), HALF, left, 0, SB)
        store(2 * i + 1 - first, rows[:, :NB])
        store(2 * i + 2 - first, rows[:, NB:])


def domain_edge(
    present, coef, ch, cl, th, tl, gradient, mixed, side_b, other,
    fresh, fh, fl, work, total, edge, cross_ref,
):
    domain_far_rows(
        present, coef, ch, cl, th, tl, gradient, mixed, side_b, other,
        fresh, fh, fl, work, total, cross_ref,
    )
    core = core_of()
    far = (fh, fl)
    owner_half(far, half_rows(edge), 1 - core)
    edge[5 * HALF :, :] = jnp.zeros((2 * TILE, NB), f32)
    at = pl.multiple_of((1 - core) * NB + lax.axis_index("orb") * HALF, HALF)
    half_rows(edge)(4 - 4 * core, outer(far, at, HALF, far, SB, NB))


def domain_give(present, coef, ch, cl, work, total, fresh, fh, fl, give):
    other_blocks(present, coef, ch, cl, work, total, fresh, fh, fl)
    core = core_of()
    rest = (fh, fl)
    owner_half(rest, half_blocks(give), core)
    at = pl.multiple_of(core * NB + lax.axis_index("orb") * HALF, HALF)
    give[4 * core] = outer(rest, at, HALF, rest, SB, NB)


def domain_last(total_blocks, own_lists, fresh1, f1h, f1l, fresh2, f2h, f2l, result, own, window, nh, nl):
    core = core_of()
    half = lax.axis_index("orb")
    nh[...] = near_rows(f1h, f2h)
    nl[...] = near_rows(f1l, f2l)
    near = (nh, nl)
    owner_half(near, half_blocks(own), 0)
    rows = pl.multiple_of(half * HALF, HALF)

    def far_or_rest(row_at, first_at, second_at):
        left = (nh[pl.ds(row_at, HALF), :], nl[pl.ds(row_at, HALF), :])
        first = pl.ds(first_at, NB)
        second = pl.ds(second_at, NB)
        right = [
            jnp.where(core == 0, a[first, :], b[second, :]) for a, b in ((f1h, f2h), (f1l, f2l))
        ]
        return dot3(left, right, ((1,), (1,)))

    def rest_or_far(row_at, first_at, second_at):
        left = (nh[pl.ds(row_at, HALF), :], nl[pl.ds(row_at, HALF), :])
        first = pl.ds(first_at, NB)
        second = pl.ds(second_at, NB)
        right = [
            jnp.where(core == 0, b[first, :], a[second, :]) for a, b in ((f1h, f2h), (f1l, f2l))
        ]
        return dot3(left, right, ((1,), (1,)))

    own[0] = far_or_rest(rows, NB, NB)
    own[5] = rest_or_far(pl.multiple_of(NB + half * HALF, HALF), 0, 0)
    for source, at, block, count in (
        (fresh1, 0, 4 * core, 2),
        (fresh1, SB, 2 + core, 1),
        (fresh2, 0, 4 - 4 * core, 2),
        (fresh2, SB, 3 - core, 1),
    ):
        window[pl.ds(aligned(block, NB), count * NB), :] = source[at : at + count * NB, :SB]
    for d in range(2):
        for i in range(4):
            at = aligned(relative(own_lists[d, i], total_blocks), NB)
            result[d, i] = window[pl.ds(at, NB), d * NB : (d + 1) * NB]


def owner_kernel(own, from_core, from_edge, out):
    core = core_of()
    edge = [from_edge[i * HALF : (i + 1) * HALF, :] for i in range(5)]
    lower = [jnp.where(core == 0, from_core[i], edge[i]) for i in range(5)]
    upper = [jnp.where(core == 0, edge[i], from_core[i]) for i in range(5)]
    out[0] = own[0] + upper[0]
    for i in range(1, 5):
        out[i] = own[i] + upper[i] + lower[i - 1]
    out[5] = own[5] + lower[4]


def to_core(value):
    count = lax.axis_size("grid")
    return lax.ppermute(value, "grid", [(i, i ^ 1) for i in range(count)])


def to_edge(value):
    count = lax.axis_size("grid")
    route = [(i, (i + 1) % count if i % 2 else (i - 1) % count) for i in range(count)]
    return lax.ppermute(value, "grid", route)


def to_orb(value):
    return lax.ppermute(value, "orb", [(0, 1), (1, 0)])


A_OUT = vmem((A_ROWS, NB))
B_OUT = vmem((B_ROWS, NB))
BK_OUT = vmem((B_ROWS + HALF, NB))
GIVE_OUT = vmem((GIVE_ROWS, NB))
KEEP_OUT = vmem((HALF, NB))
CROSS = vmem((NB, NB))


def total_over_all(made, before_last, before_sum):
    side_a, side_b, keep, arrived = made
    side_a, side_b = call(
        near_keep_kernel,
        (side_a, side_b, keep, arrived),
        (vmem((A_ROWS + HALF, NB)), B_OUT),
        "add_near",
    )
    first_b = to_edge(side_b)
    first_a = to_orb(side_a)
    side_a, keep = call(add_keep_kernel, (side_a, first_a), (A_OUT, KEEP_OUT), "add_a")
    last_a = to_edge(side_a)
    (side_b,) = call(add_kernel, (side_b, first_b), (B_OUT,), "add_b")
    side_b = before_last(side_b)
    last_b = before_sum(to_orb(side_b))
    side_a, side_b, near = call(
        total_kernel,
        (side_a, last_a, side_b, last_b, keep),
        (A_OUT, BK_OUT, GIVE_OUT),
        "add_all",
    )
    return side_a, side_b, to_core(near)


def shards(
    density, basis_values, quad_weights, ext_potential, batch_blocks, domain_blocks, coefficients
):
    total_blocks = density.shape[0] * lax.axis_size("grid")
    points = basis_values.shape[1]
    core = lax.rem(lax.axis_index("grid"), 2)
    window = 6 * NB
    row_out = vmem((1, points))
    coef_out = vmem((window, 4 * NB))
    coef_half = vmem((window, 4 * NB), bf16)
    turned_half = vmem((4 * NB, window), bf16)
    unit = 2 * 3 * points * SB * SB

    blocks = coefficients.reshape(8, NB, NB)
    own = density.reshape(6, HALF, NB)
    edge = to_edge(own)
    own_far = to_orb(own)
    other = to_core(own)
    *basis, done = sort_basis(total_blocks, batch_blocks, basis_values, unit)
    th, tl, nh, nl = basis
    near, early, rest, list_row = cut(domain_blocks, own, blocks.reshape(16, HALF, NB), other)
    early = to_orb(early)
    (own_far,) = call(hold_kernel, (own_far, done), (vmem((6, HALF, NB)),), "hold")
    other_far = to_core(own_far)
    (edge_message,) = call(
        far_kernel,
        (list_row, edge, done),
        (vmem((5 * HALF + TILE, NB)),),
        "far_message",
    )
    edge_far = to_orb(edge_message)
    (rho,) = call(
        rho_first,
        (th, tl, near, own_far, edge, other, other_far, early),
        (row_out,),
        "rho_first",
        flops=5 * unit,
    )
    edge_far, rest, rho = lax.optimization_barrier((edge_far, rest, rho))
    partner = to_orb(rest)
    other_lists = edge_far[5 * HALF, :8].reshape(2, 4).astype(jnp.int32)

    packed = None
    for iteration in range(ITERS):
        if iteration == 0:
            kernel, operands = fock_other_first, (edge_far,)
        else:
            kernel, operands = fock_other_later, packed
        scale, give, keep = call(
            kernel,
            (quad_weights, ext_potential, *basis, rho, *operands),
            (row_out, GIVE_OUT, KEEP_OUT),
            "fock_other",
            scratch=(CROSS,),
            plain=(0, 1),
            flops=3 * unit,
        )
        arrived = to_core(give)
        side_a, side_b = call(
            fock_side, (*basis, scale), (A_OUT, B_OUT), "fock_side", flops=3 * unit
        )
        ready = {}

        def before_last(value):
            if iteration == 0:
                value, ready["partner"] = lax.optimization_barrier((value, partner))
                return value
            gathered = call(
                gather_kernel,
                (fresh1, fresh2),
                (coef_out, coef_half, coef_half, turned_half, turned_half),
                "gather",
                flops=unit,
            )
            value, *ready["gathered"] = lax.optimization_barrier((value, *gathered))
            return value

        def before_sum(value):
            if iteration > 0:
                return value
            spread = call(
                functools.partial(spread_kernel, total_blocks),
                (domain_blocks, other_lists, blocks, hbm(early), hbm(ready["partner"])),
                (coef_out, coef_half, coef_half, turned_half, turned_half, vmem((24, NB))),
                "spread",
                smem=(0, 1),
                plain=(2, 3, 4),
                flops=3 * unit,
            )
            value, *ready["spread"] = lax.optimization_barrier((value, *spread))
            return value

        side_a, side_b, arriving = total_over_all(
            (side_a, side_b, keep, arrived), before_last, before_sum
        )
        if iteration == 0:
            coef, *halves, present = ready["spread"]
        else:
            coef, *halves = ready["gathered"]
        gradient, mixed = call(
            domain_side,
            (side_a, side_b, *halves),
            (vmem((4 * NB, 4 * NB)), vmem((4, NB, NB))),
            "domain_side",
            flops=unit,
        )
        operands = (
            present, coef, *halves, gradient, mixed, side_b, arriving
        )
        new_outs = (vmem((3 * NB, 4 * NB)),) + (vmem((3 * NB, 4 * NB), bf16),) * 2
        far_outs = new_outs + (coef_out, vmem((4, NB, NB)))
        if iteration < ITERS - 1:
            fresh1, f1h, f1l, work, total, mine = call(
                domain_far,
                operands,
                far_outs + (vmem((PAIR + NB, NB)),),
                "domain_far",
                scratch=(CROSS,),
                flops=2 * unit,
            )
            from_far = to_edge(mine)
            fresh2, f2h, f2l, give, keep = call(
                domain_other,
                (present, coef, *halves[:2], work, total),
                new_outs + (GIVE_OUT, KEEP_OUT),
                "domain_other",
                scratch=(CROSS,),
                flops=unit,
            )
            arrived = to_core(give)
            (near,) = call(
                density_near, (f1h, f1l, f2h, f2l), (vmem((PAIR, NB)),), "density_near"
            )
            near, keep = call(
                near_sum_kernel,
                (near, keep, arrived),
                (vmem((PAIR + STRIP, NB)), KEEP_OUT),
                "add_near",
            )
            from_near = to_edge(near)
            near_total, cross = call(
                near_total_kernel, (near, keep, mine, from_far), (GIVE_OUT, CROSS), "add_far"
            )
            arriving = to_core(near_total)
            (rho,) = call(rho_near, (th, tl, near_total, cross), (row_out,), "rho_near", flops=unit)
            (rho,) = call(
                rho_other,
                (th, tl, rho, near_total, arriving),
                (row_out,),
                "rho_other",
                scratch=(CROSS,),
            )
            packed = (mine, from_near)
    message = vmem((5, HALF, NB))
    edge_message = vmem((5 * HALF + 2 * TILE, NB))
    fresh1, f1h, f1l, work, total, edge = call(
        domain_edge, operands, far_outs + (edge_message,), "domain_edge", scratch=(CROSS,), flops=2 * unit
    )
    from_edge = to_edge(edge)
    fresh2, f2h, f2l, give = call(
        domain_give,
        (present, coef, *halves[:2], work, total),
        new_outs + (message,),
        "domain_give",
        flops=unit,
    )
    from_core = to_core(give)
    result, own = call(
        functools.partial(domain_last, total_blocks),
        (domain_blocks, fresh1, f1h, f1l, fresh2, f2h, f2l),
        (jax.ShapeDtypeStruct(coefficients.shape, f32), vmem((6, HALF, NB))),
        "domain_last",
        scratch=(vmem((window, SB)),) + (vmem((SB, 4 * NB), bf16),) * 2,
        smem=(0,),
    )
    (rows,) = call(
        owner_kernel,
        (own, from_core, from_edge),
        (jax.ShapeDtypeStruct((6, HALF, NB), f32),),
        "owner_rows",
    )
    return (rows.reshape(density.shape), result)


def solution(mesh):
    in_specs = (
        P("grid", None, "orb", None),
        P(("grid", "orb"), None, None),
        P(("grid", "orb"), None),
        P(("grid", "orb"), None),
        P(("grid", "orb"), None),
        P(("grid", "orb"), None),
        P(("grid", "orb"), None, None, None),
    )
    out_specs = (P("grid", None, "orb", None), P(("grid", "orb"), None, None, None))
    return jax.shard_map(shards, mesh=mesh, in_specs=in_specs, out_specs=out_specs, check_vma=False)
```

```python
import functools
import jax
import jax.numpy as jnp
from jax import lax
from jax.experimental import pallas as pl
from jax.experimental.pallas import tpu as pltpu
from jax.sharding import PartitionSpec as P

ITERS = 2
step_scale = 0.5

NB = 128
SB = 2 * NB
TILE = 8
HALF = NB // 2
PACKED = NB + TILE
VMEM_BYTES = 16 * 1024 * 1024
POINT_CHUNK = 256
f32 = jnp.float32
bf16 = jnp.bfloat16

LOW = slice(0, PACKED)
HIGH = slice(PACKED + HALF, 2 * PACKED + HALF)
A_ROWS = 2 * PACKED + HALF
B_ROWS = 2 * NB + HALF
PAIR = PACKED + NB
GIVE_ROWS = PAIR + HALF
EARLY = 8
STRIP = HALF + TILE
KEEP_AT = 2 * NB + HALF


def split(value):
    high = value.astype(bf16)
    return high, (value - high.astype(f32)).astype(bf16)


def dot3(left, right, contract=((1,), (0,))):
    def one(a, b):
        return lax.dot_general(a, b, (contract, ((), ())), preferred_element_type=f32)

    cross_left = jnp.concatenate([left[0], left[1]], axis=contract[0][0])
    cross_right = jnp.concatenate([right[1], right[0]], axis=contract[1][0])
    return one(left[0], right[0]) + one(cross_left, cross_right)


def both(pair, *index):
    return pair[0][index], pair[1][index]


def row_col():
    rows = lax.broadcasted_iota(jnp.int32, (NB, NB), 0)
    return rows, lax.broadcasted_iota(jnp.int32, (NB, NB), 1)


def aligned(value, unit):
    return pl.multiple_of(value * unit, unit)


def core_of():
    return lax.rem(lax.axis_index("grid"), 2)


def relative(block, total_blocks):
    anchor = (lax.axis_index("grid") - 1) * 2
    return lax.rem(block - anchor + total_blocks, total_blocks)


def vmem(shape, kind=f32):
    return pltpu.VMEM(shape, kind)


def call(kernel, operands, outs, name, scratch=(), smem=(), plain=(), flops=0):
    specs, pinned = [], []
    for i, operand in enumerate(operands):
        specs.append(pl.BlockSpec(memory_space=pltpu.SMEM if i in smem else pltpu.VMEM))
        if i in smem or i in plain:
            pinned.append(hbm(operand) if i in smem else operand)
        else:
            pinned.append(pltpu.with_memory_space_constraint(operand, pltpu.VMEM))
    return pl.pallas_call(
        kernel,
        out_shape=list(outs),
        in_specs=specs,
        out_specs=[pl.BlockSpec(memory_space=pltpu.VMEM) for _ in outs],
        scratch_shapes=list(scratch),
        compiler_params=pltpu.CompilerParams(vmem_limit_bytes=VMEM_BYTES),
        cost_estimate=pl.CostEstimate(flops=flops, bytes_accessed=0, transcendentals=0),
        name=name,
    )(*pinned)


def sort_kernel(total_blocks, blocks, basis, th, tl, nh, nl, done, columns, arrived):
    def copy(j):
        source = basis.at[0, :, pl.ds(j * NB, NB)]
        return pltpu.make_async_copy(source, columns.at[j], arrived.at[j])

    for j in range(6):
        copy(j).start()
    for j in range(6):
        at = pl.ds(aligned(relative(blocks[0, j], total_blocks), NB), NB)
        copy(j).wait()
        column = columns[j]
        nh[:, at], nl[:, at] = split(column)
        th[at, :], tl[at, :] = split(column.T)
    done[...] = jnp.zeros_like(done)


def cut_kernel(lists, own, halves, other, near, early, rest, row, sems):
    copies = [
        pltpu.make_async_copy(own, near, sems.at[0]),
        pltpu.make_async_copy(halves.at[pl.ds(0, EARLY)], early, sems.at[1]),
        pltpu.make_async_copy(halves.at[pl.ds(EARLY, 16 - EARLY)], rest, sems.at[2]),
    ]
    for copy in copies:
        copy.start()
    lanes = lax.broadcasted_iota(jnp.int32, (TILE, NB), 1)
    values = jnp.zeros((TILE, NB), f32)
    for d in range(2):
        for i in range(4):
            values = jnp.where(lanes == 4 * d + i, lists[d, i].astype(f32), values)
    row[...] = values
    for copy in copies:
        copy.wait()


def hbm(value):
    return pltpu.with_memory_space_constraint(value, pltpu.HBM)


def cut(lists, own, halves, other):
    return pl.pallas_call(
        cut_kernel,
        out_shape=[vmem(own.shape), vmem((EARLY, HALF, NB)), vmem((16 - EARLY, HALF, NB))]
        + [vmem((TILE, NB))],
        in_specs=[pl.BlockSpec(memory_space=pltpu.SMEM)]
        + [pl.BlockSpec(memory_space=pl.ANY)] * 2
        + [pl.BlockSpec(memory_space=pltpu.VMEM)],
        out_specs=[pl.BlockSpec(memory_space=pltpu.VMEM)] * 4,
        scratch_shapes=[pltpu.SemaphoreType.DMA((3,))],
        compiler_params=pltpu.CompilerParams(vmem_limit_bytes=VMEM_BYTES),
        name="cut",
    )(hbm(lists), hbm(own), hbm(halves), other)


def hold_kernel(value, done, out):
    out[...] = value[...]


def sort_basis(total_blocks, batch_blocks, basis_values, unit):
    points, window = basis_values.shape[1:]
    halves = [vmem((window, points), bf16)] * 2 + [vmem((points, window), bf16)] * 2
    return pl.pallas_call(
        functools.partial(sort_kernel, total_blocks),
        out_shape=halves + [vmem((TILE, NB))],
        in_specs=[pl.BlockSpec(memory_space=pltpu.SMEM), pl.BlockSpec(memory_space=pl.ANY)],
        out_specs=[pl.BlockSpec(memory_space=pltpu.VMEM)] * 5,
        scratch_shapes=[vmem((6, points, NB)), pltpu.SemaphoreType.DMA((6,))],
        compiler_params=pltpu.CompilerParams(vmem_limit_bytes=VMEM_BYTES),
        cost_estimate=pl.CostEstimate(flops=6 * unit, bytes_accessed=0, transcendentals=0),
        name="sort_basis",
    )(hbm(batch_blocks), hbm(basis_values))


def put_pair(pair, packed, off):
    rows, cols = row_col()
    first, last = pair[:NB, :NB], pair[NB:, NB:]
    diagonal = jnp.sum(jnp.where(rows == cols, last, 0.0), axis=0, keepdims=True)
    packed[:NB, :] = jnp.where(rows <= cols, first, last)
    packed[NB:PACKED, :] = jnp.broadcast_to(diagonal, (TILE, NB))
    off[...] = pair[:NB, NB:]


def put_side(low, cross, high, side_a, side_b):
    put_pair(low, side_a.at[LOW], side_b.at[:NB])
    put_pair(high, side_a.at[HIGH], side_b.at[KEEP_AT - NB : KEEP_AT])
    side_a[PACKED : PACKED + HALF, :] = cross[:HALF]
    side_b[NB : NB + HALF, :] = cross[HALF:]


def put_other(pair, cross_ref, give, keep):
    core = core_of()
    put_pair(pair, give.at[:PACKED], give.at[PACKED:PAIR])
    give[PAIR:, :] = cross_ref[pl.ds(aligned(1 - core, HALF), HALF), :]
    keep[...] = cross_ref[pl.ds(aligned(core, HALF), HALF), :]


def side_parts(side_a, side_b):
    low = (side_a[:NB, :], side_a[NB : NB + 1, :], side_b[:NB, :])
    start = PACKED + HALF
    high = (
        side_a[start : start + NB, :],
        side_a[start + NB : start + NB + 1, :],
        side_b[NB + HALF : KEEP_AT, :],
    )
    cross = jnp.concatenate([side_a[PACKED:start, :], side_b[NB : NB + HALF, :]], axis=0)
    return low, cross, high


def other_parts(side_b, other, cross_ref):
    core = core_of()
    cross_ref[pl.ds(aligned(core, HALF), HALF), :] = side_b[KEEP_AT:, :]
    cross_ref[pl.ds(aligned(1 - core, HALF), HALF), :] = other[PAIR:, :]
    return (other[:NB, :], other[NB : NB + 1, :], other[PACKED:PAIR, :]), cross_ref[...]


def unpack(part):
    merged, diagonal, off = part
    rows, cols = row_col()
    turned = merged.T
    first = jnp.where(rows <= cols, merged, turned)
    last = jnp.where(rows > cols, merged, jnp.where(rows < cols, turned, diagonal))
    return join(first, off, off.T, last)


def join(a, b, c, d):
    return jnp.concatenate(
        [jnp.concatenate([a, b], axis=1), jnp.concatenate([c, d], axis=1)], axis=0
    )


def upper_form(part):
    merged, diagonal, off = part
    rows, cols = row_col()
    twice = merged * 2.0
    first = jnp.where(rows < cols, twice, jnp.where(rows == cols, merged, 0.0))
    last = jnp.where(rows > cols, twice, jnp.where(rows == cols, diagonal, 0.0))
    return join(first, off * 2.0, jnp.zeros((NB, NB), f32), last)


def near_kernel(side_a, side_b, keep, arrived, out_a, out_b, out_keep):
    core = core_of()
    out_a[...] = side_a[...]
    out_b[...] = side_b[...]
    out_keep[...] = keep[...] + arrived[PAIR:, :]
    rows_a = pl.ds(pl.multiple_of((1 - core) * (PACKED + HALF), TILE), PACKED)
    rows_b = pl.ds(pl.multiple_of((1 - core) * (NB + HALF), TILE), NB)
    out_a[rows_a, :] = side_a[rows_a, :] + arrived[:PACKED, :]
    out_b[rows_b, :] = side_b[rows_b, :] + arrived[PACKED:PAIR, :]


def near_keep_kernel(side_a, side_b, keep, arrived, out_a, out_b):
    near_kernel(side_a, side_b, keep, arrived, out_a.at[:A_ROWS], out_b, out_a.at[A_ROWS:])


def add_kernel(left, right, out):
    out[...] = left[...] + right[...]


def add_keep_kernel(side_a, arrived, out, keep):
    out[...] = side_a[:A_ROWS, :] + arrived[:A_ROWS, :]
    keep[...] = side_a[A_ROWS:, :] + arrived[A_ROWS:, :]


def side_near(out_a, out_b, near):
    core = core_of()
    rows_a = pl.ds(pl.multiple_of((1 - core) * (PACKED + HALF), TILE), PACKED)
    rows_b = pl.ds(pl.multiple_of((1 - core) * (NB + HALF), TILE), NB)
    near[:PACKED, :] = out_a[rows_a, :]
    near[PACKED:PAIR, :] = out_b[rows_b, :]
    near[PAIR:, :] = out_b[KEEP_AT:, :]


def total_kernel(side_a, arrived_a, side_b, arrived_b, keep, out_a, out_b, near):
    out_a[...] = side_a[...] + arrived_a[...]
    out_b[:KEEP_AT, :] = side_b[...] + arrived_b[...]
    out_b[KEEP_AT:, :] = keep[...]
    side_near(out_a, out_b, near)


def near_sum_kernel(near, keep, arrived, out, out_keep):
    out[:PAIR, :] = near[...] + arrived[:PAIR, :]
    out[PAIR:, :] = jnp.zeros((STRIP, NB), f32)
    out_keep[...] = keep[...] + arrived[PAIR:, :]


def near_total_kernel(near, keep, mine, arrived, out, cross):
    out[:PAIR, :] = near[:PAIR, :] + arrived[:PAIR, :]
    cross[...] = mine[PAIR:, :] + arrived[PAIR:, :]
    out[PAIR:, :] = keep[...]


def add_density(terms, th, tl, before, after):
    points = th.shape[1]
    for start in range(0, points, POINT_CHUNK):
        cols = slice(start, start + POINT_CHUNK)
        rho = before(cols)
        for matrix, at, count, values in terms:
            rows = pl.ds(pl.multiple_of(at, HALF), count)
            value = []
            for value_at, value_count in values:
                value_rows = pl.ds(pl.multiple_of(value_at, HALF), value_count)
                value.append(th[value_rows, cols].astype(f32) + tl[value_rows, cols].astype(f32))
            value = value[0] if len(value) == 1 else jnp.concatenate(value, axis=0)
            product = dot3(matrix, (th[rows, cols], tl[rows, cols]))
            rho = rho + jnp.sum(product * value, axis=0, keepdims=True)
        after(cols, rho)


def half_terms(source, first, pair, half, ends):
    body = join(*[source[2 * i + j + 1 - first] for i in range(2) for j in range(2)])
    at = pair * SB
    rows = [(at + half * HALF, HALF), (at + NB + half * HALF, HALF)]
    terms = [(split(body), at, SB, rows)]
    for index, row, col in ends:
        terms.append((split(source[index]), col * NB, NB, [(row * NB + half * HALF, HALF)]))
    return terms


def rho_first(th, tl, own, own_far, edge, other, other_far, early, rho):
    core = core_of()
    orb = lax.axis_index("orb")
    own_ends = ((0, 2, 1), (5, 3, 4))
    other_ends = ((5 * core, 4 - 3 * core, 3 - core),)
    edge_ends = ((5 - 5 * core, 1 + 3 * core, 2 + core),)
    terms = (
        half_terms(own, 0, 1, orb, own_ends)
        + half_terms(own_far, 0, 1, 1 - orb, own_ends)
        + half_terms(other, 0, 2 - 2 * core, orb, other_ends)
        + half_terms(other_far, 0, 2 - 2 * core, 1 - orb, other_ends)
        + half_terms(edge, 0, 2 * core, orb, edge_ends)
    )

    def store(cols, value):
        rho[:, cols] = value

    add_density(terms, th, tl, lambda cols: jnp.zeros((1, POINT_CHUNK), f32), store)


def far_kernel(row, edge, sorted_first, out):
    first = 1 - core_of()
    for i in range(5):
        out[i * HALF : (i + 1) * HALF, :] = edge[i + first]
    out[5 * HALF :, :] = row[...]


def packed_part(ref):
    return ref[:NB, :], ref[NB : NB + 1, :], ref[PACKED:PAIR, :]


def rho_near(th, tl, near, cross, rho):
    def store(cols, value):
        rho[:, cols] = value

    side = core_of() * SB
    terms = [
        (split(upper_form(packed_part(near))), SB, SB, [(SB, SB)]),
        (split(cross[...] * 2.0), side + SB, NB, [(side + NB, NB)]),
    ]
    add_density(terms, th, tl, lambda cols: jnp.zeros((1, POINT_CHUNK), f32), store)


def rho_other(th, tl, before, near, other, rho, mid):
    core = core_of()
    mid[pl.ds(aligned(core, HALF), HALF), :] = near[PAIR:, :]
    mid[pl.ds(aligned(1 - core, HALF), HALF), :] = other[PAIR:, :]
    at = (2 - 2 * core) * SB
    row = (3 - 2 * core) * NB
    terms = [
        (split(upper_form(packed_part(other))), at, SB, [(at, SB)]),
        (split(mid[...] * 2.0), row + NB, NB, [(row, NB)]),
    ]

    def store(cols, value):
        rho[:, cols] = value

    add_density(terms, th, tl, lambda cols: before[:, cols], store)


def scaled_rows(th, tl, at, count, scale):
    rows = pl.ds(pl.multiple_of(at, NB), count)
    return split((th[rows, :].astype(f32) + tl[rows, :].astype(f32)) * scale[...])


def fock_block(left, nh, nl, at, count):
    cols = pl.ds(pl.multiple_of(at, NB), count)
    return dot3(left, (nh[:, cols], nl[:, cols]))


def fock_other(terms, weights, external, th, tl, nh, nl, rho, scale, give, keep, cross_ref):
    core = core_of()

    def store(cols, value):
        scale[:, cols] = value

    add_density(terms, th, tl, lambda cols: rho[:, cols], store)
    value = scale[...]
    potential = external[...] - jnp.exp(jnp.log(value * value + 1.0) * (1.0 / 6.0))
    scale[...] = weights[...] * potential
    at = (2 - 2 * core) * SB
    pair = fock_block(scaled_rows(th, tl, at, SB, scale), nh, nl, at, SB)
    row = (3 - 2 * core) * NB
    cross_ref[...] = fock_block(scaled_rows(th, tl, row, NB, scale), nh, nl, row + NB, NB)
    put_other(pair, cross_ref, give, keep)


def fock_other_first(
    weights, external, th, tl, nh, nl, rho, edge_far, scale, give, keep, cross_ref
):
    core = core_of()
    ends = ((4 - 4 * core, 1 + 3 * core, 2 + core),)

    def far(index):
        return edge_far[pl.ds(aligned(index, HALF), HALF), :]

    body = join(*[far(2 * i + j + core) for i in range(2) for j in range(2)])
    half = 1 - lax.axis_index("orb")
    at = 2 * core * SB
    rows = [(at + half * HALF, HALF), (at + NB + half * HALF, HALF)]
    terms = [(split(body), at, SB, rows)]
    for index, row, col in ends:
        terms.append((split(far(index)), col * NB, NB, [(row * NB + half * HALF, HALF)]))
    fock_other(terms, weights, external, th, tl, nh, nl, rho, scale, give, keep, cross_ref)


def fock_other_later(
    weights, external, th, tl, nh, nl, rho, mine, arrived, scale, give, keep, cross_ref
):
    at = core_of() * 2 * SB
    part = [
        a + b for a, b in zip(packed_part(mine), packed_part(arrived))
    ]
    terms = [(split(upper_form(part)), at, SB, [(at, SB)])]
    fock_other(terms, weights, external, th, tl, nh, nl, rho, scale, give, keep, cross_ref)


def fock_side(th, tl, nh, nl, scale, side_a, side_b):
    at = core_of() * SB
    scaled = scaled_rows(th, tl, at, 4 * NB, scale)
    low = fock_block(both(scaled, slice(0, SB)), nh, nl, at, SB)
    both_rows = fock_block(both(scaled, slice(NB, 4 * NB)), nh, nl, at + SB, SB)
    put_side(low, both_rows[:NB, :NB], both_rows[NB:], side_a, side_b)


def coefficient_parts(value, high, low, turned_high, turned_low):
    high[...], low[...] = split(value)
    turned_high[...], turned_low[...] = split(value.T)


def spread_kernel(
    total_blocks, own_lists, other_lists, own, early, partner, coef, ch, cl, th, tl, present
):
    coef[...] = jnp.zeros_like(coef)
    for d in range(4):
        for i in range(4):
            blocks = own_lists if d < 2 else other_lists
            at = aligned(relative(blocks[d % 2, i], total_blocks), NB)
            cols = slice(d * NB, (d + 1) * NB)
            if d < 2:
                coef[pl.ds(at, NB), cols] = own[4 * d + i]
                continue
            for half in range(2):
                index = 2 * (4 * (d - 2) + i) + half
                value = early[index] if index < EARLY else partner[index - EARLY]
                coef[pl.ds(at + half * HALF, HALF), cols] = value
    coefficient_parts(coef[...], ch, cl, th, tl)
    for d in range(4):
        blocks = own_lists if d < 2 else other_lists
        for r in range(6):
            held = relative(blocks[d % 2, 0], total_blocks) == r
            for i in range(1, 4):
                held = held | (relative(blocks[d % 2, i], total_blocks) == r)
            row = 6 * d + r
            present[row : row + 1, :] = jnp.full((1, NB), jnp.where(held, 1.0, 0.0), f32)


def gather_kernel(first, second, coef, ch, cl, th, tl):
    core = core_of()
    for source, at, block, count in (
        (first, 0, 4 * core, 2),
        (first, SB, 2 + core, 1),
        (second, 0, 4 - 4 * core, 2),
        (second, SB, 3 - core, 1),
    ):
        coef[pl.ds(aligned(block, NB), count * NB), :] = source[at : at + count * NB, :]
    coefficient_parts(coef[...], ch, cl, th, tl)


def mixing(th, tl, places, gradient):
    rows = lax.broadcasted_iota(jnp.int32, (SB, SB), 0) < NB
    same = rows == (lax.broadcasted_iota(jnp.int32, (SB, SB), 1) < NB)
    result = []
    for pair in range(2):
        at = slice(pair * SB, (pair + 1) * SB)
        left = []
        for ref in (th, tl):
            parts = [ref[at, pl.ds(pl.multiple_of(start, NB), count)] for start, count in places]
            left.append(parts[0] if len(parts) == 1 else jnp.concatenate(parts, axis=1))
        value = dot3(left, both(gradient, slice(None), at))
        result.append(jnp.where(same, value, 0.0))
    return result


def domain_side(side_a, side_b, ch, cl, th, tl, gradient, mixed):
    low, cross, high = side_parts(side_a, side_b)
    at = core_of() * SB
    zero = jnp.zeros((NB, NB), f32)
    first = jnp.concatenate([unpack(low), jnp.concatenate([zero, cross.T], axis=1)], axis=0)
    last = jnp.concatenate([jnp.concatenate([cross, zero], axis=1), unpack(high)], axis=0)

    def coef(start):
        rows = pl.ds(pl.multiple_of(start, SB), SB)
        return ch[rows, :], cl[rows, :]

    upper = dot3(split(first), coef(at))
    lower = dot3(split(last), coef(at + SB))
    gradient[:NB, :] = upper[:NB]
    gradient[NB : 3 * NB, :] = upper[NB:] + lower[: 2 * NB]
    gradient[3 * NB :, :] = lower[2 * NB :]
    for pair, value in enumerate(mixing(th, tl, [(at, 4 * NB)], split(gradient[...]))):
        mixed[pair] = value


def domain_mixed(
    ch, cl, th, tl, gradient, mixed, side_b, other, work, total, cross_ref
):
    core = core_of()
    part, cross = other_parts(side_b, other, cross_ref)
    zero = jnp.zeros((NB, NB), f32)
    beside = jnp.where(core == 0, cross, cross.T)
    across = jnp.where(core == 0, cross.T, cross)
    placed = jnp.concatenate(
        [jnp.where(core == 0, beside, zero), jnp.where(core == 0, zero, beside)], axis=1
    )
    slab = jnp.concatenate([unpack(part), placed], axis=0)
    other_at = (2 - 2 * core) * SB
    other_rows = pl.ds(pl.multiple_of(other_at, SB), SB)
    side_block = pl.ds(pl.multiple_of((3 - core) * NB, NB), NB)
    touching = pl.ds(pl.multiple_of((4 - 3 * core) * NB, NB), NB)
    work[pl.ds(pl.multiple_of(core * SB, SB), 4 * NB), :] = gradient[...]
    product = dot3(split(slab), (ch[other_rows, :], cl[other_rows, :]))
    work[other_rows, :] = product[:SB]
    back = dot3(split(across), (ch[side_block, :], cl[side_block, :]))
    work[touching, :] += back
    work[side_block, :] += product[SB:]
    stacked = jnp.concatenate([work[other_rows, :], product[SB:]], axis=0)
    added = mixing(th, tl, [(other_at, SB), ((3 - core) * NB, NB)], split(stacked))
    for pair in range(2):
        total[pair] = mixed[pair] + added[pair]


def new_blocks(present, coef, ch, cl, work, total, places, fresh, fh, fl):
    for d in range(0, 4, 2):
        cols = slice(d * NB, (d + 2) * NB)
        square = split(total[d // 2])
        for block, count, at in places:
            rows = pl.ds(aligned(block, NB), count * NB)
            moved = dot3((ch[rows, cols], cl[rows, cols]), square)
            for r in range(count):
                rows = pl.ds(aligned(block + r, NB), NB)
                out_rows = slice(at + r * NB, at + (r + 1) * NB)
                for e in range(2):
                    out_cols = slice((d + e) * NB, (d + e + 1) * NB)
                    kept = work[rows, out_cols] * present[pl.ds(6 * (d + e) + block + r, 1), :]
                    piece = moved[r * NB : (r + 1) * NB, e * NB : (e + 1) * NB]
                    value = coef[rows, out_cols] - step_scale * (kept - piece)
                    fresh[out_rows, out_cols] = value
                    fh[out_rows, out_cols], fl[out_rows, out_cols] = split(value)


def outer(left, at, count, right, from_at, from_count):
    left_rows, right_rows = pl.ds(at, count), pl.ds(from_at, from_count)
    return dot3(
        (left[0][left_rows, :], left[1][left_rows, :]),
        (right[0][right_rows, :], right[1][right_rows, :]),
        ((1,), (1,)),
    )


def domain_far_rows(
    present, coef, ch, cl, th, tl, gradient, mixed, side_b, other,
    fresh, fh, fl, work, total, cross_ref,
):
    domain_mixed(ch, cl, th, tl, gradient, mixed, side_b, other, work, total, cross_ref)
    core = core_of()
    places = ((4 * core, 2, 0), (2 + core, 1, SB))
    new_blocks(present, coef, ch, cl, work, total, places, fresh, fh, fl)


def domain_far(
    present, coef, ch, cl, th, tl, gradient, mixed, side_b, other,
    fresh, fh, fl, work, total, message, cross_ref,
):
    domain_far_rows(
        present, coef, ch, cl, th, tl, gradient, mixed, side_b, other,
        fresh, fh, fl, work, total, cross_ref,
    )
    core = core_of()
    far = (fh, fl)
    put_pair(outer(far, 0, SB, far, 0, SB), message.at[:PACKED], message.at[PACKED:PAIR])
    cross = outer(far, SB, NB, far, aligned(1 - core, NB), NB)
    message[PAIR:, :] = jnp.where(core == 0, cross.T, cross)


def other_blocks(present, coef, ch, cl, work, total, fresh, fh, fl):
    core = core_of()
    places = ((4 - 4 * core, 2, 0), (3 - core, 1, SB))
    new_blocks(present, coef, ch, cl, work, total, places, fresh, fh, fl)


def domain_other(
    present, coef, ch, cl, work, total, fresh, fh, fl, give, keep, cross_ref
):
    other_blocks(present, coef, ch, cl, work, total, fresh, fh, fl)
    core = core_of()
    rest = (fh, fl)
    cross = outer(rest, SB, NB, rest, aligned(core, NB), NB)
    cross_ref[...] = jnp.where(core == 0, cross, cross.T)
    put_other(outer(rest, 0, SB, rest, 0, SB), cross_ref, give, keep)


def near_rows(f1, f2):
    core = core_of()
    touching, beside = f1[SB:, :], f2[SB:, :]
    return jnp.concatenate(
        [jnp.where(core == 0, touching, beside), jnp.where(core == 0, beside, touching)], axis=0
    )


def density_near(f1h, f1l, f2h, f2l, near):
    rows = (near_rows(f1h, f2h), near_rows(f1l, f2l))
    put_pair(dot3(rows, rows, ((1,), (1,))), near.at[:PACKED], near.at[PACKED:])


def half_rows(ref):
    def store(index, value):
        ref[pl.ds(aligned(index, HALF), HALF), :] = value

    return store


def half_blocks(ref):
    def store(index, value):
        ref[index] = value

    return store


def owner_half(left, store, first):
    half = lax.axis_index("orb")
    for i in range(2):
        rows = outer(left, pl.multiple_of(i * NB + half * HALF, HALF), HALF, left, 0, SB)
        store(2 * i + 1 - first, rows[:, :NB])
        store(2 * i + 2 - first, rows[:, NB:])


def domain_edge(
    present, coef, ch, cl, th, tl, gradient, mixed, side_b, other,
    fresh, fh, fl, work, total, edge, cross_ref,
):
    domain_far_rows(
        present, coef, ch, cl, th, tl, gradient, mixed, side_b, other,
        fresh, fh, fl, work, total, cross_ref,
    )
    core = core_of()
    far = (fh, fl)
    owner_half(far, half_rows(edge), 1 - core)
    edge[5 * HALF :, :] = jnp.zeros((2 * TILE, NB), f32)
    at = pl.multiple_of((1 - core) * NB + lax.axis_index("orb") * HALF, HALF)
    half_rows(edge)(4 - 4 * core, outer(far, at, HALF, far, SB, NB))


def domain_give(present, coef, ch, cl, work, total, fresh, fh, fl, give):
    other_blocks(present, coef, ch, cl, work, total, fresh, fh, fl)
    core = core_of()
    rest = (fh, fl)
    owner_half(rest, half_blocks(give), core)
    at = pl.multiple_of(core * NB + lax.axis_index("orb") * HALF, HALF)
    give[4 * core] = outer(rest, at, HALF, rest, SB, NB)


def domain_last(total_blocks, own_lists, fresh1, f1h, f1l, fresh2, f2h, f2l, result, own, window, nh, nl):
    core = core_of()
    half = lax.axis_index("orb")
    nh[...] = near_rows(f1h, f2h)
    nl[...] = near_rows(f1l, f2l)
    near = (nh, nl)
    owner_half(near, half_blocks(own), 0)
    rows = pl.multiple_of(half * HALF, HALF)

    def far_or_rest(row_at, first_at, second_at):
        left = (nh[pl.ds(row_at, HALF), :], nl[pl.ds(row_at, HALF), :])
        first = pl.ds(first_at, NB)
        second = pl.ds(second_at, NB)
        right = [
            jnp.where(core == 0, a[first, :], b[second, :]) for a, b in ((f1h, f2h), (f1l, f2l))
        ]
        return dot3(left, right, ((1,), (1,)))

    def rest_or_far(row_at, first_at, second_at):
        left = (nh[pl.ds(row_at, HALF), :], nl[pl.ds(row_at, HALF), :])
        first = pl.ds(first_at, NB)
        second = pl.ds(second_at, NB)
        right = [
            jnp.where(core == 0, b[first, :], a[second, :]) for a, b in ((f1h, f2h), (f1l, f2l))
        ]
        return dot3(left, right, ((1,), (1,)))

    own[0] = far_or_rest(rows, NB, NB)
    own[5] = rest_or_far(pl.multiple_of(NB + half * HALF, HALF), 0, 0)
    for source, at, block, count in (
        (fresh1, 0, 4 * core, 2),
        (fresh1, SB, 2 + core, 1),
        (fresh2, 0, 4 - 4 * core, 2),
        (fresh2, SB, 3 - core, 1),
    ):
        window[pl.ds(aligned(block, NB), count * NB), :] = source[at : at + count * NB, :SB]
    for d in range(2):
        for i in range(4):
            at = aligned(relative(own_lists[d, i], total_blocks), NB)
            result[d, i] = window[pl.ds(at, NB), d * NB : (d + 1) * NB]


def owner_kernel(own, from_core, from_edge, out):
    core = core_of()
    edge = [from_edge[i * HALF : (i + 1) * HALF, :] for i in range(5)]
    lower = [jnp.where(core == 0, from_core[i], edge[i]) for i in range(5)]
    upper = [jnp.where(core == 0, edge[i], from_core[i]) for i in range(5)]
    out[0] = own[0] + upper[0]
    for i in range(1, 5):
        out[i] = own[i] + upper[i] + lower[i - 1]
    out[5] = own[5] + lower[4]


def to_core(value):
    count = lax.axis_size("grid")
    return lax.ppermute(value, "grid", [(i, i ^ 1) for i in range(count)])


def to_edge(value):
    count = lax.axis_size("grid")
    route = [(i, (i + 1) % count if i % 2 else (i - 1) % count) for i in range(count)]
    return lax.ppermute(value, "grid", route)


def to_orb(value):
    return lax.ppermute(value, "orb", [(0, 1), (1, 0)])


A_OUT = vmem((A_ROWS, NB))
B_OUT = vmem((B_ROWS, NB))
BK_OUT = vmem((B_ROWS + HALF, NB))
GIVE_OUT = vmem((GIVE_ROWS, NB))
KEEP_OUT = vmem((HALF, NB))
CROSS = vmem((NB, NB))


def total_over_all(made, after_near, before_sum):
    side_a, side_b, keep, arrived = made
    side_a, side_b = call(
        near_keep_kernel,
        (side_a, side_b, keep, arrived),
        (vmem((A_ROWS + HALF, NB)), B_OUT),
        "add_near",
    )
    side_b = after_near(side_b)
    first_b = to_edge(side_b)
    first_a = to_orb(side_a)
    side_a, keep = call(add_keep_kernel, (side_a, first_a), (A_OUT, KEEP_OUT), "add_a")
    last_a = to_edge(side_a)
    (side_b,) = call(add_kernel, (side_b, first_b), (B_OUT,), "add_b")
    last_b = before_sum(to_orb(side_b))
    side_a, side_b, near = call(
        total_kernel,
        (side_a, last_a, side_b, last_b, keep),
        (A_OUT, BK_OUT, GIVE_OUT),
        "add_all",
    )
    return side_a, side_b, to_core(near)


def shards(
    density, basis_values, quad_weights, ext_potential, batch_blocks, domain_blocks, coefficients
):
    total_blocks = density.shape[0] * lax.axis_size("grid")
    points = basis_values.shape[1]
    core = lax.rem(lax.axis_index("grid"), 2)
    window = 6 * NB
    row_out = vmem((1, points))
    coef_out = vmem((window, 4 * NB))
    coef_half = vmem((window, 4 * NB), bf16)
    turned_half = vmem((4 * NB, window), bf16)
    unit = 2 * 3 * points * SB * SB

    blocks = coefficients.reshape(8, NB, NB)
    own = density.reshape(6, HALF, NB)
    edge = to_edge(own)
    own_far = to_orb(own)
    other = to_core(own)
    *basis, done = sort_basis(total_blocks, batch_blocks, basis_values, unit)
    th, tl, nh, nl = basis
    near, early, rest, list_row = cut(domain_blocks, own, blocks.reshape(16, HALF, NB), other)
    early = to_orb(early)
    (own_far,) = call(hold_kernel, (own_far, done), (vmem((6, HALF, NB)),), "hold")
    other_far = to_core(own_far)
    (edge_message,) = call(
        far_kernel,
        (list_row, edge, done),
        (vmem((5 * HALF + TILE, NB)),),
        "far_message",
    )
    edge_far = to_orb(edge_message)
    (rho,) = call(
        rho_first,
        (th, tl, near, own_far, edge, other, other_far, early),
        (row_out,),
        "rho_first",
        flops=5 * unit,
    )
    edge_far, rho = lax.optimization_barrier((edge_far, rho))
    other_lists = edge_far[5 * HALF, :8].reshape(2, 4).astype(jnp.int32)

    packed = None
    for iteration in range(ITERS):
        if iteration == 0:
            kernel, operands = fock_other_first, (edge_far,)
        else:
            kernel, operands = fock_other_later, packed
        scale, give, keep = call(
            kernel,
            (quad_weights, ext_potential, *basis, rho, *operands),
            (row_out, GIVE_OUT, KEEP_OUT),
            "fock_other",
            scratch=(CROSS,),
            plain=(0, 1),
            flops=3 * unit,
        )
        arrived = to_core(give)
        side_a, side_b = call(
            fock_side, (*basis, scale), (A_OUT, B_OUT), "fock_side", flops=3 * unit
        )
        ready = {}

        def after_near(value):
            if iteration == 0:
                value, mine = lax.optimization_barrier((value, rest))
                ready["partner"] = to_orb(mine)
            return value

        def before_sum(value):
            if iteration == 0:
                made = call(
                    functools.partial(spread_kernel, total_blocks),
                    (domain_blocks, other_lists, blocks, hbm(early), hbm(ready["partner"])),
                    (coef_out, coef_half, coef_half, turned_half, turned_half, vmem((24, NB))),
                    "spread",
                    smem=(0, 1),
                    plain=(2, 3, 4),
                    flops=3 * unit,
                )
            else:
                made = call(
                    gather_kernel,
                    (fresh1, fresh2),
                    (coef_out, coef_half, coef_half, turned_half, turned_half),
                    "gather",
                    flops=3 * unit,
                )
            value, *ready["made"] = lax.optimization_barrier((value, *made))
            return value

        side_a, side_b, arriving = total_over_all(
            (side_a, side_b, keep, arrived), after_near, before_sum
        )
        if iteration == 0:
            coef, *halves, present = ready["made"]
        else:
            coef, *halves = ready["made"]
        gradient, mixed = call(
            domain_side,
            (side_a, side_b, *halves),
            (vmem((4 * NB, 4 * NB)), vmem((2, SB, SB))),
            "domain_side",
            flops=unit,
        )
        operands = (
            present, coef, *halves, gradient, mixed, side_b, arriving
        )
        new_outs = (vmem((3 * NB, 4 * NB)),) + (vmem((3 * NB, 4 * NB), bf16),) * 2
        far_outs = new_outs + (coef_out, vmem((2, SB, SB)))
        if iteration < ITERS - 1:
            fresh1, f1h, f1l, work, total, mine = call(
                domain_far,
                operands,
                far_outs + (vmem((PAIR + NB, NB)),),
                "domain_far",
                scratch=(CROSS,),
                flops=2 * unit,
            )
            from_far = to_edge(mine)
            fresh2, f2h, f2l, give, keep = call(
                domain_other,
                (present, coef, *halves[:2], work, total),
                new_outs + (GIVE_OUT, KEEP_OUT),
                "domain_other",
                scratch=(CROSS,),
                flops=unit,
            )
            arrived = to_core(give)
            (near,) = call(
                density_near, (f1h, f1l, f2h, f2l), (vmem((PAIR, NB)),), "density_near"
            )
            near, keep = call(
                near_sum_kernel,
                (near, keep, arrived),
                (vmem((PAIR + STRIP, NB)), KEEP_OUT),
                "add_near",
            )
            from_near = to_edge(near)
            near_total, cross = call(
                near_total_kernel, (near, keep, mine, from_far), (GIVE_OUT, CROSS), "add_far"
            )
            arriving = to_core(near_total)
            (rho,) = call(rho_near, (th, tl, near_total, cross), (row_out,), "rho_near", flops=unit)
            (rho,) = call(
                rho_other,
                (th, tl, rho, near_total, arriving),
                (row_out,),
                "rho_other",
                scratch=(CROSS,),
            )
            packed = (mine, from_near)
    message = vmem((5, HALF, NB))
    edge_message = vmem((5 * HALF + 2 * TILE, NB))
    fresh1, f1h, f1l, work, total, edge = call(
        domain_edge, operands, far_outs + (edge_message,), "domain_edge", scratch=(CROSS,), flops=2 * unit
    )
    from_edge = to_edge(edge)
    fresh2, f2h, f2l, give = call(
        domain_give,
        (present, coef, *halves[:2], work, total),
        new_outs + (message,),
        "domain_give",
        flops=unit,
    )
    from_core = to_core(give)
    result, own = call(
        functools.partial(domain_last, total_blocks),
        (domain_blocks, fresh1, f1h, f1l, fresh2, f2h, f2l),
        (jax.ShapeDtypeStruct(coefficients.shape, f32), vmem((6, HALF, NB))),
        "domain_last",
        scratch=(vmem((window, SB)),) + (vmem((SB, 4 * NB), bf16),) * 2,
        smem=(0,),
    )
    (rows,) = call(
        owner_kernel,
        (own, from_core, from_edge),
        (jax.ShapeDtypeStruct((6, HALF, NB), f32),),
        "owner_rows",
    )
    return (rows.reshape(density.shape), result)


def solution(mesh):
    in_specs = (
        P("grid", None, "orb", None),
        P(("grid", "orb"), None, None),
        P(("grid", "orb"), None),
        P(("grid", "orb"), None),
        P(("grid", "orb"), None),
        P(("grid", "orb"), None),
        P(("grid", "orb"), None, None, None),
    )
    out_specs = (P("grid", None, "orb", None), P(("grid", "orb"), None, None, None))
    return jax.shard_map(shards, mesh=mesh, in_specs=in_specs, out_specs=out_specs, check_vma=False)
```

```python
import functools
import jax
import jax.numpy as jnp
from jax import lax
from jax.experimental import pallas as pl
from jax.experimental.pallas import tpu as pltpu
from jax.sharding import PartitionSpec as P

ITERS = 2
step_scale = 0.5

NB = 128
SB = 2 * NB
TILE = 8
HALF = NB // 2
PACKED = NB + TILE
VMEM_BYTES = 16 * 1024 * 1024
POINT_CHUNK = 256
f32 = jnp.float32
bf16 = jnp.bfloat16

LOW = slice(0, PACKED)
HIGH = slice(PACKED + HALF, 2 * PACKED + HALF)
A_ROWS = 2 * PACKED + HALF
B_ROWS = 2 * NB + HALF
PAIR = PACKED + NB
GIVE_ROWS = PAIR + HALF
EARLY = 8
STRIP = HALF + TILE
KEEP_AT = 2 * NB + HALF


def split(value):
    high = value.astype(bf16)
    return high, (value - high.astype(f32)).astype(bf16)


def dot3(left, right, contract=((1,), (0,))):
    def one(a, b):
        return lax.dot_general(a, b, (contract, ((), ())), preferred_element_type=f32)

    cross_left = jnp.concatenate([left[0], left[1]], axis=contract[0][0])
    cross_right = jnp.concatenate([right[1], right[0]], axis=contract[1][0])
    return one(left[0], right[0]) + one(cross_left, cross_right)


def both(pair, *index):
    return pair[0][index], pair[1][index]


def row_col():
    rows = lax.broadcasted_iota(jnp.int32, (NB, NB), 0)
    return rows, lax.broadcasted_iota(jnp.int32, (NB, NB), 1)


def aligned(value, unit):
    return pl.multiple_of(value * unit, unit)


def core_of():
    return lax.rem(lax.axis_index("grid"), 2)


def relative(block, total_blocks):
    anchor = (lax.axis_index("grid") - 1) * 2
    return lax.rem(block - anchor + total_blocks, total_blocks)


def vmem(shape, kind=f32):
    return pltpu.VMEM(shape, kind)


def call(kernel, operands, outs, name, scratch=(), smem=(), plain=(), flops=0):
    specs, pinned = [], []
    for i, operand in enumerate(operands):
        specs.append(pl.BlockSpec(memory_space=pltpu.SMEM if i in smem else pltpu.VMEM))
        if i in smem or i in plain:
            pinned.append(hbm(operand) if i in smem else operand)
        else:
            pinned.append(pltpu.with_memory_space_constraint(operand, pltpu.VMEM))
    return pl.pallas_call(
        kernel,
        out_shape=list(outs),
        in_specs=specs,
        out_specs=[pl.BlockSpec(memory_space=pltpu.VMEM) for _ in outs],
        scratch_shapes=list(scratch),
        compiler_params=pltpu.CompilerParams(vmem_limit_bytes=VMEM_BYTES),
        cost_estimate=pl.CostEstimate(flops=flops, bytes_accessed=0, transcendentals=0),
        name=name,
    )(*pinned)


def sort_kernel(total_blocks, blocks, basis, th, tl, nh, nl, done, columns, arrived):
    def copy(j):
        source = basis.at[0, :, pl.ds(j * NB, NB)]
        return pltpu.make_async_copy(source, columns.at[j], arrived.at[j])

    for j in range(6):
        copy(j).start()
    for j in range(6):
        at = pl.ds(aligned(relative(blocks[0, j], total_blocks), NB), NB)
        copy(j).wait()
        column = columns[j]
        nh[:, at], nl[:, at] = split(column)
        th[at, :], tl[at, :] = split(column.T)
    done[...] = jnp.zeros_like(done)


def cut_kernel(lists, own, halves, other, near, early, rest, row, sems):
    copies = [
        pltpu.make_async_copy(own, near, sems.at[0]),
        pltpu.make_async_copy(halves.at[pl.ds(0, EARLY)], early, sems.at[1]),
        pltpu.make_async_copy(halves.at[pl.ds(EARLY, 16 - EARLY)], rest, sems.at[2]),
    ]
    for copy in copies:
        copy.start()
    lanes = lax.broadcasted_iota(jnp.int32, (TILE, NB), 1)
    values = jnp.zeros((TILE, NB), f32)
    for d in range(2):
        for i in range(4):
            values = jnp.where(lanes == 4 * d + i, lists[d, i].astype(f32), values)
    row[...] = values
    for copy in copies:
        copy.wait()


def hbm(value):
    return pltpu.with_memory_space_constraint(value, pltpu.HBM)


def cut(lists, own, halves, other):
    return pl.pallas_call(
        cut_kernel,
        out_shape=[vmem(own.shape), vmem((EARLY, HALF, NB)), vmem((16 - EARLY, HALF, NB))]
        + [vmem((TILE, NB))],
        in_specs=[pl.BlockSpec(memory_space=pltpu.SMEM)]
        + [pl.BlockSpec(memory_space=pl.ANY)] * 2
        + [pl.BlockSpec(memory_space=pltpu.VMEM)],
        out_specs=[pl.BlockSpec(memory_space=pltpu.VMEM)] * 4,
        scratch_shapes=[pltpu.SemaphoreType.DMA((3,))],
        compiler_params=pltpu.CompilerParams(vmem_limit_bytes=VMEM_BYTES),
        name="cut",
    )(hbm(lists), hbm(own), hbm(halves), other)


def hold_kernel(value, done, out):
    out[...] = value[...]


def sort_basis(total_blocks, batch_blocks, basis_values, unit):
    points, window = basis_values.shape[1:]
    halves = [vmem((window, points), bf16)] * 2 + [vmem((points, window), bf16)] * 2
    return pl.pallas_call(
        functools.partial(sort_kernel, total_blocks),
        out_shape=halves + [vmem((TILE, NB))],
        in_specs=[pl.BlockSpec(memory_space=pltpu.SMEM), pl.BlockSpec(memory_space=pl.ANY)],
        out_specs=[pl.BlockSpec(memory_space=pltpu.VMEM)] * 5,
        scratch_shapes=[vmem((6, points, NB)), pltpu.SemaphoreType.DMA((6,))],
        compiler_params=pltpu.CompilerParams(vmem_limit_bytes=VMEM_BYTES),
        cost_estimate=pl.CostEstimate(flops=6 * unit, bytes_accessed=0, transcendentals=0),
        name="sort_basis",
    )(hbm(batch_blocks), hbm(basis_values))


def put_pair(pair, packed, off):
    rows, cols = row_col()
    first, last = pair[:NB, :NB], pair[NB:, NB:]
    diagonal = jnp.sum(jnp.where(rows == cols, last, 0.0), axis=0, keepdims=True)
    packed[:NB, :] = jnp.where(rows <= cols, first, last)
    packed[NB:PACKED, :] = jnp.broadcast_to(diagonal, (TILE, NB))
    off[...] = pair[:NB, NB:]


def put_side(low, cross, high, side_a, side_b):
    put_pair(low, side_a.at[LOW], side_b.at[:NB])
    put_pair(high, side_a.at[HIGH], side_b.at[KEEP_AT - NB : KEEP_AT])
    side_a[PACKED : PACKED + HALF, :] = cross[:HALF]
    side_b[NB : NB + HALF, :] = cross[HALF:]


def put_other(pair, cross_ref, give, keep):
    core = core_of()
    put_pair(pair, give.at[:PACKED], give.at[PACKED:PAIR])
    give[PAIR:, :] = cross_ref[pl.ds(aligned(1 - core, HALF), HALF), :]
    keep[...] = cross_ref[pl.ds(aligned(core, HALF), HALF), :]


def side_parts(side_a, side_b):
    low = (side_a[:NB, :], side_a[NB : NB + 1, :], side_b[:NB, :])
    start = PACKED + HALF
    high = (
        side_a[start : start + NB, :],
        side_a[start + NB : start + NB + 1, :],
        side_b[NB + HALF : KEEP_AT, :],
    )
    cross = jnp.concatenate([side_a[PACKED:start, :], side_b[NB : NB + HALF, :]], axis=0)
    return low, cross, high


def other_parts(side_b, other, cross_ref):
    core = core_of()
    cross_ref[pl.ds(aligned(core, HALF), HALF), :] = side_b[KEEP_AT:, :]
    cross_ref[pl.ds(aligned(1 - core, HALF), HALF), :] = other[PAIR:, :]
    return (other[:NB, :], other[NB : NB + 1, :], other[PACKED:PAIR, :]), cross_ref[...]


def unpack(part):
    merged, diagonal, off = part
    rows, cols = row_col()
    turned = merged.T
    first = jnp.where(rows <= cols, merged, turned)
    last = jnp.where(rows > cols, merged, jnp.where(rows < cols, turned, diagonal))
    return join(first, off, off.T, last)


def join(a, b, c, d):
    return jnp.concatenate(
        [jnp.concatenate([a, b], axis=1), jnp.concatenate([c, d], axis=1)], axis=0
    )


def upper_form(part):
    merged, diagonal, off = part
    rows, cols = row_col()
    twice = merged * 2.0
    first = jnp.where(rows < cols, twice, jnp.where(rows == cols, merged, 0.0))
    last = jnp.where(rows > cols, twice, jnp.where(rows == cols, diagonal, 0.0))
    return join(first, off * 2.0, jnp.zeros((NB, NB), f32), last)


def near_kernel(side_a, side_b, keep, arrived, out_a, out_b, out_keep):
    core = core_of()
    out_a[...] = side_a[...]
    out_b[...] = side_b[...]
    out_keep[...] = keep[...] + arrived[PAIR:, :]
    rows_a = pl.ds(pl.multiple_of((1 - core) * (PACKED + HALF), TILE), PACKED)
    rows_b = pl.ds(pl.multiple_of((1 - core) * (NB + HALF), TILE), NB)
    out_a[rows_a, :] = side_a[rows_a, :] + arrived[:PACKED, :]
    out_b[rows_b, :] = side_b[rows_b, :] + arrived[PACKED:PAIR, :]


def near_keep_kernel(side_a, side_b, keep, arrived, out_a, out_b):
    near_kernel(side_a, side_b, keep, arrived, out_a.at[:A_ROWS], out_b, out_a.at[A_ROWS:])


def add_kernel(left, right, out):
    out[...] = left[...] + right[...]


def add_keep_kernel(side_a, arrived, out, keep):
    out[...] = side_a[:A_ROWS, :] + arrived[:A_ROWS, :]
    keep[...] = side_a[A_ROWS:, :] + arrived[A_ROWS:, :]


def side_near(out_a, out_b, near):
    core = core_of()
    rows_a = pl.ds(pl.multiple_of((1 - core) * (PACKED + HALF), TILE), PACKED)
    rows_b = pl.ds(pl.multiple_of((1 - core) * (NB + HALF), TILE), NB)
    near[:PACKED, :] = out_a[rows_a, :]
    near[PACKED:PAIR, :] = out_b[rows_b, :]
    near[PAIR:, :] = out_b[KEEP_AT:, :]


def total_kernel(side_a, arrived_a, side_b, arrived_b, keep, out_a, out_b, near):
    out_a[...] = side_a[...] + arrived_a[...]
    out_b[:KEEP_AT, :] = side_b[...] + arrived_b[...]
    out_b[KEEP_AT:, :] = keep[...]
    side_near(out_a, out_b, near)


def near_sum_kernel(near, keep, arrived, out, out_keep):
    out[:PAIR, :] = near[...] + arrived[:PAIR, :]
    out[PAIR:, :] = jnp.zeros((STRIP, NB), f32)
    out_keep[...] = keep[...] + arrived[PAIR:, :]


def near_total_kernel(near, keep, mine, arrived, out, cross):
    out[:PAIR, :] = near[:PAIR, :] + arrived[:PAIR, :]
    cross[...] = mine[PAIR:, :] + arrived[PAIR:, :]
    out[PAIR:, :] = keep[...]


def add_density(terms, th, tl, before, after):
    points = th.shape[1]
    for start in range(0, points, POINT_CHUNK):
        cols = slice(start, start + POINT_CHUNK)
        rho = before(cols)
        for matrix, at, count, values in terms:
            rows = pl.ds(pl.multiple_of(at, HALF), count)
            value = []
            for value_at, value_count in values:
                value_rows = pl.ds(pl.multiple_of(value_at, HALF), value_count)
                value.append(th[value_rows, cols].astype(f32) + tl[value_rows, cols].astype(f32))
            value = value[0] if len(value) == 1 else jnp.concatenate(value, axis=0)
            product = dot3(matrix, (th[rows, cols], tl[rows, cols]))
            rho = rho + jnp.sum(product * value, axis=0, keepdims=True)
        after(cols, rho)


def half_terms(source, first, pair, half, ends):
    body = join(*[source[2 * i + j + 1 - first] for i in range(2) for j in range(2)])
    at = pair * SB
    rows = [(at + half * HALF, HALF), (at + NB + half * HALF, HALF)]
    terms = [(split(body), at, SB, rows)]
    for index, row, col in ends:
        terms.append((split(source[index]), col * NB, NB, [(row * NB + half * HALF, HALF)]))
    return terms


def rho_first(th, tl, own, own_far, edge, other, other_far, early, rho):
    core = core_of()
    orb = lax.axis_index("orb")
    own_ends = ((0, 2, 1), (5, 3, 4))
    other_ends = ((5 * core, 4 - 3 * core, 3 - core),)
    edge_ends = ((5 - 5 * core, 1 + 3 * core, 2 + core),)
    terms = (
        half_terms(own, 0, 1, orb, own_ends)
        + half_terms(own_far, 0, 1, 1 - orb, own_ends)
        + half_terms(other, 0, 2 - 2 * core, orb, other_ends)
        + half_terms(other_far, 0, 2 - 2 * core, 1 - orb, other_ends)
        + half_terms(edge, 0, 2 * core, orb, edge_ends)
    )

    def store(cols, value):
        rho[:, cols] = value

    add_density(terms, th, tl, lambda cols: jnp.zeros((1, POINT_CHUNK), f32), store)


def far_kernel(row, edge, sorted_first, out):
    first = 1 - core_of()
    for i in range(5):
        out[i * HALF : (i + 1) * HALF, :] = edge[i + first]
    out[5 * HALF :, :] = row[...]


def packed_part(ref):
    return ref[:NB, :], ref[NB : NB + 1, :], ref[PACKED:PAIR, :]


def rho_near(th, tl, near, cross, rho):
    def store(cols, value):
        rho[:, cols] = value

    side = core_of() * SB
    terms = [
        (split(upper_form(packed_part(near))), SB, SB, [(SB, SB)]),
        (split(cross[...] * 2.0), side + SB, NB, [(side + NB, NB)]),
    ]
    add_density(terms, th, tl, lambda cols: jnp.zeros((1, POINT_CHUNK), f32), store)


def rho_other(th, tl, before, near, other, rho, mid):
    core = core_of()
    mid[pl.ds(aligned(core, HALF), HALF), :] = near[PAIR:, :]
    mid[pl.ds(aligned(1 - core, HALF), HALF), :] = other[PAIR:, :]
    at = (2 - 2 * core) * SB
    row = (3 - 2 * core) * NB
    terms = [
        (split(upper_form(packed_part(other))), at, SB, [(at, SB)]),
        (split(mid[...] * 2.0), row + NB, NB, [(row, NB)]),
    ]

    def store(cols, value):
        rho[:, cols] = value

    add_density(terms, th, tl, lambda cols: before[:, cols], store)


def scaled_rows(th, tl, at, count, scale):
    rows = pl.ds(pl.multiple_of(at, NB), count)
    return split((th[rows, :].astype(f32) + tl[rows, :].astype(f32)) * scale[...])


def fock_block(left, nh, nl, at, count):
    cols = pl.ds(pl.multiple_of(at, NB), count)
    return dot3(left, (nh[:, cols], nl[:, cols]))


def fock_other(terms, weights, external, th, tl, nh, nl, rho, scale, give, keep, cross_ref):
    core = core_of()

    def store(cols, value):
        scale[:, cols] = value

    add_density(terms, th, tl, lambda cols: rho[:, cols], store)
    value = scale[...]
    potential = external[...] - jnp.exp(jnp.log(value * value + 1.0) * (1.0 / 6.0))
    scale[...] = weights[...] * potential
    at = (2 - 2 * core) * SB
    pair = fock_block(scaled_rows(th, tl, at, SB, scale), nh, nl, at, SB)
    row = (3 - 2 * core) * NB
    cross_ref[...] = fock_block(scaled_rows(th, tl, row, NB, scale), nh, nl, row + NB, NB)
    put_other(pair, cross_ref, give, keep)


def fock_other_first(
    weights, external, th, tl, nh, nl, rho, edge_far, scale, give, keep, cross_ref
):
    core = core_of()
    ends = ((4 - 4 * core, 1 + 3 * core, 2 + core),)

    def far(index):
        return edge_far[pl.ds(aligned(index, HALF), HALF), :]

    body = join(*[far(2 * i + j + core) for i in range(2) for j in range(2)])
    half = 1 - lax.axis_index("orb")
    at = 2 * core * SB
    rows = [(at + half * HALF, HALF), (at + NB + half * HALF, HALF)]
    terms = [(split(body), at, SB, rows)]
    for index, row, col in ends:
        terms.append((split(far(index)), col * NB, NB, [(row * NB + half * HALF, HALF)]))
    fock_other(terms, weights, external, th, tl, nh, nl, rho, scale, give, keep, cross_ref)


def fock_other_later(
    weights, external, th, tl, nh, nl, rho, mine, arrived, scale, give, keep, cross_ref
):
    at = core_of() * 2 * SB
    part = [
        a + b for a, b in zip(packed_part(mine), packed_part(arrived))
    ]
    terms = [(split(upper_form(part)), at, SB, [(at, SB)])]
    fock_other(terms, weights, external, th, tl, nh, nl, rho, scale, give, keep, cross_ref)


def fock_side(th, tl, nh, nl, scale, side_a, side_b):
    at = core_of() * SB
    scaled = scaled_rows(th, tl, at, 4 * NB, scale)
    low = fock_block(both(scaled, slice(0, SB)), nh, nl, at, SB)
    both_rows = fock_block(both(scaled, slice(NB, 4 * NB)), nh, nl, at + SB, SB)
    put_side(low, both_rows[:NB, :NB], both_rows[NB:], side_a, side_b)


def coefficient_parts(value, high, low, turned_high, turned_low):
    high[...], low[...] = split(value)
    turned_high[...], turned_low[...] = split(value.T)


def spread_kernel(
    total_blocks, own_lists, other_lists, own, early, partner, coef, ch, cl, th, tl, present
):
    coef[...] = jnp.zeros_like(coef)
    for d in range(4):
        for i in range(4):
            blocks = own_lists if d < 2 else other_lists
            at = aligned(relative(blocks[d % 2, i], total_blocks), NB)
            cols = slice(d * NB, (d + 1) * NB)
            if d < 2:
                coef[pl.ds(at, NB), cols] = own[4 * d + i]
                continue
            for half in range(2):
                index = 2 * (4 * (d - 2) + i) + half
                value = early[index] if index < EARLY else partner[index - EARLY]
                coef[pl.ds(at + half * HALF, HALF), cols] = value
    coefficient_parts(coef[...], ch, cl, th, tl)
    for d in range(4):
        blocks = own_lists if d < 2 else other_lists
        for r in range(6):
            held = relative(blocks[d % 2, 0], total_blocks) == r
            for i in range(1, 4):
                held = held | (relative(blocks[d % 2, i], total_blocks) == r)
            row = 6 * d + r
            present[row : row + 1, :] = jnp.full((1, NB), jnp.where(held, 1.0, 0.0), f32)


def gather_kernel(first, second, coef, ch, cl, th, tl):
    core = core_of()
    for source, at, block, count in (
        (first, 0, 4 * core, 2),
        (first, SB, 2 + core, 1),
        (second, 0, 4 - 4 * core, 2),
        (second, SB, 3 - core, 1),
    ):
        coef[pl.ds(aligned(block, NB), count * NB), :] = source[at : at + count * NB, :]
    coefficient_parts(coef[...], ch, cl, th, tl)


def mixing(th, tl, places, gradient):
    rows = lax.broadcasted_iota(jnp.int32, (SB, SB), 0) < NB
    same = rows == (lax.broadcasted_iota(jnp.int32, (SB, SB), 1) < NB)
    result = []
    for pair in range(2):
        at = slice(pair * SB, (pair + 1) * SB)
        left = []
        for ref in (th, tl):
            parts = [ref[at, pl.ds(pl.multiple_of(start, NB), count)] for start, count in places]
            left.append(parts[0] if len(parts) == 1 else jnp.concatenate(parts, axis=1))
        value = dot3(left, both(gradient, slice(None), at))
        result.append(jnp.where(same, value, 0.0))
    return result


def domain_side(side_a, side_b, ch, cl, th, tl, gradient, mixed):
    low, cross, high = side_parts(side_a, side_b)
    at = core_of() * SB
    zero = jnp.zeros((NB, NB), f32)
    first = jnp.concatenate([unpack(low), jnp.concatenate([zero, cross.T], axis=1)], axis=0)
    last = jnp.concatenate([jnp.concatenate([cross, zero], axis=1), unpack(high)], axis=0)

    def coef(start):
        rows = pl.ds(pl.multiple_of(start, SB), SB)
        return ch[rows, :], cl[rows, :]

    upper = dot3(split(first), coef(at))
    lower = dot3(split(last), coef(at + SB))
    gradient[:NB, :] = upper[:NB]
    gradient[NB : 3 * NB, :] = upper[NB:] + lower[: 2 * NB]
    gradient[3 * NB :, :] = lower[2 * NB :]
    for pair, value in enumerate(mixing(th, tl, [(at, 4 * NB)], split(gradient[...]))):
        mixed[pair] = value


def domain_mixed(
    ch, cl, th, tl, gradient, mixed, side_b, other, work, total, cross_ref
):
    core = core_of()
    part, cross = other_parts(side_b, other, cross_ref)
    zero = jnp.zeros((NB, NB), f32)
    beside = jnp.where(core == 0, cross, cross.T)
    across = jnp.where(core == 0, cross.T, cross)
    placed = jnp.concatenate(
        [jnp.where(core == 0, beside, zero), jnp.where(core == 0, zero, beside)], axis=1
    )
    slab = jnp.concatenate([unpack(part), placed], axis=0)
    other_at = (2 - 2 * core) * SB
    other_rows = pl.ds(pl.multiple_of(other_at, SB), SB)
    side_block = pl.ds(pl.multiple_of((3 - core) * NB, NB), NB)
    touching = pl.ds(pl.multiple_of((4 - 3 * core) * NB, NB), NB)
    work[pl.ds(pl.multiple_of(core * SB, SB), 4 * NB), :] = gradient[...]
    product = dot3(split(slab), (ch[other_rows, :], cl[other_rows, :]))
    work[other_rows, :] = product[:SB]
    back = dot3(split(across), (ch[side_block, :], cl[side_block, :]))
    work[touching, :] += back
    work[side_block, :] += product[SB:]
    stacked = jnp.concatenate([work[other_rows, :], product[SB:]], axis=0)
    added = mixing(th, tl, [(other_at, SB), ((3 - core) * NB, NB)], split(stacked))
    for pair in range(2):
        total[pair] = mixed[pair] + added[pair]


def new_blocks(present, coef, ch, cl, work, total, places, fresh, fh, fl):
    for d in range(0, 4, 2):
        cols = slice(d * NB, (d + 2) * NB)
        square = split(total[d // 2])
        for block, count, at in places:
            rows = pl.ds(aligned(block, NB), count * NB)
            moved = dot3((ch[rows, cols], cl[rows, cols]), square)
            for r in range(count):
                rows = pl.ds(aligned(block + r, NB), NB)
                out_rows = slice(at + r * NB, at + (r + 1) * NB)
                for e in range(2):
                    out_cols = slice((d + e) * NB, (d + e + 1) * NB)
                    kept = work[rows, out_cols] * present[pl.ds(6 * (d + e) + block + r, 1), :]
                    piece = moved[r * NB : (r + 1) * NB, e * NB : (e + 1) * NB]
                    value = coef[rows, out_cols] - step_scale * (kept - piece)
                    fresh[out_rows, out_cols] = value
                    fh[out_rows, out_cols], fl[out_rows, out_cols] = split(value)


def outer(left, at, count, right, from_at, from_count):
    left_rows, right_rows = pl.ds(at, count), pl.ds(from_at, from_count)
    return dot3(
        (left[0][left_rows, :], left[1][left_rows, :]),
        (right[0][right_rows, :], right[1][right_rows, :]),
        ((1,), (1,)),
    )


def domain_far_rows(
    present, coef, ch, cl, th, tl, gradient, mixed, side_b, other,
    fresh, fh, fl, work, total, cross_ref,
):
    domain_mixed(ch, cl, th, tl, gradient, mixed, side_b, other, work, total, cross_ref)
    core = core_of()
    places = ((4 * core, 2, 0), (2 + core, 1, SB))
    new_blocks(present, coef, ch, cl, work, total, places, fresh, fh, fl)


def domain_far(
    present, coef, ch, cl, th, tl, gradient, mixed, side_b, other,
    fresh, fh, fl, work, total, message, cross_ref,
):
    domain_far_rows(
        present, coef, ch, cl, th, tl, gradient, mixed, side_b, other,
        fresh, fh, fl, work, total, cross_ref,
    )
    core = core_of()
    far = (fh, fl)
    put_pair(outer(far, 0, SB, far, 0, SB), message.at[:PACKED], message.at[PACKED:PAIR])
    cross = outer(far, SB, NB, far, aligned(1 - core, NB), NB)
    message[PAIR:, :] = jnp.where(core == 0, cross.T, cross)


def other_blocks(present, coef, ch, cl, work, total, fresh, fh, fl):
    core = core_of()
    places = ((4 - 4 * core, 2, 0), (3 - core, 1, SB))
    new_blocks(present, coef, ch, cl, work, total, places, fresh, fh, fl)


def domain_other(
    present, coef, ch, cl, work, total, fresh, fh, fl, give, keep, cross_ref
):
    other_blocks(present, coef, ch, cl, work, total, fresh, fh, fl)
    core = core_of()
    rest = (fh, fl)
    cross = outer(rest, SB, NB, rest, aligned(core, NB), NB)
    cross_ref[...] = jnp.where(core == 0, cross, cross.T)
    put_other(outer(rest, 0, SB, rest, 0, SB), cross_ref, give, keep)


def near_rows(f1, f2):
    core = core_of()
    touching, beside = f1[SB:, :], f2[SB:, :]
    return jnp.concatenate(
        [jnp.where(core == 0, touching, beside), jnp.where(core == 0, beside, touching)], axis=0
    )


def density_near(f1h, f1l, f2h, f2l, near):
    rows = (near_rows(f1h, f2h), near_rows(f1l, f2l))
    put_pair(dot3(rows, rows, ((1,), (1,))), near.at[:PACKED], near.at[PACKED:])


def half_rows(ref):
    def store(index, value):
        ref[pl.ds(aligned(index, HALF), HALF), :] = value

    return store


def half_blocks(ref):
    def store(index, value):
        ref[index] = value

    return store


def owner_half(left, store, first):
    half = lax.axis_index("orb")
    for i in range(2):
        rows = outer(left, pl.multiple_of(i * NB + half * HALF, HALF), HALF, left, 0, SB)
        store(2 * i + 1 - first, rows[:, :NB])
        store(2 * i + 2 - first, rows[:, NB:])


def domain_edge(
    present, coef, ch, cl, th, tl, gradient, mixed, side_b, other,
    fresh, fh, fl, work, total, edge, cross_ref,
):
    domain_far_rows(
        present, coef, ch, cl, th, tl, gradient, mixed, side_b, other,
        fresh, fh, fl, work, total, cross_ref,
    )
    core = core_of()
    far = (fh, fl)
    owner_half(far, half_rows(edge), 1 - core)
    edge[5 * HALF :, :] = jnp.zeros((2 * TILE, NB), f32)
    at = pl.multiple_of((1 - core) * NB + lax.axis_index("orb") * HALF, HALF)
    half_rows(edge)(4 - 4 * core, outer(far, at, HALF, far, SB, NB))


def domain_give(present, coef, ch, cl, work, total, fresh, fh, fl, give):
    other_blocks(present, coef, ch, cl, work, total, fresh, fh, fl)
    core = core_of()
    rest = (fh, fl)
    owner_half(rest, half_blocks(give), core)
    at = pl.multiple_of(core * NB + lax.axis_index("orb") * HALF, HALF)
    give[4 * core] = outer(rest, at, HALF, rest, SB, NB)


def domain_last(total_blocks, own_lists, fresh1, f1h, f1l, fresh2, f2h, f2l, result, own, window, nh, nl):
    core = core_of()
    half = lax.axis_index("orb")
    nh[...] = near_rows(f1h, f2h)
    nl[...] = near_rows(f1l, f2l)
    near = (nh, nl)
    owner_half(near, half_blocks(own), 0)
    rows = pl.multiple_of(half * HALF, HALF)

    def far_or_rest(row_at, first_at, second_at):
        left = (nh[pl.ds(row_at, HALF), :], nl[pl.ds(row_at, HALF), :])
        first = pl.ds(first_at, NB)
        second = pl.ds(second_at, NB)
        right = [
            jnp.where(core == 0, a[first, :], b[second, :]) for a, b in ((f1h, f2h), (f1l, f2l))
        ]
        return dot3(left, right, ((1,), (1,)))

    def rest_or_far(row_at, first_at, second_at):
        left = (nh[pl.ds(row_at, HALF), :], nl[pl.ds(row_at, HALF), :])
        first = pl.ds(first_at, NB)
        second = pl.ds(second_at, NB)
        right = [
            jnp.where(core == 0, b[first, :], a[second, :]) for a, b in ((f1h, f2h), (f1l, f2l))
        ]
        return dot3(left, right, ((1,), (1,)))

    own[0] = far_or_rest(rows, NB, NB)
    own[5] = rest_or_far(pl.multiple_of(NB + half * HALF, HALF), 0, 0)
    for source, at, block, count in (
        (fresh1, 0, 4 * core, 2),
        (fresh1, SB, 2 + core, 1),
        (fresh2, 0, 4 - 4 * core, 2),
        (fresh2, SB, 3 - core, 1),
    ):
        window[pl.ds(aligned(block, NB), count * NB), :] = source[at : at + count * NB, :SB]
    for d in range(2):
        for i in range(4):
            at = aligned(relative(own_lists[d, i], total_blocks), NB)
            result[d, i] = window[pl.ds(at, NB), d * NB : (d + 1) * NB]


def owner_kernel(own, from_core, from_edge, out):
    core = core_of()
    edge = [from_edge[i * HALF : (i + 1) * HALF, :] for i in range(5)]
    lower = [jnp.where(core == 0, from_core[i], edge[i]) for i in range(5)]
    upper = [jnp.where(core == 0, edge[i], from_core[i]) for i in range(5)]
    out[0] = own[0] + upper[0]
    for i in range(1, 5):
        out[i] = own[i] + upper[i] + lower[i - 1]
    out[5] = own[5] + lower[4]


def to_core(value):
    count = lax.axis_size("grid")
    return lax.ppermute(value, "grid", [(i, i ^ 1) for i in range(count)])


def to_edge(value):
    count = lax.axis_size("grid")
    route = [(i, (i + 1) % count if i % 2 else (i - 1) % count) for i in range(count)]
    return lax.ppermute(value, "grid", route)


def to_orb(value):
    return lax.ppermute(value, "orb", [(0, 1), (1, 0)])


A_OUT = vmem((A_ROWS, NB))
B_OUT = vmem((B_ROWS, NB))
BK_OUT = vmem((B_ROWS + HALF, NB))
GIVE_OUT = vmem((GIVE_ROWS, NB))
KEEP_OUT = vmem((HALF, NB))
CROSS = vmem((NB, NB))


def total_over_all(made, after_near, before_sum):
    side_a, side_b, keep, arrived = made
    side_a, side_b = call(
        near_keep_kernel,
        (side_a, side_b, keep, arrived),
        (vmem((A_ROWS + HALF, NB)), B_OUT),
        "add_near",
    )
    side_b = after_near(side_b)
    first_b = to_edge(side_b)
    first_a = to_orb(side_a)
    side_a, keep = call(add_keep_kernel, (side_a, first_a), (A_OUT, KEEP_OUT), "add_a")
    last_a = to_edge(side_a)
    (side_b,) = call(add_kernel, (side_b, first_b), (B_OUT,), "add_b")
    last_b = before_sum(to_orb(side_b))
    side_a, side_b, near = call(
        total_kernel,
        (side_a, last_a, side_b, last_b, keep),
        (A_OUT, BK_OUT, GIVE_OUT),
        "add_all",
    )
    return side_a, side_b, to_core(near)


def shards(
    density, basis_values, quad_weights, ext_potential, batch_blocks, domain_blocks, coefficients
):
    total_blocks = density.shape[0] * lax.axis_size("grid")
    points = basis_values.shape[1]
    core = lax.rem(lax.axis_index("grid"), 2)
    window = 6 * NB
    row_out = vmem((1, points))
    coef_out = vmem((window, 4 * NB))
    coef_half = vmem((window, 4 * NB), bf16)
    turned_half = vmem((4 * NB, window), bf16)
    unit = 2 * 3 * points * SB * SB

    blocks = coefficients.reshape(8, NB, NB)
    own = density.reshape(6, HALF, NB)
    edge = to_edge(own)
    own_far = to_orb(own)
    other = to_core(own)
    *basis, done = sort_basis(total_blocks, batch_blocks, basis_values, unit)
    th, tl, nh, nl = basis
    near, early, rest, list_row = cut(domain_blocks, own, blocks.reshape(16, HALF, NB), other)
    early = to_orb(early)
    (own_far,) = call(hold_kernel, (own_far, done), (vmem((6, HALF, NB)),), "hold")
    other_far = to_core(own_far)
    (edge_message,) = call(
        far_kernel,
        (list_row, edge, done),
        (vmem((5 * HALF + TILE, NB)),),
        "far_message",
    )
    edge_far = to_orb(edge_message)
    (rho,) = call(
        rho_first,
        (th, tl, near, own_far, edge, other, other_far, early),
        (row_out,),
        "rho_first",
        flops=5 * unit,
    )
    edge_far, rho = lax.optimization_barrier((edge_far, rho))
    other_lists = edge_far[5 * HALF, :8].reshape(2, 4).astype(jnp.int32)

    packed = None
    for iteration in range(ITERS):
        if iteration == 0:
            kernel, operands = fock_other_first, (edge_far,)
        else:
            kernel, operands = fock_other_later, packed
        scale, give, keep = call(
            kernel,
            (quad_weights, ext_potential, *basis, rho, *operands),
            (row_out, GIVE_OUT, KEEP_OUT),
            "fock_other",
            scratch=(CROSS,),
            plain=(0, 1),
            flops=3 * unit,
        )
        arrived = to_core(give)
        side_a, side_b = call(
            fock_side, (*basis, scale), (A_OUT, B_OUT), "fock_side", flops=3 * unit
        )
        ready = {}

        def after_near(value):
            if iteration == 0:
                value, mine = lax.optimization_barrier((value, rest))
                ready["partner"] = to_orb(mine)
            return value

        def before_sum(value):
            if iteration == 0:
                made = call(
                    functools.partial(spread_kernel, total_blocks),
                    (domain_blocks, other_lists, blocks, hbm(early), hbm(ready["partner"])),
                    (coef_out, coef_half, coef_half, turned_half, turned_half, vmem((24, NB))),
                    "spread",
                    smem=(0, 1),
                    plain=(2, 3, 4),
                    flops=unit,
                )
            else:
                made = call(
                    gather_kernel,
                    (fresh1, fresh2),
                    (coef_out, coef_half, coef_half, turned_half, turned_half),
                    "gather",
                    flops=3 * unit,
                )
            value, *ready["made"] = lax.optimization_barrier((value, *made))
            return value

        side_a, side_b, arriving = total_over_all(
            (side_a, side_b, keep, arrived), after_near, before_sum
        )
        if iteration == 0:
            coef, *halves, present = ready["made"]
        else:
            coef, *halves = ready["made"]
        gradient, mixed = call(
            domain_side,
            (side_a, side_b, *halves),
            (vmem((4 * NB, 4 * NB)), vmem((2, SB, SB))),
            "domain_side",
            flops=unit,
        )
        operands = (
            present, coef, *halves, gradient, mixed, side_b, arriving
        )
        new_outs = (vmem((3 * NB, 4 * NB)),) + (vmem((3 * NB, 4 * NB), bf16),) * 2
        far_outs = new_outs + (coef_out, vmem((2, SB, SB)))
        if iteration < ITERS - 1:
            fresh1, f1h, f1l, work, total, mine = call(
                domain_far,
                operands,
                far_outs + (vmem((PAIR + NB, NB)),),
                "domain_far",
                scratch=(CROSS,),
                flops=2 * unit,
            )
            from_far = to_edge(mine)
            fresh2, f2h, f2l, give, keep = call(
                domain_other,
                (present, coef, *halves[:2], work, total),
                new_outs + (GIVE_OUT, KEEP_OUT),
                "domain_other",
                scratch=(CROSS,),
                flops=unit,
            )
            arrived = to_core(give)
            (near,) = call(
                density_near, (f1h, f1l, f2h, f2l), (vmem((PAIR, NB)),), "density_near"
            )
            near, keep = call(
                near_sum_kernel,
                (near, keep, arrived),
                (vmem((PAIR + STRIP, NB)), KEEP_OUT),
                "add_near",
            )
            from_near = to_edge(near)
            near_total, cross = call(
                near_total_kernel, (near, keep, mine, from_far), (GIVE_OUT, CROSS), "add_far"
            )
            arriving = to_core(near_total)
            (rho,) = call(rho_near, (th, tl, near_total, cross), (row_out,), "rho_near", flops=unit)
            (rho,) = call(
                rho_other,
                (th, tl, rho, near_total, arriving),
                (row_out,),
                "rho_other",
                scratch=(CROSS,),
            )
            packed = (mine, from_near)
    message = vmem((5, HALF, NB))
    edge_message = vmem((5 * HALF + 2 * TILE, NB))
    fresh1, f1h, f1l, work, total, edge = call(
        domain_edge, operands, far_outs + (edge_message,), "domain_edge", scratch=(CROSS,), flops=2 * unit
    )
    from_edge = to_edge(edge)
    fresh2, f2h, f2l, give = call(
        domain_give,
        (present, coef, *halves[:2], work, total),
        new_outs + (message,),
        "domain_give",
        flops=unit,
    )
    from_core = to_core(give)
    result, own = call(
        functools.partial(domain_last, total_blocks),
        (domain_blocks, fresh1, f1h, f1l, fresh2, f2h, f2l),
        (jax.ShapeDtypeStruct(coefficients.shape, f32), vmem((6, HALF, NB))),
        "domain_last",
        scratch=(vmem((window, SB)),) + (vmem((SB, 4 * NB), bf16),) * 2,
        smem=(0,),
    )
    (rows,) = call(
        owner_kernel,
        (own, from_core, from_edge),
        (jax.ShapeDtypeStruct((6, HALF, NB), f32),),
        "owner_rows",
    )
    return (rows.reshape(density.shape), result)


def solution(mesh):
    in_specs = (
        P("grid", None, "orb", None),
        P(("grid", "orb"), None, None),
        P(("grid", "orb"), None),
        P(("grid", "orb"), None),
        P(("grid", "orb"), None),
        P(("grid", "orb"), None),
        P(("grid", "orb"), None, None, None),
    )
    out_specs = (P("grid", None, "orb", None), P(("grid", "orb"), None, None, None))
    return jax.shard_map(shards, mesh=mesh, in_specs=in_specs, out_specs=out_specs, check_vma=False)
```
